32 devices in a mesh: parts: 2 (over y), tile: 4 (over z), src: 2 (over x), focus: 2 (over core).
Axes of the slice: x: 2, y: 2, z: 4, core: 2. Of those that a mesh axis runs over, the one named last changes fastest.
Arguments:
- mask: float32 [768, 1536], P('parts', 'tile'), parts along dimension 0, may hold values from -1 to 1
- target: float32 [768, 1536], P('parts', 'tile'), parts along dimension 0, may hold values from 0 to 1
- pupil: float32 [2, 16, 4, 64, 64], P(None, 'src', 'focus'), may hold values from -6 to 6
- weights: float32 [16], P('src'), may hold values from 0.25 to 4
- counts: int32 [8], P('parts'), parts along dimension 0, may hold values from 1 to 4, as said below
Outputs:
- gradient: float32 [768, 1536], P(('parts', 'src', 'focus'), 'tile'), parts along dimension 0
The draws below stay inside these ranges and needn't reach their ends.
There are 2 independent parts, one for each index of `parts`. The reference program is written for one: setup_inputs(seed, part) draws one part's arguments, and reference() takes and returns one part's arrays. A program takes and returns all parts, laid end to end along the dimension named above; an argument that names none is the same for every part. Nothing has to cross between parts.
Inputs may be any that keep to these rules, and one draw needn't show every extreme that they name: Corners 0 to counts - 1 of a subtile are in use; of the two subtiles t and t + 2 at least one uses a single corner; some subtile uses all 4.
All inputs are finite; a program needn't handle non-finite values.
Results may differ from the reference program's by a relative error of at most 0.0003.
Values sent between devices are 32-bit elements; how exact they have to be, the bound alone decides.
A program may use at most 128 MiB of HBM per device.

```python
import math
import jax
import jax.numpy as jnp
from jax import lax

TILE = 384
AMBIT = 64
KF = 64
CMAX = 4
WIN = 512
SOURCES = 16
TILES = 4


def draw_counts(key, part):
    half = TILES // 2
    dense = jax.random.randint(key, (half,), 1, CMAX + 1)
    order = jax.random.permutation(jax.random.fold_in(key, 7), half)
    dense = dense.at[order[0]].set(CMAX)
    which = jax.random.randint(jax.random.fold_in(key, 11), (half,), 0, 2)
    single = jnp.ones((half,), jnp.int32)
    lower = jnp.where(which == 0, dense, single)
    upper = jnp.where(which == 0, single, dense)
    return jnp.concatenate([lower, upper]).astype(jnp.int32)


def block_scale(key, extent, pieces, least, high):
    gain, own = 1.0, jax.random.fold_in(key, 6)
    for position, shards_of in pieces:
        steps = jnp.exp(jax.random.uniform(jax.random.fold_in(own, position), (shards_of,), jnp.float32, least / len(pieces), high / len(pieces)))
        gain = gain * jnp.repeat(steps, extent[position] // shards_of).reshape([-1 if axis == position else 1 for axis in range(len(extent))])
    return gain


def scatter_about(rng, extent, width, most, pieces=(), kind=jnp.bfloat16):
    result = width * jax.random.normal(rng, extent, jnp.float32)
    if pieces:
        result = result * block_scale(rng, extent, pieces, -0.22, 0.18)
    return jnp.clip(result, -most, most).astype(kind)


def setup_inputs(seed: int = 0, part: int = 0) -> dict:
    streams_of = jax.random.split(jax.random.key(seed), 6)
    own_keys = jax.random.split(jax.random.fold_in(streams_of[5], part), 6)
    mask = jnp.clip(jax.random.uniform(own_keys[0], (TILE, TILES * TILE), jnp.float32, -1.0, 1.0) * block_scale(own_keys[0], (TILE, TILES * TILE), ((1, 4),), -0.4, 0.0), -1.0, 1.0)
    target = jnp.clip(1.0 * jax.random.uniform(own_keys[1], (TILE, TILES * TILE), jnp.float32) ** block_scale(own_keys[1], (TILE, TILES * TILE), ((1, 4),), -0.2, 0.2), 0.0, 1.0)
    pupil = scatter_about(streams_of[2], (2, SOURCES, CMAX, KF, KF), 1.0, 6.0, ((1, 2), (2, 2)), jnp.float32)
    weights = jnp.clip(jnp.exp(math.log(4.0) - 2.7725887 * jax.random.uniform(streams_of[3], (SOURCES,), jnp.float32) ** block_scale(streams_of[3], (SOURCES,), ((0, 2),), -0.2, 0.2)), 0.25, 4.0)
    counts = draw_counts(jax.random.fold_in(jax.random.fold_in(streams_of[5], part), 71), part)
    return {"mask": mask, "target": target, "pupil": pupil, "weights": weights, "counts": counts}


resist_slope = 4.0
resist_level = 0.5

def product(left, right):
    return jnp.dot(left, right, precision=lax.Precision.HIGHEST, preferred_element_type=jnp.float32)

def contract(form, left, right):
    return jnp.einsum(form, left, right, precision=lax.Precision.HIGHEST, preferred_element_type=jnp.float32)

def phase_table(freqs, length, offset, count):
    kvalues = jnp.arange(freqs, dtype=jnp.int32) - freqs // 2
    nvalues = jnp.arange(count, dtype=jnp.int32) + offset
    phase = jnp.mod(kvalues[:, None] * nvalues[None, :], length).astype(jnp.float32) * (2.0 * math.pi / length)
    return (jnp.cos(phase), jnp.sin(phase))

def reference(mask, target, pupil, weights, counts):
    norm_win = 1.0 / math.sqrt(WIN)
    norm_back = math.sqrt(2.0 / KF)
    cos_col, sin_col = phase_table(KF, WIN, 0, WIN)
    col_re = cos_col * norm_win
    col_im = -sin_col * norm_win
    cos_row, sin_row = phase_table(KF, WIN, AMBIT, TILE)
    row_re = cos_row * norm_win
    row_im = -sin_row * norm_win
    back_re = cos_row.T * norm_back
    back_im = sin_row.T * norm_back
    padded = jnp.pad(mask, ((0, 0), (AMBIT, AMBIT)))
    pup_re = pupil[0]
    pup_im = pupil[1]
    src_scale = weights / SOURCES
    corner_ids = jnp.arange(CMAX, dtype=jnp.int32)

    def one_tile(tile_index):
        window = lax.dynamic_slice_in_dim(padded, tile_index * TILE, WIN, 1)
        x_re = product(window, col_re.T)
        x_im = product(window, col_im.T)
        spec_re = product(row_re, x_re) - product(row_im, x_im)
        spec_im = product(row_re, x_im) + product(row_im, x_re)
        g_re = pup_re * spec_re - pup_im * spec_im
        g_im = pup_re * spec_im + pup_im * spec_re
        h_re = contract('sckl,nl->sckn', g_re, back_re) - contract('sckl,nl->sckn', g_im, back_im)
        h_im = contract('sckl,nl->sckn', g_re, back_im) + contract('sckl,nl->sckn', g_im, back_re)
        e_re = contract('mk,sckn->scmn', back_re, h_re) - contract('mk,sckn->scmn', back_im, h_im)
        e_im = contract('mk,sckn->scmn', back_re, h_im) + contract('mk,sckn->scmn', back_im, h_re)
        intensity = contract('s,scmn->cmn', src_scale, e_re * e_re + e_im * e_im)
        resist = jax.nn.sigmoid(resist_slope * (intensity - resist_level))
        tgt = lax.dynamic_slice_in_dim(target, tile_index * TILE, TILE, 1)
        active = (corner_ids < counts[tile_index]).astype(jnp.float32)
        slope = 2.0 * (resist - tgt[None]) * resist_slope * resist * (1.0 - resist) * active[:, None, None]
        factor = 2.0 * src_scale[:, None, None, None] * slope[None]
        ge_re = factor * e_re
        ge_im = factor * e_im
        gh_re = contract('mk,scmn->sckn', back_re, ge_re) + contract('mk,scmn->sckn', back_im, ge_im)
        gh_im = contract('mk,scmn->sckn', back_re, ge_im) - contract('mk,scmn->sckn', back_im, ge_re)
        gg_re = contract('sckn,nl->sckl', gh_re, back_re) + contract('sckn,nl->sckl', gh_im, back_im)
        gg_im = contract('sckn,nl->sckl', gh_im, back_re) - contract('sckn,nl->sckl', gh_re, back_im)
        gs_re = lax.optimization_barrier(jnp.sum(pup_re * gg_re + pup_im * gg_im, axis=(0, 1)))
        gs_im = lax.optimization_barrier(jnp.sum(pup_re * gg_im - pup_im * gg_re, axis=(0, 1)))
        gx_re = product(row_re.T, gs_re) + product(row_im.T, gs_im)
        gx_im = product(row_re.T, gs_im) - product(row_im.T, gs_re)
        return product(gx_re, col_re) + product(gx_im, col_im)

    def accumulate(tile_index, total):
        piece = one_tile(tile_index)
        start = (tile_index * TILE).astype(jnp.int32)
        zero = jnp.zeros((), jnp.int32)
        current = lax.dynamic_slice(total, (zero, start), (TILE, WIN))
        return lax.dynamic_update_slice(total, current + piece, (zero, start))
    total = jnp.zeros((TILE, TILES * TILE + 2 * AMBIT), jnp.float32)
    total = lax.fori_loop(0, TILES, accumulate, total)
    return total[:, AMBIT:AMBIT + TILES * TILE]
```

```python
import functools
import math

import jax
import jax.numpy as jnp
import ml_dtypes
import numpy as np
from jax import lax
from jax.experimental import pallas as pl
from jax.experimental.pallas import tpu as pltpu
from jax.sharding import PartitionSpec as P

AMBIT = 64
MESH = pl.DeviceIdType.MESH

resist_slope = 4.0
resist_level = 0.5


def halves(table):
    table = table.astype(np.float32)
    high = table.astype(ml_dtypes.bfloat16)
    low = (table - high.astype(np.float32)).astype(ml_dtypes.bfloat16)
    return high, low


def left_table(table):
    high, low = halves(table)
    return np.concatenate([high, low, high], axis=1)


def right_table(table):
    high, low = halves(table)
    return np.concatenate([high, low, high], axis=0)


def tables(tile, freqs, width):
    win = tile + 2 * width
    grid = 2 * freqs
    k = np.arange(freqs) - freqs // 2
    row = 2.0 * np.pi * ((k[:, None] * (np.arange(tile) + width)[None, :]) % win) / win
    row2 = np.concatenate([np.cos(row), -np.sin(row)], axis=0) / math.sqrt(win)
    col = 2.0 * np.pi * ((k[:, None] * np.arange(win)[None, :]) % win) / win
    col2 = np.concatenate([np.cos(col), -np.sin(col)], axis=0) / math.sqrt(win)
    own = col2[:, width : width + tile]
    to_left = np.zeros((2 * width, 2 * freqs))
    to_left[:width] = col2[:, width + tile :].T
    to_right = np.zeros((2 * width, 2 * freqs))
    to_right[width:] = col2[:, :width].T
    at = 2.0 * np.pi * ((k[:, None] * np.arange(grid)[None, :]) % grid) / grid
    c, s = np.cos(at) * math.sqrt(2.0 / freqs), np.sin(at) * math.sqrt(2.0 / freqs)
    field = np.block([[c, s], [-s, c]])
    q = np.arange(1 - freqs, freqs)
    gap = (np.arange(tile) + width)[:, None] / win - np.arange(grid)[None, :] / grid
    fine = np.cos(2.0 * np.pi * gap[:, :, None] * q[None, None, :]).sum(-1) / grid
    back = np.zeros((6 * freqs, tile))
    back[: 2 * freqs] = own
    back[2 * freqs : 4 * freqs, :width] = col2[:, width + tile :]
    back[4 * freqs :, tile - width :] = col2[:, :width]
    return dict(
        row=left_table(row2),
        own=right_table(own.T),
        to_left=right_table(to_left),
        to_right=right_table(to_right),
        f1r=right_table(field),
        f2l=left_table(field.T),
        f1l=left_table(field),
        f2r=right_table(field.T),
        ul=left_table(fine),
        utr=right_table(fine.T),
        ur=right_table(fine),
        utl=left_table(fine.T),
        rowt=left_table(row2.T),
        back=right_table(back),
    )


def split(x):
    high = x.astype(jnp.bfloat16)
    low = (x - high.astype(jnp.float32)).astype(jnp.bfloat16)
    return high, low


def dot(a, b):
    return jnp.dot(a, b, preferred_element_type=jnp.float32)


def times_table(x, table):
    high, low = split(x)
    return dot(jnp.concatenate([high, high, low], axis=1), table)


def table_times(table, x):
    high, low = split(x)
    return dot(table, jnp.concatenate([high, high, low], axis=0))


NAMES = (
    "row", "own", "to_left", "to_right", "f1r", "f2l", "f1l", "f2r",
    "ul", "utr", "ur", "utl", "rowt", "back",
)


def kernel(dims, counts_ref, w_ref, mask_ref, target_ref, pup_ref, *refs):
    ns, nf, nt, local_src, corners, freqs, tile = dims
    tab = dict(zip(NAMES, refs[: len(NAMES)]))
    (out_ref, p_ref, e_ref, zs_send, zs_recv, i_send, i_recv, g_send, g_recv, zg_send, zg_recv,
     zs_ss, zs_rs, i_ss, i_rs, g_ss, g_rs, zg_ss, zg_rs) = refs[len(NAMES):]
    grid = 2 * freqs
    rows = out_ref.shape[0]
    sources = local_src * ns
    t = lax.axis_index("tile")
    src = lax.axis_index("src")
    focus = lax.axis_index("focus")
    has_left = t > 0
    has_right = t < nt - 1
    left = {"tile": jnp.maximum(t - 1, 0)}
    right = {"tile": jnp.minimum(t + 1, nt - 1)}
    peers = [(a, b) for a in range(ns) for b in range(nf) if a + b > 0]

    def peer(a, b):
        return {"src": lax.rem(src + a, ns), "focus": lax.rem(focus + b, nf)}

    def remote(source, dest, ssem, rsem, device):
        return pltpu.make_async_remote_copy(
            src_ref=source, dst_ref=dest, send_sem=ssem, recv_sem=rsem,
            device_id=device, device_id_type=MESH,
        )

    def along(send, recv, ssem, rsem):
        return (
            remote(send.at[0], recv.at[1], ssem.at[0], rsem.at[1], left),
            remote(send.at[1], recv.at[0], ssem.at[1], rsem.at[0], right),
        )

    zs_recv[...] = jnp.zeros_like(zs_recv)
    zg_recv[...] = jnp.zeros_like(zg_recv)
    barrier = pltpu.get_barrier_semaphore()
    for a, b in peers:
        pl.semaphore_signal(barrier, inc=1, device_id=peer(a, b), device_id_type=MESH)

    @pl.when(has_left)
    def _():
        pl.semaphore_signal(barrier, inc=1, device_id=left, device_id_type=MESH)

    @pl.when(has_right)
    def _():
        pl.semaphore_signal(barrier, inc=1, device_id=right, device_id_type=MESH)

    lane = lax.broadcasted_iota(jnp.int32, (freqs, grid), 1)
    first = lane < freqs

    def swap(x):
        return pltpu.roll(x, freqs, 1)

    def complex_of(q):
        top, low = q[:freqs], swap(q[freqs:])
        return jnp.where(first, top - low, top + low)

    ah, al = split(table_times(tab["row"][...], mask_ref[...]))

    def columns(begin, end, table):
        high, low = ah[:, begin:end], al[:, begin:end]
        return complex_of(dot(jnp.concatenate([high, high, low], axis=1), table[...]))

    zs_send[0] = columns(0, 2 * AMBIT, tab["to_left"])
    zs_send[1] = columns(tile - 2 * AMBIT, tile, tab["to_right"])
    pl.semaphore_wait(
        barrier, len(peers) + has_left.astype(jnp.int32) + has_right.astype(jnp.int32)
    )
    zs_left, zs_right = along(zs_send, zs_recv, zs_ss, zs_rs)
    pl.when(has_left)(zs_left.start)
    pl.when(has_right)(zs_right.start)
    spec = columns(0, tile, tab["own"])
    for corner in range(corners):
        for s in range(local_src):
            p_ref[corner, s] = jnp.concatenate(
                [pup_ref[0, s, corner], pup_ref[1, s, corner]], axis=1
            )
    pl.when(has_left)(zs_right.wait_recv)
    pl.when(has_right)(zs_left.wait_recv)
    spec = spec + zs_recv[0] + zs_recv[1]
    turned = swap(spec)
    same = jnp.where(first, spec, turned)
    cross = jnp.where(first, -turned, spec)

    i_copies = []
    for corner in range(corners):
        parts = []
        for s in range(local_src):
            p = p_ref[corner, s]
            parts.append(p * same + swap(p) * cross)
        h = times_table(jnp.concatenate(parts, axis=0), tab["f1r"][...])
        h = jnp.concatenate(
            [
                jnp.concatenate(
                    [h[s * freqs : (s + 1) * freqs, :grid], h[s * freqs : (s + 1) * freqs, grid:]],
                    axis=0,
                )
                for s in range(local_src)
            ],
            axis=1,
        )
        e = table_times(tab["f2l"][...], h)
        e_ref[corner] = e
        total = jnp.zeros((grid, grid), jnp.float32)
        for s in range(local_src):
            e_re = e[:grid, s * grid : (s + 1) * grid]
            e_im = e[grid:, s * grid : (s + 1) * grid]
            total = total + (w_ref[s] * (1.0 / sources)) * (e_re * e_re + e_im * e_im)
        i_send[corner] = total
        for a in range(1, ns):
            copy = remote(
                i_send.at[corner], i_recv.at[a - 1, corner],
                i_ss.at[a - 1, corner], i_rs.at[a - 1, corner], peer(a, 0),
            )
            copy.start()
            i_copies.append(copy)

    count = counts_ref[t]
    sum_x = jnp.zeros((freqs, grid), jnp.float32)
    sum_y = jnp.zeros((freqs, grid), jnp.float32)
    for corner in range(corners):
        total = i_send[corner]
        for a in range(1, ns):
            i_copies[corner * (ns - 1) + a - 1].wait_recv()
            total = total + i_recv[a - 1, corner]
        intensity = times_table(table_times(tab["ul"][...], total), tab["utr"][...])
        decay = jnp.exp(-resist_slope * (intensity - resist_level))
        resist = 1.0 / (1.0 + decay)
        active = jnp.where(focus * corners + corner < count, 2.0 * resist_slope, 0.0)
        slope = active * (resist - target_ref[...]) * (decay * resist * resist)
        slope = table_times(tab["utl"][...], times_table(slope, tab["ur"][...]))
        slope = jnp.concatenate([slope, slope], axis=0)
        ge = jnp.concatenate(
            [e_ref[corner, :, s * grid : (s + 1) * grid] * slope for s in range(local_src)], axis=1
        )
        gh = table_times(tab["f1l"][...], ge)
        gh = jnp.concatenate(
            [
                jnp.concatenate(
                    [gh[:freqs, s * grid : (s + 1) * grid], gh[freqs:, s * grid : (s + 1) * grid]],
                    axis=1,
                )
                for s in range(local_src)
            ],
            axis=0,
        )
        gg = times_table(gh, tab["f2r"][...])
        for s in range(local_src):
            p = p_ref[corner, s]
            part = (w_ref[s] * (2.0 / sources)) * gg[s * freqs : (s + 1) * freqs]
            sum_x = sum_x + p * part
            sum_y = sum_y + swap(p) * part
    gs = jnp.where(first, sum_x + swap(sum_x), sum_y - swap(sum_y))

    g_send[...] = gs
    g_copies = []
    for n, (a, b) in enumerate(peers):
        copy = remote(g_send, g_recv.at[n], g_ss.at[n], g_rs.at[n], peer(a, b))
        copy.start()
        g_copies.append(copy)
    for n, copy in enumerate(g_copies):
        copy.wait_recv()
        gs = gs + g_recv[n]
    zg_send[0] = gs
    zg_send[1] = gs
    zg_left, zg_right = along(zg_send, zg_recv, zg_ss, zg_rs)
    pl.when(has_left)(zg_left.start)
    pl.when(has_right)(zg_right.start)

    def stacked(g):
        turned = swap(g)
        return jnp.concatenate([g, jnp.where(first, turned, -turned)], axis=0)

    begin = pl.multiple_of((src * nf + focus) * rows, 16)
    rowt = tab["rowt"][pl.ds(begin, rows), :]
    pl.when(has_left)(zg_right.wait_recv)
    pl.when(has_right)(zg_left.wait_recv)
    gx = table_times(
        rowt, jnp.concatenate([stacked(gs), stacked(zg_recv[0]), stacked(zg_recv[1])], axis=1)
    )
    out_ref[...] = times_table(gx, tab["back"][...])

    pl.when(has_left)(zs_left.wait_send)
    pl.when(has_right)(zs_right.wait_send)
    pl.when(has_left)(zg_left.wait_send)
    pl.when(has_right)(zg_right.wait_send)
    for copy in i_copies + g_copies:
        copy.wait_send()


def per_device(mask, target, pupil, weights, counts):
    tile = mask.shape[0]
    freqs = pupil.shape[-1]
    local_src = weights.shape[0]
    corners = pupil.shape[2]
    ns, nf, nt = (lax.axis_size(axis) for axis in ("src", "focus", "tile"))
    grid = 2 * freqs
    rows = tile // (ns * nf)
    peers = ns * nf - 1
    held = tables(tile, freqs, AMBIT)
    vmem = pl.BlockSpec(memory_space=pltpu.VMEM)
    smem = pl.BlockSpec(memory_space=pltpu.SMEM)
    f32 = jnp.float32
    dma = pltpu.SemaphoreType.DMA
    return pl.pallas_call(
        functools.partial(kernel, (ns, nf, nt, local_src, corners, freqs, tile)),
        out_shape=jax.ShapeDtypeStruct((rows, tile), f32),
        in_specs=[smem, smem] + [vmem] * (3 + len(NAMES)),
        out_specs=vmem,
        scratch_shapes=[
            pltpu.VMEM((corners, local_src, freqs, grid), f32),
            pltpu.VMEM((corners, 2 * grid, local_src * grid), f32),
            pltpu.VMEM((2, freqs, grid), f32),
            pltpu.VMEM((2, freqs, grid), f32),
            pltpu.VMEM((corners, grid, grid), f32),
            pltpu.VMEM((max(ns - 1, 1), corners, grid, grid), f32),
            pltpu.VMEM((freqs, grid), f32),
            pltpu.VMEM((max(peers, 1), freqs, grid), f32),
            pltpu.VMEM((2, freqs, grid), f32),
            pltpu.VMEM((2, freqs, grid), f32),
            dma((2,)),
            dma((2,)),
            dma((max(ns - 1, 1), corners)),
            dma((max(ns - 1, 1), corners)),
            dma((max(peers, 1),)),
            dma((max(peers, 1),)),
            dma((2,)),
            dma((2,)),
        ],
        compiler_params=pltpu.CompilerParams(
            collective_id=0, has_side_effects=True, vmem_limit_bytes=48 * 1024 * 1024
        ),
        name="abbe_gradient",
    )(counts, weights, mask, target, pupil, *[jnp.asarray(held[name]) for name in NAMES])


def solution(mesh):
    return jax.shard_map(
        per_device,
        mesh=mesh,
        in_specs=(
            P("parts", "tile"),
            P("parts", "tile"),
            P(None, "src", "focus", None, None),
            P("src"),
            P("parts"),
        ),
        out_specs=P(("parts", "src", "focus"), "tile"),
        check_vma=False,
    )
```

```python
import functools
import math

import jax
import jax.numpy as jnp
import ml_dtypes
import numpy as np
from jax import lax
from jax.experimental import pallas as pl
from jax.experimental.pallas import tpu as pltpu
from jax.sharding import PartitionSpec as P

AMBIT = 64
MESH = pl.DeviceIdType.MESH

resist_slope = 4.0
resist_level = 0.5


def halves(table):
    table = table.astype(np.float32)
    high = table.astype(ml_dtypes.bfloat16)
    low = (table - high.astype(np.float32)).astype(ml_dtypes.bfloat16)
    return np.stack([high, low])


def tables(tile, freqs, width):
    win = tile + 2 * width
    grid = 2 * freqs
    k = np.arange(freqs) - freqs // 2
    row = 2.0 * np.pi * ((k[:, None] * (np.arange(tile) + width)[None, :]) % win) / win
    row2 = np.concatenate([np.cos(row), -np.sin(row)], axis=0) / math.sqrt(win)
    col = 2.0 * np.pi * ((k[:, None] * np.arange(win)[None, :]) % win) / win
    col2 = np.concatenate([np.cos(col), -np.sin(col)], axis=0) / math.sqrt(win)
    own = col2[:, width : width + tile]
    edges = np.zeros((2, 2 * freqs, 2 * width))
    edges[0, :, :width] = col2[:, width + tile :]
    edges[1, :, width:] = col2[:, :width]
    at = 2.0 * np.pi * ((k[:, None] * np.arange(grid)[None, :]) % grid) / grid
    c, s = np.cos(at) * math.sqrt(2.0 / freqs), np.sin(at) * math.sqrt(2.0 / freqs)
    field = np.block([[c, s], [-s, c]])
    q = np.arange(1 - freqs, freqs)
    gap = (np.arange(tile) + width)[:, None] / win - np.arange(grid)[None, :] / grid
    fine = np.cos(2.0 * np.pi * gap[:, :, None] * q[None, None, :]).sum(-1) / grid
    return dict(
        row=halves(row2),
        own=halves(own),
        left=halves(edges[0]),
        right=halves(edges[1]),
        f1=halves(field),
        f2=halves(field.T),
        fine=halves(fine),
        finet=halves(fine.T),
        rowt=halves(row2.T),
    )


def split(x):
    high = x.astype(jnp.bfloat16)
    low = (x - high.astype(jnp.float32)).astype(jnp.bfloat16)
    return high, low


def dot(a, b):
    return jnp.dot(a, b, preferred_element_type=jnp.float32)


def dot_t(a, b):
    return lax.dot_general(a, b, (((1,), (1,)), ((), ())), preferred_element_type=jnp.float32)


def times_table(x, table):
    high, low = split(x)
    return dot(
        jnp.concatenate([high, high, low], axis=1),
        jnp.concatenate([table[0], table[1], table[0]], axis=0),
    )


def times_turned(x, table):
    high, low = split(x)
    return dot_t(
        jnp.concatenate([high, high, low], axis=1),
        jnp.concatenate([table[0], table[1], table[0]], axis=1),
    )


def table_times(table, x):
    high, low = split(x)
    return dot(
        jnp.concatenate([table[0], table[1], table[0]], axis=1),
        jnp.concatenate([high, high, low], axis=0),
    )


NAMES = ("row", "left", "right", "own", "f1", "f2", "fine", "finet", "rowt")


def kernel(dims, counts_ref, w_ref, mask_hbm, target_hbm, pup_hbm, *refs):
    ns, nf, nt, local_src, corners, freqs, tile = dims
    many = len(NAMES)
    held = dict(zip(NAMES, refs[:many]))
    out_ref = refs[many]
    mask_ref, target_ref, pup_ref = refs[many + 1 : many + 4]
    tab = dict(zip(NAMES, refs[many + 4 : 2 * many + 4]))
    (load_sem, p_ref, e_ref, zs_send, zs_recv, i_send, i_recv, g_send, g_recv, zg_send, zg_recv,
     zs_ss, zs_rs, i_ss, i_rs, g_ss, g_rs, zg_ss, zg_rs) = refs[2 * many + 4 :]
    grid = 2 * freqs
    rows = out_ref.shape[0]
    sources = local_src * ns
    t = lax.axis_index("tile")
    src = lax.axis_index("src")
    focus = lax.axis_index("focus")
    has_left = t > 0
    has_right = t < nt - 1
    left = {"tile": jnp.maximum(t - 1, 0)}
    right = {"tile": jnp.minimum(t + 1, nt - 1)}
    peers = [(a, b) for a in range(ns) for b in range(nf) if a + b > 0]

    def peer(a, b):
        return {"src": lax.rem(src + a, ns), "focus": lax.rem(focus + b, nf)}

    def remote(source, dest, ssem, rsem, device):
        return pltpu.make_async_remote_copy(
            src_ref=source, dst_ref=dest, send_sem=ssem, recv_sem=rsem,
            device_id=device, device_id_type=MESH,
        )

    def along(send, recv, ssem, rsem):
        return (
            remote(send.at[0], recv.at[1], ssem.at[0], rsem.at[1], left),
            remote(send.at[1], recv.at[0], ssem.at[1], rsem.at[0], right),
        )

    begin = pl.multiple_of((src * nf + focus) * rows, 16)
    loads = {}

    def load(name, source, dest):
        loads[name] = pltpu.make_async_copy(source, dest, load_sem.at[len(loads)])
        loads[name].start()

    load("row", held["row"], tab["row"])
    load("mask", mask_hbm, mask_ref)
    for name in ("left", "right", "own"):
        load(name, held[name], tab[name])
    load("pupil", pup_hbm, pup_ref)
    for name in ("f1", "f2", "fine"):
        load(name, held[name], tab[name])
    load("target", target_hbm, target_ref)
    load("finet", held["finet"], tab["finet"])
    load("rowt", held["rowt"].at[:, pl.ds(begin, rows), :], tab["rowt"])

    def need(*names):
        for name in names:
            loads[name].wait()

    zs_recv[...] = jnp.zeros_like(zs_recv)
    zg_recv[...] = jnp.zeros_like(zg_recv)
    barrier = pltpu.get_barrier_semaphore()
    for a, b in peers:
        pl.semaphore_signal(barrier, inc=1, device_id=peer(a, b), device_id_type=MESH)

    @pl.when(has_left)
    def _():
        pl.semaphore_signal(barrier, inc=1, device_id=left, device_id_type=MESH)

    @pl.when(has_right)
    def _():
        pl.semaphore_signal(barrier, inc=1, device_id=right, device_id_type=MESH)

    lane = lax.broadcasted_iota(jnp.int32, (freqs, grid), 1)
    first = lane < freqs

    def swap(x):
        return pltpu.roll(x, freqs, 1)

    def complex_of(q):
        top, low = q[:freqs], swap(q[freqs:])
        return jnp.where(first, top - low, top + low)

    need("row", "mask", "left", "right")
    ah, al = split(table_times(tab["row"], mask_ref[...]))

    def columns(begin, end, table):
        high, low = ah[:, begin:end], al[:, begin:end]
        wide = jnp.concatenate([table[0], table[1], table[0]], axis=1)
        return complex_of(dot_t(jnp.concatenate([high, high, low], axis=1), wide))

    zs_send[0] = columns(0, 2 * AMBIT, tab["left"])
    zs_send[1] = columns(tile - 2 * AMBIT, tile, tab["right"])
    pl.semaphore_wait(
        barrier, len(peers) + has_left.astype(jnp.int32) + has_right.astype(jnp.int32)
    )
    zs_left, zs_right = along(zs_send, zs_recv, zs_ss, zs_rs)
    pl.when(has_left)(zs_left.start)
    pl.when(has_right)(zs_right.start)
    need("own")
    spec = columns(0, tile, tab["own"])
    need("pupil")
    for corner in range(corners):
        for s in range(local_src):
            p_ref[corner, s] = jnp.concatenate(
                [pup_ref[0, s, corner], pup_ref[1, s, corner]], axis=1
            )
    pl.when(has_left)(zs_right.wait_recv)
    pl.when(has_right)(zs_left.wait_recv)
    spec = spec + zs_recv[0] + zs_recv[1]
    turned = swap(spec)
    same = jnp.where(first, spec, turned)
    cross = jnp.where(first, -turned, spec)

    need("f1", "f2")
    i_copies = []
    for corner in range(corners):
        parts = []
        for s in range(local_src):
            p = p_ref[corner, s]
            parts.append(p * same + swap(p) * cross)
        h = times_table(jnp.concatenate(parts, axis=0), tab["f1"])
        h = jnp.concatenate(
            [
                jnp.concatenate(
                    [h[s * freqs : (s + 1) * freqs, :grid], h[s * freqs : (s + 1) * freqs, grid:]],
                    axis=0,
                )
                for s in range(local_src)
            ],
            axis=1,
        )
        e = table_times(tab["f2"], h)
        e_ref[corner] = e
        total = jnp.zeros((grid, grid), jnp.float32)
        for s in range(local_src):
            e_re = e[:grid, s * grid : (s + 1) * grid]
            e_im = e[grid:, s * grid : (s + 1) * grid]
            total = total + (w_ref[s] * (1.0 / sources)) * (e_re * e_re + e_im * e_im)
        i_send[corner] = total
        for a in range(1, ns):
            copy = remote(
                i_send.at[corner], i_recv.at[a - 1, corner],
                i_ss.at[a - 1, corner], i_rs.at[a - 1, corner], peer(a, 0),
            )
            copy.start()
            i_copies.append(copy)

    need("fine", "target", "finet", "rowt")
    count = counts_ref[t]
    sum_x = jnp.zeros((freqs, grid), jnp.float32)
    sum_y = jnp.zeros((freqs, grid), jnp.float32)
    for corner in range(corners):
        total = i_send[corner]
        for a in range(1, ns):
            i_copies[corner * (ns - 1) + a - 1].wait_recv()
            total = total + i_recv[a - 1, corner]
        intensity = times_turned(table_times(tab["fine"], total), tab["fine"])
        decay = jnp.exp(-resist_slope * (intensity - resist_level))
        resist = 1.0 / (1.0 + decay)
        active = jnp.where(focus * corners + corner < count, 2.0 * resist_slope, 0.0)
        slope = active * (resist - target_ref[...]) * (decay * resist * resist)
        slope = table_times(tab["finet"], times_table(slope, tab["fine"]))
        slope = jnp.concatenate([slope, slope], axis=0)
        ge = jnp.concatenate(
            [e_ref[corner, :, s * grid : (s + 1) * grid] * slope for s in range(local_src)], axis=1
        )
        gh = table_times(tab["f1"], ge)
        gh = jnp.concatenate(
            [
                jnp.concatenate(
                    [gh[:freqs, s * grid : (s + 1) * grid], gh[freqs:, s * grid : (s + 1) * grid]],
                    axis=1,
                )
                for s in range(local_src)
            ],
            axis=0,
        )
        gg = times_turned(gh, tab["f1"])
        for s in range(local_src):
            p = p_ref[corner, s]
            part = (w_ref[s] * (2.0 / sources)) * gg[s * freqs : (s + 1) * freqs]
            sum_x = sum_x + p * part
            sum_y = sum_y + swap(p) * part
    gs = jnp.where(first, sum_x + swap(sum_x), sum_y - swap(sum_y))

    g_send[...] = gs
    g_copies = []
    for n, (a, b) in enumerate(peers):
        copy = remote(g_send, g_recv.at[n], g_ss.at[n], g_rs.at[n], peer(a, b))
        copy.start()
        g_copies.append(copy)
    for n, copy in enumerate(g_copies):
        copy.wait_recv()
        gs = gs + g_recv[n]
    zg_send[0] = gs
    zg_send[1] = gs
    zg_left, zg_right = along(zg_send, zg_recv, zg_ss, zg_rs)
    pl.when(has_left)(zg_left.start)
    pl.when(has_right)(zg_right.start)

    def stacked(g):
        turned = swap(g)
        return jnp.concatenate([g, jnp.where(first, turned, -turned)], axis=0)

    pl.when(has_left)(zg_right.wait_recv)
    pl.when(has_right)(zg_left.wait_recv)
    gx = table_times(
        tab["rowt"],
        jnp.concatenate([stacked(gs), stacked(zg_recv[0]), stacked(zg_recv[1])], axis=1),
    )
    out = times_table(gx[:, :grid], tab["own"])
    from_left = times_table(gx[:, grid : 2 * grid], tab["left"])
    from_right = times_table(gx[:, 2 * grid :], tab["right"])
    filler = jnp.zeros((rows, tile - 2 * AMBIT), jnp.float32)
    out_ref[...] = (
        out
        + jnp.concatenate([from_left, filler], axis=1)
        + jnp.concatenate([filler, from_right], axis=1)
    )

    pl.when(has_left)(zs_left.wait_send)
    pl.when(has_right)(zs_right.wait_send)
    pl.when(has_left)(zg_left.wait_send)
    pl.when(has_right)(zg_right.wait_send)
    for copy in i_copies + g_copies:
        copy.wait_send()


def per_device(mask, target, pupil, weights, counts):
    tile = mask.shape[0]
    freqs = pupil.shape[-1]
    local_src = weights.shape[0]
    corners = pupil.shape[2]
    ns, nf, nt = (lax.axis_size(axis) for axis in ("src", "focus", "tile"))
    grid = 2 * freqs
    rows = tile // (ns * nf)
    peers = ns * nf - 1
    held = tables(tile, freqs, AMBIT)
    held = {name: jnp.asarray(held[name]) for name in NAMES}
    vmem = pl.BlockSpec(memory_space=pltpu.VMEM)
    smem = pl.BlockSpec(memory_space=pltpu.SMEM)
    hbm = pl.BlockSpec(memory_space=pltpu.HBM)
    f32 = jnp.float32
    dma = pltpu.SemaphoreType.DMA
    return pl.pallas_call(
        functools.partial(kernel, (ns, nf, nt, local_src, corners, freqs, tile)),
        out_shape=jax.ShapeDtypeStruct((rows, tile), f32),
        in_specs=[smem, smem] + [hbm] * (3 + len(NAMES)),
        out_specs=vmem,
        scratch_shapes=[
            pltpu.VMEM(mask.shape, f32),
            pltpu.VMEM(target.shape, f32),
            pltpu.VMEM(pupil.shape, f32),
            *[
                pltpu.VMEM((2, rows, grid) if name == "rowt" else held[name].shape, jnp.bfloat16)
                for name in NAMES
            ],
            dma((len(NAMES) + 3,)),
            pltpu.VMEM((corners, local_src, freqs, grid), f32),
            pltpu.VMEM((corners, 2 * grid, local_src * grid), f32),
            pltpu.VMEM((2, freqs, grid), f32),
            pltpu.VMEM((2, freqs, grid), f32),
            pltpu.VMEM((corners, grid, grid), f32),
            pltpu.VMEM((max(ns - 1, 1), corners, grid, grid), f32),
            pltpu.VMEM((freqs, grid), f32),
            pltpu.VMEM((max(peers, 1), freqs, grid), f32),
            pltpu.VMEM((2, freqs, grid), f32),
            pltpu.VMEM((2, freqs, grid), f32),
            dma((2,)),
            dma((2,)),
            dma((max(ns - 1, 1), corners)),
            dma((max(ns - 1, 1), corners)),
            dma((max(peers, 1),)),
            dma((max(peers, 1),)),
            dma((2,)),
            dma((2,)),
        ],
        compiler_params=pltpu.CompilerParams(
            collective_id=0, has_side_effects=True, vmem_limit_bytes=64 * 1024 * 1024
        ),
        name="abbe_gradient",
    )(counts, weights, mask, target, pupil, *[held[name] for name in NAMES])


def solution(mesh):
    return jax.shard_map(
        per_device,
        mesh=mesh,
        in_specs=(
            P("parts", "tile"),
            P("parts", "tile"),
            P(None, "src", "focus", None, None),
            P("src"),
            P("parts"),
        ),
        out_specs=P(("parts", "src", "focus"), "tile"),
        check_vma=False,
    )
```

```python
import functools
import math

import jax
import jax.numpy as jnp
import ml_dtypes
import numpy as np
from jax import lax
from jax.experimental import pallas as pl
from jax.experimental.pallas import tpu as pltpu
from jax.sharding import PartitionSpec as P

AMBIT = 64
MESH = pl.DeviceIdType.MESH

resist_slope = 4.0
resist_level = 0.5


def halves(table):
    table = table.astype(np.float32)
    high = table.astype(ml_dtypes.bfloat16)
    low = (table - high.astype(np.float32)).astype(ml_dtypes.bfloat16)
    return np.stack([high, low])


def tables(tile, freqs, width):
    win = tile + 2 * width
    grid = 2 * freqs
    k = np.arange(freqs) - freqs // 2
    row = 2.0 * np.pi * ((k[:, None] * (np.arange(tile) + width)[None, :]) % win) / win
    row2 = np.concatenate([np.cos(row), -np.sin(row)], axis=0) / math.sqrt(win)
    col = 2.0 * np.pi * ((k[:, None] * np.arange(win)[None, :]) % win) / win
    col2 = np.concatenate([np.cos(col), -np.sin(col)], axis=0) / math.sqrt(win)
    own = col2[:, width : width + tile]
    edges = np.zeros((2, 2 * freqs, 2 * width))
    edges[0, :, :width] = col2[:, width + tile :]
    edges[1, :, width:] = col2[:, :width]
    at = 2.0 * np.pi * ((k[:, None] * np.arange(grid)[None, :]) % grid) / grid
    c, s = np.cos(at) * math.sqrt(2.0 / freqs), np.sin(at) * math.sqrt(2.0 / freqs)
    field = np.block([[c, s], [-s, c]])
    q = np.arange(1 - freqs, freqs)
    gap = (np.arange(tile) + width)[:, None] / win - np.arange(grid)[None, :] / grid
    fine = np.cos(2.0 * np.pi * gap[:, :, None] * q[None, None, :]).sum(-1) / grid
    return dict(
        row=halves(row2),
        own=halves(own),
        left=halves(edges[0]),
        right=halves(edges[1]),
        f1=halves(field),
        f2=halves(field.T),
        fine=halves(fine),
        finet=halves(fine.T),
        rowt=halves(row2.T),
    )


def split(x):
    high = x.astype(jnp.bfloat16)
    low = (x - high.astype(jnp.float32)).astype(jnp.bfloat16)
    return high, low


def dot(a, b):
    return jnp.dot(a, b, preferred_element_type=jnp.float32)


def dot_t(a, b):
    return lax.dot_general(a, b, (((1,), (1,)), ((), ())), preferred_element_type=jnp.float32)


def times_table(x, table):
    high, low = split(x)
    return dot(
        jnp.concatenate([high, high, low], axis=1),
        jnp.concatenate([table[0], table[1], table[0]], axis=0),
    )


def times_turned(x, table):
    high, low = split(x)
    return dot_t(
        jnp.concatenate([high, high, low], axis=1),
        jnp.concatenate([table[0], table[1], table[0]], axis=1),
    )


def table_times(table, x):
    high, low = split(x)
    return dot(
        jnp.concatenate([table[0], table[1], table[0]], axis=1),
        jnp.concatenate([high, high, low], axis=0),
    )


NAMES = ("row", "left", "right", "own", "f1", "f2", "fine", "finet", "rowt")


def kernel(dims, counts_ref, w_ref, mask_hbm, target_hbm, pup_hbm, *refs):
    ns, nf, nt, local_src, corners, freqs, tile = dims
    many = len(NAMES)
    held = dict(zip(NAMES, refs[:many]))
    out_ref = refs[many]
    mask_ref, target_ref, pup_ref = refs[many + 1 : many + 4]
    tab = dict(zip(NAMES, refs[many + 4 : 2 * many + 4]))
    (load_sem, p_ref, e_ref, zs_send, zs_recv, i_send, i_recv, g_send, g_recv, g_sum, g_all,
     zs_ss, zs_rs, i_ss, i_rs, g_ss, g_rs, a_ss, a_rs) = refs[2 * many + 4 :]
    grid = 2 * freqs
    rows = out_ref.shape[0]
    sources = local_src * ns
    t = lax.axis_index("tile")
    src = lax.axis_index("src")
    focus = lax.axis_index("focus")
    has_left = t > 0
    has_right = t < nt - 1
    left, right = jnp.maximum(t - 1, 0), jnp.minimum(t + 1, nt - 1)
    group = [(a, b) for a in range(ns) for b in range(nf)]
    peers = group[1:]
    piece = freqs // len(group)

    def moved(a, b):
        return lax.rem(src + a, ns), lax.rem(focus + b, nf)

    def peer(a, b):
        s, f = moved(a, b)
        return {"src": s, "focus": f}

    def across(a, b, tile_index):
        return {"tile": tile_index, **peer(a, b)}

    def remote(source, dest, ssem, rsem, device):
        return pltpu.make_async_remote_copy(
            src_ref=source, dst_ref=dest, send_sem=ssem, recv_sem=rsem,
            device_id=device, device_id_type=MESH,
        )

    begin = pl.multiple_of((src * nf + focus) * rows, 16)
    loads = {}

    def load(name, source, dest):
        loads[name] = pltpu.make_async_copy(source, dest, load_sem.at[len(loads)])
        loads[name].start()

    load("row", held["row"], tab["row"])
    load("mask", mask_hbm, mask_ref)
    for name in ("left", "right", "own"):
        load(name, held[name], tab[name])
    load("pupil", pup_hbm, pup_ref)
    for name in ("f1", "f2", "fine"):
        load(name, held[name], tab[name])
    load("target", target_hbm, target_ref)
    load("finet", held["finet"], tab["finet"])
    load("rowt", held["rowt"].at[:, pl.ds(begin, rows), :], tab["rowt"])

    def need(*names):
        for name in names:
            loads[name].wait()

    zs_recv[...] = jnp.zeros_like(zs_recv)
    g_all[...] = jnp.zeros_like(g_all)
    barrier = pltpu.get_barrier_semaphore()
    for a, b in peers:
        pl.semaphore_signal(barrier, inc=1, device_id=peer(a, b), device_id_type=MESH)

    def greet(tile_index):
        for a, b in group:
            pl.semaphore_signal(
                barrier, inc=1, device_id=across(a, b, tile_index), device_id_type=MESH
            )

    pl.when(has_left)(functools.partial(greet, left))
    pl.when(has_right)(functools.partial(greet, right))

    lane = lax.broadcasted_iota(jnp.int32, (freqs, grid), 1)
    first = lane < freqs

    def swap(x):
        return pltpu.roll(x, freqs, 1)

    def complex_of(q):
        top, low = q[:freqs], swap(q[freqs:])
        return jnp.where(first, top - low, top + low)

    need("row", "mask", "left", "right")
    ah, al = split(table_times(tab["row"], mask_ref[...]))

    def columns(begin, end, table):
        high, low = ah[:, begin:end], al[:, begin:end]
        wide = jnp.concatenate([table[0], table[1], table[0]], axis=1)
        return complex_of(dot_t(jnp.concatenate([high, high, low], axis=1), wide))

    zs_send[0] = columns(0, 2 * AMBIT, tab["left"])
    zs_send[1] = columns(tile - 2 * AMBIT, tile, tab["right"])
    pl.semaphore_wait(
        barrier,
        len(peers) + len(group) * (has_left.astype(jnp.int32) + has_right.astype(jnp.int32)),
    )
    zs_left = remote(zs_send.at[0], zs_recv.at[1], zs_ss.at[0], zs_rs.at[1], {"tile": left})
    zs_right = remote(zs_send.at[1], zs_recv.at[0], zs_ss.at[1], zs_rs.at[0], {"tile": right})
    pl.when(has_left)(zs_left.start)
    pl.when(has_right)(zs_right.start)
    need("own")
    spec = columns(0, tile, tab["own"])
    need("pupil")
    for corner in range(corners):
        for s in range(local_src):
            p_ref[corner, s] = jnp.concatenate(
                [pup_ref[0, s, corner], pup_ref[1, s, corner]], axis=1
            )
    pl.when(has_left)(zs_right.wait_recv)
    pl.when(has_right)(zs_left.wait_recv)
    spec = spec + zs_recv[0] + zs_recv[1]
    turned = swap(spec)
    same = jnp.where(first, spec, turned)
    cross = jnp.where(first, -turned, spec)

    need("f1", "f2")
    i_copies = []
    for corner in range(corners):
        parts = []
        for s in range(local_src):
            p = p_ref[corner, s]
            parts.append(p * same + swap(p) * cross)
        h = times_table(jnp.concatenate(parts, axis=0), tab["f1"])
        h = jnp.concatenate(
            [
                jnp.concatenate(
                    [h[s * freqs : (s + 1) * freqs, :grid], h[s * freqs : (s + 1) * freqs, grid:]],
                    axis=0,
                )
                for s in range(local_src)
            ],
            axis=1,
        )
        e = table_times(tab["f2"], h)
        e_ref[corner] = e
        total = jnp.zeros((grid, grid), jnp.float32)
        for s in range(local_src):
            e_re = e[:grid, s * grid : (s + 1) * grid]
            e_im = e[grid:, s * grid : (s + 1) * grid]
            total = total + (w_ref[s] * (1.0 / sources)) * (e_re * e_re + e_im * e_im)
        i_send[corner] = total
        for a in range(1, ns):
            copy = remote(
                i_send.at[corner], i_recv.at[a - 1, corner],
                i_ss.at[a - 1, corner], i_rs.at[a - 1, corner], peer(a, 0),
            )
            copy.start()
            i_copies.append(copy)

    need("fine", "target", "finet", "rowt")
    count = counts_ref[t]
    sum_x = jnp.zeros((freqs, grid), jnp.float32)
    sum_y = jnp.zeros((freqs, grid), jnp.float32)
    for corner in range(corners):
        total = i_send[corner]
        for a in range(1, ns):
            i_copies[corner * (ns - 1) + a - 1].wait_recv()
            total = total + i_recv[a - 1, corner]
        intensity = times_turned(table_times(tab["fine"], total), tab["fine"])
        wave = jnp.tanh((0.5 * resist_slope) * (intensity - resist_level))
        active = jnp.where(focus * corners + corner < count, 0.25 * resist_slope, 0.0)
        slope = active * ((1.0 - 2.0 * target_ref[...]) + wave) * (1.0 - wave * wave)
        slope = table_times(tab["finet"], times_table(slope, tab["fine"]))
        slope = jnp.concatenate([slope, slope], axis=0)
        ge = jnp.concatenate(
            [e_ref[corner, :, s * grid : (s + 1) * grid] * slope for s in range(local_src)], axis=1
        )
        gh = table_times(tab["f1"], ge)
        gh = jnp.concatenate(
            [
                jnp.concatenate(
                    [gh[:freqs, s * grid : (s + 1) * grid], gh[freqs:, s * grid : (s + 1) * grid]],
                    axis=1,
                )
                for s in range(local_src)
            ],
            axis=0,
        )
        gg = times_turned(gh, tab["f1"])
        for s in range(local_src):
            p = p_ref[corner, s]
            part = (w_ref[s] * (2.0 / sources)) * gg[s * freqs : (s + 1) * freqs]
            sum_x = sum_x + p * part
            sum_y = sum_y + swap(p) * part
    gs = jnp.where(first, sum_x + swap(sum_x), sum_y - swap(sum_y))

    g_send[...] = gs
    mine = pl.multiple_of((src * nf + focus) * piece, 8)
    g_copies = []
    for n, (a, b) in enumerate(peers):
        to_src, to_focus = moved(a, b)
        theirs = pl.multiple_of((to_src * nf + to_focus) * piece, 8)
        copy = remote(
            g_send.at[pl.ds(theirs, piece), :], g_recv.at[n], g_ss.at[n], g_rs.at[n], peer(a, b)
        )
        copy.start()
        g_copies.append(copy)
    part = g_send[pl.ds(mine, piece), :]
    for n, copy in enumerate(g_copies):
        copy.wait_recv()
        part = part + g_recv[n]
    g_sum[...] = part
    g_all[0, pl.ds(mine, piece), :] = part

    def finished(kind, n, device):
        place = g_all.at[kind, pl.ds(mine, piece), :]
        return remote(g_sum, place, a_ss.at[kind, n], a_rs.at[kind, n], device)

    a_peers = [finished(0, n, peer(a, b)) for n, (a, b) in enumerate(group) if n > 0]
    a_right = [finished(1, n, across(a, b, right)) for n, (a, b) in enumerate(group)]
    a_left = [finished(2, n, across(a, b, left)) for n, (a, b) in enumerate(group)]

    def every(copies, step):
        def run():
            for copy in copies:
                getattr(copy, step)()

        return run

    pl.when(has_left)(every(a_left, "start"))
    pl.when(has_right)(every(a_right, "start"))
    every(a_peers, "start")()

    def stacked(g):
        turned = swap(g)
        return jnp.concatenate([g, jnp.where(first, turned, -turned)], axis=0)

    every(a_peers, "wait_recv")()
    pl.when(has_left)(every(a_right, "wait_recv"))
    pl.when(has_right)(every(a_left, "wait_recv"))
    gx = table_times(
        tab["rowt"],
        jnp.concatenate([stacked(g_all[n]) for n in range(3)], axis=1),
    )
    out = times_table(gx[:, :grid], tab["own"])
    from_left = times_table(gx[:, grid : 2 * grid], tab["left"])
    from_right = times_table(gx[:, 2 * grid :], tab["right"])
    filler = jnp.zeros((rows, tile - 2 * AMBIT), jnp.float32)
    out_ref[...] = (
        out
        + jnp.concatenate([from_left, filler], axis=1)
        + jnp.concatenate([filler, from_right], axis=1)
    )

    pl.when(has_left)(zs_left.wait_send)
    pl.when(has_right)(zs_right.wait_send)
    pl.when(has_left)(every(a_left, "wait_send"))
    pl.when(has_right)(every(a_right, "wait_send"))
    for copy in i_copies + g_copies + a_peers:
        copy.wait_send()


def per_device(mask, target, pupil, weights, counts):
    tile = mask.shape[0]
    freqs = pupil.shape[-1]
    local_src = weights.shape[0]
    corners = pupil.shape[2]
    ns, nf, nt = (lax.axis_size(axis) for axis in ("src", "focus", "tile"))
    grid = 2 * freqs
    rows = tile // (ns * nf)
    peers = ns * nf - 1
    piece = freqs // (ns * nf)
    held = tables(tile, freqs, AMBIT)
    held = {name: jnp.asarray(held[name]) for name in NAMES}
    vmem = pl.BlockSpec(memory_space=pltpu.VMEM)
    smem = pl.BlockSpec(memory_space=pltpu.SMEM)
    hbm = pl.BlockSpec(memory_space=pltpu.HBM)
    f32 = jnp.float32
    dma = pltpu.SemaphoreType.DMA
    return pl.pallas_call(
        functools.partial(kernel, (ns, nf, nt, local_src, corners, freqs, tile)),
        out_shape=jax.ShapeDtypeStruct((rows, tile), f32),
        in_specs=[smem, smem] + [hbm] * (3 + len(NAMES)),
        out_specs=vmem,
        scratch_shapes=[
            pltpu.VMEM(mask.shape, f32),
            pltpu.VMEM(target.shape, f32),
            pltpu.VMEM(pupil.shape, f32),
            *[
                pltpu.VMEM((2, rows, grid) if name == "rowt" else held[name].shape, jnp.bfloat16)
                for name in NAMES
            ],
            dma((len(NAMES) + 3,)),
            pltpu.VMEM((corners, local_src, freqs, grid), f32),
            pltpu.VMEM((corners, 2 * grid, local_src * grid), f32),
            pltpu.VMEM((2, freqs, grid), f32),
            pltpu.VMEM((2, freqs, grid), f32),
            pltpu.VMEM((corners, grid, grid), f32),
            pltpu.VMEM((max(ns - 1, 1), corners, grid, grid), f32),
            pltpu.VMEM((freqs, grid), f32),
            pltpu.VMEM((max(peers, 1), piece, grid), f32),
            pltpu.VMEM((piece, grid), f32),
            pltpu.VMEM((3, freqs, grid), f32),
            dma((2,)),
            dma((2,)),
            dma((max(ns - 1, 1), corners)),
            dma((max(ns - 1, 1), corners)),
            dma((max(peers, 1),)),
            dma((max(peers, 1),)),
            dma((3, peers + 1)),
            dma((3, peers + 1)),
        ],
        compiler_params=pltpu.CompilerParams(
            collective_id=0, has_side_effects=True, vmem_limit_bytes=64 * 1024 * 1024
        ),
        name="abbe_gradient",
    )(counts, weights, mask, target, pupil, *[held[name] for name in NAMES])


def solution(mesh):
    return jax.shard_map(
        per_device,
        mesh=mesh,
        in_specs=(
            P("parts", "tile"),
            P("parts", "tile"),
            P(None, "src", "focus", None, None),
            P("src"),
            P("parts"),
        ),
        out_specs=P(("parts", "src", "focus"), "tile"),
        check_vma=False,
    )
```

```python
import functools
import math

import jax
import jax.numpy as jnp
import ml_dtypes
import numpy as np
from jax import lax
from jax.experimental import pallas as pl
from jax.experimental.pallas import tpu as pltpu
from jax.sharding import PartitionSpec as P

AMBIT = 64
MESH = pl.DeviceIdType.MESH

resist_slope = 4.0
resist_level = 0.5


def halves(table):
    table = table.astype(np.float32)
    high = table.astype(ml_dtypes.bfloat16)
    low = (table - high.astype(np.float32)).astype(ml_dtypes.bfloat16)
    return np.stack([high, low])


def tables(tile, freqs, width):
    win = tile + 2 * width
    grid = 2 * freqs
    k = np.arange(freqs) - freqs // 2
    row = 2.0 * np.pi * ((k[:, None] * (np.arange(tile) + width)[None, :]) % win) / win
    row2 = np.concatenate([np.cos(row), -np.sin(row)], axis=0) / math.sqrt(win)
    col = 2.0 * np.pi * ((k[:, None] * np.arange(win)[None, :]) % win) / win
    col2 = np.concatenate([np.cos(col), -np.sin(col)], axis=0) / math.sqrt(win)
    own = col2[:, width : width + tile]
    edges = np.zeros((2, 2 * freqs, 2 * width))
    edges[0, :, :width] = col2[:, width + tile :]
    edges[1, :, width:] = col2[:, :width]
    at = 2.0 * np.pi * ((k[:, None] * np.arange(grid)[None, :]) % grid) / grid
    c, s = np.cos(at) * math.sqrt(2.0 / freqs), np.sin(at) * math.sqrt(2.0 / freqs)
    field = np.block([[c, s], [-s, c]])
    q = np.arange(1 - freqs, freqs)
    gap = (np.arange(tile) + width)[:, None] / win - np.arange(grid)[None, :] / grid
    fine = np.cos(2.0 * np.pi * gap[:, :, None] * q[None, None, :]).sum(-1) / grid
    return dict(
        row=halves(row2),
        own=halves(own),
        left=halves(edges[0]),
        right=halves(edges[1]),
        f1=halves(field),
        f2=halves(field.T),
        fine=halves(fine),
        finet=halves(fine.T),
        rowt=halves(row2.T),
    )


def split(x):
    high = x.astype(jnp.bfloat16)
    low = (x - high.astype(jnp.float32)).astype(jnp.bfloat16)
    return high, low


def dot(a, b):
    return jnp.dot(a, b, preferred_element_type=jnp.float32)


def dot_t(a, b):
    return lax.dot_general(a, b, (((1,), (1,)), ((), ())), preferred_element_type=jnp.float32)


def times_table(x, table):
    high, low = split(x)
    return dot(
        jnp.concatenate([high, high, low], axis=1),
        jnp.concatenate([table[0], table[1], table[0]], axis=0),
    )


def times_turned(x, table):
    high, low = split(x)
    return dot_t(
        jnp.concatenate([high, high, low], axis=1),
        jnp.concatenate([table[0], table[1], table[0]], axis=1),
    )


def table_times(table, x):
    high, low = split(x)
    return dot(
        jnp.concatenate([table[0], table[1], table[0]], axis=1),
        jnp.concatenate([high, high, low], axis=0),
    )


NAMES = ("row", "left", "right", "own", "f1", "f2", "fine", "finet", "rowt")


def kernel(dims, counts_ref, w_ref, mask_hbm, target_hbm, pup_hbm, *refs):
    ns, nf, nt, local_src, corners, freqs, tile = dims
    many = len(NAMES)
    held = dict(zip(NAMES, refs[:many]))
    out_ref = refs[many]
    mask_ref, target_ref, pup_ref = refs[many + 1 : many + 4]
    tab = dict(zip(NAMES, refs[many + 4 : 2 * many + 4]))
    (load_sem, p_ref, e_ref, zs_send, zs_recv, i_send, i_recv, g_send, g_recv, zg_send, zg_recv,
     zs_ss, zs_rs, i_ss, i_rs, g_ss, g_rs, zg_ss, zg_rs) = refs[2 * many + 4 :]
    grid = 2 * freqs
    rows = out_ref.shape[0]
    sources = local_src * ns
    t = lax.axis_index("tile")
    src = lax.axis_index("src")
    focus = lax.axis_index("focus")
    has_left = t > 0
    has_right = t < nt - 1
    left = {"tile": jnp.maximum(t - 1, 0)}
    right = {"tile": jnp.minimum(t + 1, nt - 1)}
    peers = [(a, b) for a in range(ns) for b in range(nf) if a + b > 0]

    def peer(a, b):
        return {"src": lax.rem(src + a, ns), "focus": lax.rem(focus + b, nf)}

    def remote(source, dest, ssem, rsem, device):
        return pltpu.make_async_remote_copy(
            src_ref=source, dst_ref=dest, send_sem=ssem, recv_sem=rsem,
            device_id=device, device_id_type=MESH,
        )

    def along(send, recv, ssem, rsem):
        return (
            remote(send.at[0], recv.at[1], ssem.at[0], rsem.at[1], left),
            remote(send.at[1], recv.at[0], ssem.at[1], rsem.at[0], right),
        )

    begin = pl.multiple_of((src * nf + focus) * rows, 16)
    loads = {}

    def load(name, source, dest):
        loads[name] = pltpu.make_async_copy(source, dest, load_sem.at[len(loads)])
        loads[name].start()

    load("row", held["row"], tab["row"])
    load("mask", mask_hbm, mask_ref)
    for name in ("left", "right", "own"):
        load(name, held[name], tab[name])
    load("pupil", pup_hbm, pup_ref)
    for name in ("f1", "f2", "fine"):
        load(name, held[name], tab[name])
    load("target", target_hbm, target_ref)
    load("finet", held["finet"], tab["finet"])
    load("rowt", held["rowt"].at[:, pl.ds(begin, rows), :], tab["rowt"])

    def need(*names):
        for name in names:
            loads[name].wait()

    zs_recv[...] = jnp.zeros_like(zs_recv)
    zg_recv[...] = jnp.zeros_like(zg_recv)
    barrier = pltpu.get_barrier_semaphore()
    for a, b in peers:
        pl.semaphore_signal(barrier, inc=1, device_id=peer(a, b), device_id_type=MESH)

    @pl.when(has_left)
    def _():
        pl.semaphore_signal(barrier, inc=1, device_id=left, device_id_type=MESH)

    @pl.when(has_right)
    def _():
        pl.semaphore_signal(barrier, inc=1, device_id=right, device_id_type=MESH)

    lane = lax.broadcasted_iota(jnp.int32, (freqs, grid), 1)
    first = lane < freqs

    def swap(x):
        return pltpu.roll(x, freqs, 1)

    def complex_of(q):
        top, low = q[:freqs], swap(q[freqs:])
        return jnp.where(first, top - low, top + low)

    need("row", "mask", "left", "right")
    ah, al = split(table_times(tab["row"], mask_ref[...]))

    def columns(begin, end, table):
        high, low = ah[:, begin:end], al[:, begin:end]
        wide = jnp.concatenate([table[0], table[1], table[0]], axis=1)
        return complex_of(dot_t(jnp.concatenate([high, high, low], axis=1), wide))

    zs_send[0] = columns(0, 2 * AMBIT, tab["left"])
    zs_send[1] = columns(tile - 2 * AMBIT, tile, tab["right"])
    pl.semaphore_wait(
        barrier, len(peers) + has_left.astype(jnp.int32) + has_right.astype(jnp.int32)
    )
    zs_left, zs_right = along(zs_send, zs_recv, zs_ss, zs_rs)
    pl.when(has_left)(zs_left.start)
    pl.when(has_right)(zs_right.start)
    need("own")
    spec = columns(0, tile, tab["own"])
    need("pupil")
    for corner in range(corners):
        for s in range(local_src):
            p_ref[corner, s] = jnp.concatenate(
                [pup_ref[0, s, corner], pup_ref[1, s, corner]], axis=1
            )
    pl.when(has_left)(zs_right.wait_recv)
    pl.when(has_right)(zs_left.wait_recv)
    spec = spec + zs_recv[0] + zs_recv[1]
    turned = swap(spec)
    same = jnp.where(first, spec, turned)
    cross = jnp.where(first, -turned, spec)

    need("f1", "f2")
    i_copies = []
    for corner in range(corners):
        parts = []
        for s in range(local_src):
            p = p_ref[corner, s]
            parts.append(p * same + swap(p) * cross)
        h = times_table(jnp.concatenate(parts, axis=0), tab["f1"])
        h = jnp.concatenate(
            [
                jnp.concatenate(
                    [h[s * freqs : (s + 1) * freqs, :grid], h[s * freqs : (s + 1) * freqs, grid:]],
                    axis=0,
                )
                for s in range(local_src)
            ],
            axis=1,
        )
        e = table_times(tab["f2"], h)
        e_ref[corner] = e
        total = jnp.zeros((grid, grid), jnp.float32)
        for s in range(local_src):
            e_re = e[:grid, s * grid : (s + 1) * grid]
            e_im = e[grid:, s * grid : (s + 1) * grid]
            total = total + (w_ref[s] * (1.0 / sources)) * (e_re * e_re + e_im * e_im)
        i_send[corner] = total
        for a in range(1, ns):
            copy = remote(
                i_send.at[corner], i_recv.at[a - 1, corner],
                i_ss.at[a - 1, corner], i_rs.at[a - 1, corner], peer(a, 0),
            )
            copy.start()
            i_copies.append(copy)

    need("fine", "target", "finet", "rowt")
    count = counts_ref[t]
    sum_x = jnp.zeros((freqs, grid), jnp.float32)
    sum_y = jnp.zeros((freqs, grid), jnp.float32)
    for corner in range(corners):
        total = i_send[corner]
        for a in range(1, ns):
            i_copies[corner * (ns - 1) + a - 1].wait_recv()
            total = total + i_recv[a - 1, corner]
        intensity = times_turned(table_times(tab["fine"], total), tab["fine"])
        wave = jnp.tanh((0.5 * resist_slope) * (intensity - resist_level))
        active = jnp.where(focus * corners + corner < count, 0.25 * resist_slope, 0.0)
        slope = active * ((1.0 - 2.0 * target_ref[...]) + wave) * (1.0 - wave * wave)
        slope = table_times(tab["finet"], times_table(slope, tab["fine"]))
        slope = jnp.concatenate([slope, slope], axis=0)
        ge = jnp.concatenate(
            [e_ref[corner, :, s * grid : (s + 1) * grid] * slope for s in range(local_src)], axis=1
        )
        gh = table_times(tab["f1"], ge)
        gh = jnp.concatenate(
            [
                jnp.concatenate(
                    [gh[:freqs, s * grid : (s + 1) * grid], gh[freqs:, s * grid : (s + 1) * grid]],
                    axis=1,
                )
                for s in range(local_src)
            ],
            axis=0,
        )
        gg = times_turned(gh, tab["f1"])
        for s in range(local_src):
            p = p_ref[corner, s]
            part = (w_ref[s] * (2.0 / sources)) * gg[s * freqs : (s + 1) * freqs]
            sum_x = sum_x + p * part
            sum_y = sum_y + swap(p) * part
    gs = jnp.where(first, sum_x + swap(sum_x), sum_y - swap(sum_y))

    g_send[...] = gs
    g_copies = []
    for n, (a, b) in enumerate(peers):
        copy = remote(g_send, g_recv.at[n], g_ss.at[n], g_rs.at[n], peer(a, b))
        copy.start()
        g_copies.append(copy)
    for n, copy in enumerate(g_copies):
        copy.wait_recv()
        gs = gs + g_recv[n]
    zg_send[0] = gs
    zg_send[1] = gs
    zg_left, zg_right = along(zg_send, zg_recv, zg_ss, zg_rs)
    pl.when(has_left)(zg_left.start)
    pl.when(has_right)(zg_right.start)

    def stacked(g):
        turned = swap(g)
        return jnp.concatenate([g, jnp.where(first, turned, -turned)], axis=0)

    out = times_table(table_times(tab["rowt"], stacked(gs)), tab["own"])
    pl.when(has_left)(zg_right.wait_recv)
    pl.when(has_right)(zg_left.wait_recv)
    gx = table_times(
        tab["rowt"], jnp.concatenate([stacked(zg_recv[0]), stacked(zg_recv[1])], axis=1)
    )
    edge = 2 * AMBIT
    from_left = times_table(gx[:, :grid], tab["left"])
    from_right = times_table(gx[:, grid:], tab["right"])
    out_ref[:, :edge] = out[:, :edge] + from_left
    out_ref[:, edge : tile - edge] = out[:, edge : tile - edge]
    out_ref[:, tile - edge :] = out[:, tile - edge :] + from_right

    pl.when(has_left)(zs_left.wait_send)
    pl.when(has_right)(zs_right.wait_send)
    pl.when(has_left)(zg_left.wait_send)
    pl.when(has_right)(zg_right.wait_send)
    for copy in i_copies + g_copies:
        copy.wait_send()


def per_device(mask, target, pupil, weights, counts):
    tile = mask.shape[0]
    freqs = pupil.shape[-1]
    local_src = weights.shape[0]
    corners = pupil.shape[2]
    ns, nf, nt = (lax.axis_size(axis) for axis in ("src", "focus", "tile"))
    grid = 2 * freqs
    rows = tile // (ns * nf)
    peers = ns * nf - 1
    held = tables(tile, freqs, AMBIT)
    held = {name: jnp.asarray(held[name]) for name in NAMES}
    vmem = pl.BlockSpec(memory_space=pltpu.VMEM)
    smem = pl.BlockSpec(memory_space=pltpu.SMEM)
    hbm = pl.BlockSpec(memory_space=pltpu.HBM)
    f32 = jnp.float32
    dma = pltpu.SemaphoreType.DMA
    return pl.pallas_call(
        functools.partial(kernel, (ns, nf, nt, local_src, corners, freqs, tile)),
        out_shape=jax.ShapeDtypeStruct((rows, tile), f32),
        in_specs=[smem, smem] + [hbm] * (3 + len(NAMES)),
        out_specs=vmem,
        scratch_shapes=[
            pltpu.VMEM(mask.shape, f32),
            pltpu.VMEM(target.shape, f32),
            pltpu.VMEM(pupil.shape, f32),
            *[
                pltpu.VMEM((2, rows, grid) if name == "rowt" else held[name].shape, jnp.bfloat16)
                for name in NAMES
            ],
            dma((len(NAMES) + 3,)),
            pltpu.VMEM((corners, local_src, freqs, grid), f32),
            pltpu.VMEM((corners, 2 * grid, local_src * grid), f32),
            pltpu.VMEM((2, freqs, grid), f32),
            pltpu.VMEM((2, freqs, grid), f32),
            pltpu.VMEM((corners, grid, grid), f32),
            pltpu.VMEM((max(ns - 1, 1), corners, grid, grid), f32),
            pltpu.VMEM((freqs, grid), f32),
            pltpu.VMEM((max(peers, 1), freqs, grid), f32),
            pltpu.VMEM((2, freqs, grid), f32),
            pltpu.VMEM((2, freqs, grid), f32),
            dma((2,)),
            dma((2,)),
            dma((max(ns - 1, 1), corners)),
            dma((max(ns - 1, 1), corners)),
            dma((max(peers, 1),)),
            dma((max(peers, 1),)),
            dma((2,)),
            dma((2,)),
        ],
        compiler_params=pltpu.CompilerParams(
            collective_id=0, has_side_effects=True, vmem_limit_bytes=64 * 1024 * 1024
        ),
        name="abbe_gradient",
    )(counts, weights, mask, target, pupil, *[held[name] for name in NAMES])


def solution(mesh):
    return jax.shard_map(
        per_device,
        mesh=mesh,
        in_specs=(
            P("parts", "tile"),
            P("parts", "tile"),
            P(None, "src", "focus", None, None),
            P("src"),
            P("parts"),
        ),
        out_specs=P(("parts", "src", "focus"), "tile"),
        check_vma=False,
    )
```

```python
import functools
import math

import jax
import jax.numpy as jnp
import ml_dtypes
import numpy as np
from jax import lax
from jax.experimental import pallas as pl
from jax.experimental.pallas import tpu as pltpu
from jax.sharding import PartitionSpec as P

AMBIT = 64
MESH = pl.DeviceIdType.MESH

resist_slope = 4.0
resist_level = 0.5


def halves(table):
    table = table.astype(np.float32)
    high = table.astype(ml_dtypes.bfloat16)
    low = (table - high.astype(np.float32)).astype(ml_dtypes.bfloat16)
    return np.stack([high, low])


def tables(tile, freqs, width):
    win = tile + 2 * width
    grid = 2 * freqs
    k = np.arange(freqs) - freqs // 2
    row = 2.0 * np.pi * ((k[:, None] * (np.arange(tile) + width)[None, :]) % win) / win
    row2 = np.concatenate([np.cos(row), -np.sin(row)], axis=0) / math.sqrt(win)
    col = 2.0 * np.pi * ((k[:, None] * np.arange(win)[None, :]) % win) / win
    col2 = np.concatenate([np.cos(col), -np.sin(col)], axis=0) / math.sqrt(win)
    own = col2[:, width : width + tile]
    edges = np.zeros((2, 2 * freqs, 2 * width))
    edges[0, :, :width] = col2[:, width + tile :]
    edges[1, :, width:] = col2[:, :width]
    at = 2.0 * np.pi * ((k[:, None] * np.arange(grid)[None, :]) % grid) / grid
    c, s = np.cos(at) * math.sqrt(2.0 / freqs), np.sin(at) * math.sqrt(2.0 / freqs)
    field = np.block([[c, s], [-s, c]])
    q = np.arange(1 - freqs, freqs)
    gap = (np.arange(tile) + width)[:, None] / win - np.arange(grid)[None, :] / grid
    fine = np.cos(2.0 * np.pi * gap[:, :, None] * q[None, None, :]).sum(-1) / grid
    return dict(
        row=halves(row2),
        own=halves(own),
        left=halves(edges[0]),
        right=halves(edges[1]),
        f1=halves(field),
        f2=halves(field.T),
        fine=halves(fine),
        finet=halves(fine.T),
        rowt=halves(row2.T),
    )


def split(x):
    high = x.astype(jnp.bfloat16)
    low = (x - high.astype(jnp.float32)).astype(jnp.bfloat16)
    return high, low


def dot(a, b):
    return jnp.dot(a, b, preferred_element_type=jnp.float32)


def dot_t(a, b):
    return lax.dot_general(a, b, (((1,), (1,)), ((), ())), preferred_element_type=jnp.float32)


def times_table(x, table):
    high, low = split(x)
    return dot(
        jnp.concatenate([high, high, low], axis=1),
        jnp.concatenate([table[0], table[1], table[0]], axis=0),
    )


def times_turned(x, table):
    high, low = split(x)
    return dot_t(
        jnp.concatenate([high, high, low], axis=1),
        jnp.concatenate([table[0], table[1], table[0]], axis=1),
    )


def table_times(table, x):
    high, low = split(x)
    return dot(
        jnp.concatenate([table[0], table[1], table[0]], axis=1),
        jnp.concatenate([high, high, low], axis=0),
    )


NAMES = ("row", "left", "right", "own", "f1", "f2", "fine", "finet", "rowt")


def kernel(dims, counts_ref, w_ref, mask_hbm, target_hbm, pup_hbm, *refs):
    ns, nf, nt, local_src, corners, freqs, tile = dims
    many = len(NAMES)
    held = dict(zip(NAMES, refs[:many]))
    out_ref = refs[many]
    mask_ref, target_ref, pup_ref = refs[many + 1 : many + 4]
    tab = dict(zip(NAMES, refs[many + 4 : 2 * many + 4]))
    (load_sem, p_ref, e_ref, zs_send, zs_recv, i_send, i_recv, g_send, g_recv, c_recv, g_half, g_all,
     zs_ss, zs_rs, i_ss, i_rs, g_ss, g_rs, c_ss, c_rs, h_ss, h_rs) = refs[2 * many + 4 :]
    grid = 2 * freqs
    rows = out_ref.shape[0]
    sources = local_src * ns
    t = lax.axis_index("tile")
    src = lax.axis_index("src")
    focus = lax.axis_index("focus")
    has_left = t > 0
    has_right = t < nt - 1
    left, right = jnp.maximum(t - 1, 0), jnp.minimum(t + 1, nt - 1)
    half = freqs // nf
    mine = pl.multiple_of(focus * half, 8)

    def chip(a):
        return lax.rem(src + a, ns)

    def core(b):
        return lax.rem(focus + b, nf)

    def remote(source, dest, ssem, rsem, device):
        return pltpu.make_async_remote_copy(
            src_ref=source, dst_ref=dest, send_sem=ssem, recv_sem=rsem,
            device_id=device, device_id_type=MESH,
        )

    begin = pl.multiple_of((src * nf + focus) * rows, 16)
    loads = {}

    def load(name, source, dest):
        loads[name] = pltpu.make_async_copy(source, dest, load_sem.at[len(loads)])
        loads[name].start()

    load("row", held["row"], tab["row"])
    load("mask", mask_hbm, mask_ref)
    for name in ("left", "right", "own"):
        load(name, held[name], tab[name])
    load("pupil", pup_hbm, pup_ref)
    for name in ("f1", "f2", "fine"):
        load(name, held[name], tab[name])
    load("target", target_hbm, target_ref)
    load("finet", held["finet"], tab["finet"])
    load("rowt", held["rowt"].at[:, pl.ds(begin, rows), :], tab["rowt"])

    def need(*names):
        for name in names:
            loads[name].wait()

    zs_recv[...] = jnp.zeros_like(zs_recv)
    c_recv[...] = jnp.zeros_like(c_recv)
    barrier = pltpu.get_barrier_semaphore()

    def greet(device):
        pl.semaphore_signal(barrier, inc=1, device_id=device, device_id_type=MESH)

    for b in range(1, nf):
        greet({"focus": core(b)})
    for a in range(1, ns):
        greet({"src": chip(a)})

    def greet_tile(tile_index):
        for a in range(ns):
            greet({"tile": tile_index, "src": chip(a)})

    pl.when(has_left)(functools.partial(greet_tile, left))
    pl.when(has_right)(functools.partial(greet_tile, right))

    lane = lax.broadcasted_iota(jnp.int32, (freqs, grid), 1)
    first = lane < freqs

    def swap(x):
        return pltpu.roll(x, freqs, 1)

    def complex_of(q):
        top, low = q[:freqs], swap(q[freqs:])
        return jnp.where(first, top - low, top + low)

    need("row", "mask", "left", "right")
    ah, al = split(table_times(tab["row"], mask_ref[...]))

    def columns(begin, end, table):
        high, low = ah[:, begin:end], al[:, begin:end]
        wide = jnp.concatenate([table[0], table[1], table[0]], axis=1)
        return complex_of(dot_t(jnp.concatenate([high, high, low], axis=1), wide))

    zs_send[0] = columns(0, 2 * AMBIT, tab["left"])
    zs_send[1] = columns(tile - 2 * AMBIT, tile, tab["right"])
    pl.semaphore_wait(
        barrier,
        (ns + nf - 2) + ns * (has_left.astype(jnp.int32) + has_right.astype(jnp.int32)),
    )
    zs_left = remote(zs_send.at[0], zs_recv.at[1], zs_ss.at[0], zs_rs.at[1], {"tile": left})
    zs_right = remote(zs_send.at[1], zs_recv.at[0], zs_ss.at[1], zs_rs.at[0], {"tile": right})
    pl.when(has_left)(zs_left.start)
    pl.when(has_right)(zs_right.start)
    need("own")
    spec = columns(0, tile, tab["own"])
    need("pupil")
    for corner in range(corners):
        for s in range(local_src):
            p_ref[corner, s] = jnp.concatenate(
                [pup_ref[0, s, corner], pup_ref[1, s, corner]], axis=1
            )
    pl.when(has_left)(zs_right.wait_recv)
    pl.when(has_right)(zs_left.wait_recv)
    spec = spec + zs_recv[0] + zs_recv[1]
    turned = swap(spec)
    same = jnp.where(first, spec, turned)
    cross = jnp.where(first, -turned, spec)

    need("f1", "f2")
    i_copies = []
    for corner in range(corners):
        parts = []
        for s in range(local_src):
            p = p_ref[corner, s]
            parts.append(p * same + swap(p) * cross)
        h = times_table(jnp.concatenate(parts, axis=0), tab["f1"])
        h = jnp.concatenate(
            [
                jnp.concatenate(
                    [h[s * freqs : (s + 1) * freqs, :grid], h[s * freqs : (s + 1) * freqs, grid:]],
                    axis=0,
                )
                for s in range(local_src)
            ],
            axis=1,
        )
        e = table_times(tab["f2"], h)
        e_ref[corner] = e
        total = jnp.zeros((grid, grid), jnp.float32)
        for s in range(local_src):
            e_re = e[:grid, s * grid : (s + 1) * grid]
            e_im = e[grid:, s * grid : (s + 1) * grid]
            total = total + (w_ref[s] * (1.0 / sources)) * (e_re * e_re + e_im * e_im)
        i_send[corner] = total
        for a in range(1, ns):
            copy = remote(
                i_send.at[corner], i_recv.at[a - 1, corner],
                i_ss.at[a - 1, corner], i_rs.at[a - 1, corner], {"src": chip(a)},
            )
            copy.start()
            i_copies.append(copy)

    need("fine", "target", "finet", "rowt")
    count = counts_ref[t]
    sum_x = jnp.zeros((freqs, grid), jnp.float32)
    sum_y = jnp.zeros((freqs, grid), jnp.float32)
    for corner in range(corners):
        total = i_send[corner]
        for a in range(1, ns):
            i_copies[corner * (ns - 1) + a - 1].wait_recv()
            total = total + i_recv[a - 1, corner]
        intensity = times_turned(table_times(tab["fine"], total), tab["fine"])
        wave = jnp.tanh((0.5 * resist_slope) * (intensity - resist_level))
        active = jnp.where(focus * corners + corner < count, 0.25 * resist_slope, 0.0)
        slope = active * ((1.0 - 2.0 * target_ref[...]) + wave) * (1.0 - wave * wave)
        slope = table_times(tab["finet"], times_table(slope, tab["fine"]))
        slope = jnp.concatenate([slope, slope], axis=0)
        ge = jnp.concatenate(
            [e_ref[corner, :, s * grid : (s + 1) * grid] * slope for s in range(local_src)], axis=1
        )
        gh = table_times(tab["f1"], ge)
        gh = jnp.concatenate(
            [
                jnp.concatenate(
                    [gh[:freqs, s * grid : (s + 1) * grid], gh[freqs:, s * grid : (s + 1) * grid]],
                    axis=1,
                )
                for s in range(local_src)
            ],
            axis=0,
        )
        gg = times_turned(gh, tab["f1"])
        for s in range(local_src):
            p = p_ref[corner, s]
            part = (w_ref[s] * (2.0 / sources)) * gg[s * freqs : (s + 1) * freqs]
            sum_x = sum_x + p * part
            sum_y = sum_y + swap(p) * part
    gs = jnp.where(first, sum_x + swap(sum_x), sum_y - swap(sum_y))

    def every(copies, step):
        def run():
            for copy in copies:
                getattr(copy, step)()

        return run

    g_send[...] = gs
    g_copies = []
    for b in range(1, nf):
        theirs = pl.multiple_of(core(b) * half, 8)
        g_copies.append(
            remote(
                g_send.at[pl.ds(theirs, half), :], g_recv.at[b - 1],
                g_ss.at[b - 1], g_rs.at[b - 1], {"focus": core(b)},
            )
        )
    every(g_copies, "start")()
    part = g_send[pl.ds(mine, half), :]
    for b, copy in enumerate(g_copies):
        copy.wait_recv()
        part = part + g_recv[b]
    c_recv[0, 0] = part

    def onward(kind, a, device):
        return remote(
            c_recv.at[0, 0], c_recv.at[kind, a], c_ss.at[kind, a], c_rs.at[kind, a],
            {"src": chip(a), **device},
        )

    chips = range(ns - 1, -1, -1)
    c_peers = [onward(0, a, {}) for a in chips if a > 0]
    c_right = [onward(1, a, {"tile": right}) for a in chips]
    c_left = [onward(2, a, {"tile": left}) for a in chips]
    pl.when(has_left)(every(c_left, "start"))
    pl.when(has_right)(every(c_right, "start"))
    every(c_peers, "start")()
    every(c_peers, "wait_recv")()
    pl.when(has_left)(every(c_right, "wait_recv"))
    pl.when(has_right)(every(c_left, "wait_recv"))
    for kind in range(3):
        total = c_recv[kind, 0]
        for a in range(1, ns):
            total = total + c_recv[kind, a]
        g_half[kind] = total
        g_all[kind, pl.ds(mine, half), :] = total

    h_copies = [
        remote(
            g_half, g_all.at[:, pl.ds(mine, half), :],
            h_ss.at[b - 1], h_rs.at[b - 1], {"focus": core(b)},
        )
        for b in range(1, nf)
    ]
    every(h_copies, "start")()

    def stacked(g):
        turned = swap(g)
        return jnp.concatenate([g, jnp.where(first, turned, -turned)], axis=0)

    every(h_copies, "wait_recv")()
    gx = table_times(
        tab["rowt"], jnp.concatenate([stacked(g_all[kind]) for kind in range(3)], axis=1)
    )
    out = times_table(gx[:, :grid], tab["own"])
    gx = gx[:, grid:]
    edge = 2 * AMBIT
    from_left = times_table(gx[:, :grid], tab["left"])
    from_right = times_table(gx[:, grid:], tab["right"])
    out_ref[:, :edge] = out[:, :edge] + from_left
    out_ref[:, edge : tile - edge] = out[:, edge : tile - edge]
    out_ref[:, tile - edge :] = out[:, tile - edge :] + from_right

    pl.when(has_left)(zs_left.wait_send)
    pl.when(has_right)(zs_right.wait_send)
    pl.when(has_left)(every(c_left, "wait_send"))
    pl.when(has_right)(every(c_right, "wait_send"))
    for copy in i_copies + g_copies + c_peers + h_copies:
        copy.wait_send()


def per_device(mask, target, pupil, weights, counts):
    tile = mask.shape[0]
    freqs = pupil.shape[-1]
    local_src = weights.shape[0]
    corners = pupil.shape[2]
    ns, nf, nt = (lax.axis_size(axis) for axis in ("src", "focus", "tile"))
    grid = 2 * freqs
    rows = tile // (ns * nf)
    half = freqs // nf
    held = tables(tile, freqs, AMBIT)
    held = {name: jnp.asarray(held[name]) for name in NAMES}
    vmem = pl.BlockSpec(memory_space=pltpu.VMEM)
    smem = pl.BlockSpec(memory_space=pltpu.SMEM)
    hbm = pl.BlockSpec(memory_space=pltpu.HBM)
    f32 = jnp.float32
    dma = pltpu.SemaphoreType.DMA
    return pl.pallas_call(
        functools.partial(kernel, (ns, nf, nt, local_src, corners, freqs, tile)),
        out_shape=jax.ShapeDtypeStruct((rows, tile), f32),
        in_specs=[smem, smem] + [hbm] * (3 + len(NAMES)),
        out_specs=vmem,
        scratch_shapes=[
            pltpu.VMEM(mask.shape, f32),
            pltpu.VMEM(target.shape, f32),
            pltpu.VMEM(pupil.shape, f32),
            *[
                pltpu.VMEM((2, rows, grid) if name == "rowt" else held[name].shape, jnp.bfloat16)
                for name in NAMES
            ],
            dma((len(NAMES) + 3,)),
            pltpu.VMEM((corners, local_src, freqs, grid), f32),
            pltpu.VMEM((corners, 2 * grid, local_src * grid), f32),
            pltpu.VMEM((2, freqs, grid), f32),
            pltpu.VMEM((2, freqs, grid), f32),
            pltpu.VMEM((corners, grid, grid), f32),
            pltpu.VMEM((max(ns - 1, 1), corners, grid, grid), f32),
            pltpu.VMEM((freqs, grid), f32),
            pltpu.VMEM((max(nf - 1, 1), half, grid), f32),
            pltpu.VMEM((3, ns, half, grid), f32),
            pltpu.VMEM((3, half, grid), f32),
            pltpu.VMEM((3, freqs, grid), f32),
            dma((2,)),
            dma((2,)),
            dma((max(ns - 1, 1), corners)),
            dma((max(ns - 1, 1), corners)),
            dma((max(nf - 1, 1),)),
            dma((max(nf - 1, 1),)),
            dma((3, ns)),
            dma((3, ns)),
            dma((max(nf - 1, 1),)),
            dma((max(nf - 1, 1),)),
        ],
        compiler_params=pltpu.CompilerParams(
            collective_id=0, has_side_effects=True, vmem_limit_bytes=64 * 1024 * 1024
        ),
        name="abbe_gradient",
    )(counts, weights, mask, target, pupil, *[held[name] for name in NAMES])


def solution(mesh):
    return jax.shard_map(
        per_device,
        mesh=mesh,
        in_specs=(
            P("parts", "tile"),
            P("parts", "tile"),
            P(None, "src", "focus", None, None),
            P("src"),
            P("parts"),
        ),
        out_specs=P(("parts", "src", "focus"), "tile"),
        check_vma=False,
    )
```

```python
import functools
import math

import jax
import jax.numpy as jnp
import ml_dtypes
import numpy as np
from jax import lax
from jax.experimental import pallas as pl
from jax.experimental.pallas import tpu as pltpu
from jax.sharding import PartitionSpec as P

AMBIT = 64
MESH = pl.DeviceIdType.MESH

resist_slope = 4.0
resist_level = 0.5


def halves(table):
    table = table.astype(np.float32)
    high = table.astype(ml_dtypes.bfloat16)
    low = (table - high.astype(np.float32)).astype(ml_dtypes.bfloat16)
    return np.stack([high, low])


def tables(tile, freqs, width):
    win = tile + 2 * width
    grid = 2 * freqs
    k = np.arange(freqs) - freqs // 2
    row = 2.0 * np.pi * ((k[:, None] * (np.arange(tile) + width)[None, :]) % win) / win
    row2 = np.concatenate([np.cos(row), -np.sin(row)], axis=0) / math.sqrt(win)
    col = 2.0 * np.pi * ((k[:, None] * np.arange(win)[None, :]) % win) / win
    col2 = np.concatenate([np.cos(col), -np.sin(col)], axis=0) / math.sqrt(win)
    own = col2[:, width : width + tile]
    edges = np.zeros((2, 2 * freqs, 2 * width))
    edges[0, :, :width] = col2[:, width + tile :]
    edges[1, :, width:] = col2[:, :width]
    at = 2.0 * np.pi * ((k[:, None] * np.arange(grid)[None, :]) % grid) / grid
    c, s = np.cos(at) * math.sqrt(2.0 / freqs), np.sin(at) * math.sqrt(2.0 / freqs)
    field = np.block([[c, s], [-s, c]])
    q = np.arange(1 - freqs, freqs)
    gap = (np.arange(tile) + width)[:, None] / win - np.arange(grid)[None, :] / grid
    fine = np.cos(2.0 * np.pi * gap[:, :, None] * q[None, None, :]).sum(-1) / grid
    return dict(
        row=halves(row2),
        own=halves(own),
        left=halves(edges[0]),
        right=halves(edges[1]),
        f1=halves(field),
        f2=halves(field.T),
        fine=halves(fine),
        finet=halves(fine.T),
        rowt=halves(row2.T),
    )


def split(x):
    high = x.astype(jnp.bfloat16)
    low = (x - high.astype(jnp.float32)).astype(jnp.bfloat16)
    return high, low


def dot(a, b):
    return jnp.dot(a, b, preferred_element_type=jnp.float32)


def dot_t(a, b):
    return lax.dot_general(a, b, (((1,), (1,)), ((), ())), preferred_element_type=jnp.float32)


def times_table(x, table):
    high, low = split(x)
    return dot(
        jnp.concatenate([high, high, low], axis=1),
        jnp.concatenate([table[0], table[1], table[0]], axis=0),
    )


def times_turned(x, table):
    high, low = split(x)
    return dot_t(
        jnp.concatenate([high, high, low], axis=1),
        jnp.concatenate([table[0], table[1], table[0]], axis=1),
    )


def table_times(table, x):
    high, low = split(x)
    return dot(
        jnp.concatenate([table[0], table[1], table[0]], axis=1),
        jnp.concatenate([high, high, low], axis=0),
    )


def narrow(high, low, table_high, table_low, axis, product):
    size = table_high.shape[axis]
    both = product(high, jnp.concatenate([table_high, table_low], axis=axis))
    return both[:, :size] + (both[:, size:] + product(low, table_high))


NAMES = ("row", "left", "right", "own", "f1", "f2", "fine", "finet", "rowt")


def kernel(dims, counts_ref, w_ref, mask_hbm, target_hbm, pup_hbm, *refs):
    ns, nf, nt, local_src, corners, freqs, tile = dims
    many = len(NAMES)
    held = dict(zip(NAMES, refs[:many]))
    out_ref = refs[many]
    mask_ref, target_ref, pup_ref = refs[many + 1 : many + 4]
    tab = dict(zip(NAMES, refs[many + 4 : 2 * many + 4]))
    (load_sem, p_ref, e_ref, zs_send, zs_recv, i_send, i_recv, g_send, g_recv, c_recv, g_half, g_all,
     zs_ss, zs_rs, i_ss, i_rs, g_ss, g_rs, c_ss, c_rs, h_ss, h_rs) = refs[2 * many + 4 :]
    grid = 2 * freqs
    rows = out_ref.shape[0]
    sources = local_src * ns
    t = lax.axis_index("tile")
    src = lax.axis_index("src")
    focus = lax.axis_index("focus")
    has_left = t > 0
    has_right = t < nt - 1
    left, right = jnp.maximum(t - 1, 0), jnp.minimum(t + 1, nt - 1)
    half = freqs // nf
    mine = pl.multiple_of(focus * half, 8)

    def chip(a):
        return lax.rem(src + a, ns)

    def core(b):
        return lax.rem(focus + b, nf)

    def remote(source, dest, ssem, rsem, device):
        return pltpu.make_async_remote_copy(
            src_ref=source, dst_ref=dest, send_sem=ssem, recv_sem=rsem,
            device_id=device, device_id_type=MESH,
        )

    begin = pl.multiple_of((src * nf + focus) * rows, 16)
    loads = {}

    def load(name, source, dest):
        loads[name] = pltpu.make_async_copy(source, dest, load_sem.at[len(loads)])
        loads[name].start()

    load("row", held["row"], tab["row"])
    load("mask", mask_hbm, mask_ref)
    for name in ("left", "right"):
        load(name, held[name], tab[name])

    def need(*names):
        for name in names:
            loads[name].wait()

    zs_recv[...] = jnp.zeros_like(zs_recv)
    c_recv[...] = jnp.zeros_like(c_recv)
    barrier = pltpu.get_barrier_semaphore()

    def greet(device):
        pl.semaphore_signal(barrier, inc=1, device_id=device, device_id_type=MESH)

    for b in range(1, nf):
        greet({"focus": core(b)})
    for a in range(1, ns):
        greet({"src": chip(a)})

    def greet_tile(tile_index):
        for a in range(ns):
            greet({"tile": tile_index, "src": chip(a)})

    pl.when(has_left)(functools.partial(greet_tile, left))
    pl.when(has_right)(functools.partial(greet_tile, right))

    lane = lax.broadcasted_iota(jnp.int32, (freqs, grid), 1)
    first = lane < freqs

    def swap(x):
        return pltpu.roll(x, freqs, 1)

    def complex_of(q):
        top, low = q[:freqs], swap(q[freqs:])
        return jnp.where(first, top - low, top + low)

    need("row", "mask", "left", "right")
    load("own", held["own"], tab["own"])
    load("pupil", pup_hbm, pup_ref)
    for name in ("f1", "f2", "fine"):
        load(name, held[name], tab[name])
    load("target", target_hbm, target_ref)
    load("finet", held["finet"], tab["finet"])
    load("rowt", held["rowt"].at[:, pl.ds(begin, rows), :], tab["rowt"])

    edge = 2 * AMBIT

    def columns(high, low, table):
        wide = jnp.concatenate([table[0], table[1], table[0]], axis=1)
        return complex_of(dot_t(jnp.concatenate([high, high, low], axis=1), wide))

    sides = jnp.concatenate([mask_ref[:, :edge], mask_ref[:, tile - edge :]], axis=1)
    sh, sl = split(table_times(tab["row"], sides))
    zs_send[0] = columns(sh[:, :edge], sl[:, :edge], tab["left"])
    zs_send[1] = columns(sh[:, edge:], sl[:, edge:], tab["right"])
    pl.semaphore_wait(
        barrier,
        (ns + nf - 2) + ns * (has_left.astype(jnp.int32) + has_right.astype(jnp.int32)),
    )
    zs_left = remote(zs_send.at[0], zs_recv.at[1], zs_ss.at[0], zs_rs.at[1], {"tile": left})
    zs_right = remote(zs_send.at[1], zs_recv.at[0], zs_ss.at[1], zs_rs.at[0], {"tile": right})
    pl.when(has_left)(zs_left.start)
    pl.when(has_right)(zs_right.start)
    mh, ml = split(table_times(tab["row"], mask_ref[:, edge : tile - edge]))
    need("own")
    spec = columns(
        jnp.concatenate([sh[:, :edge], mh, sh[:, edge:]], axis=1),
        jnp.concatenate([sl[:, :edge], ml, sl[:, edge:]], axis=1),
        tab["own"],
    )
    need("pupil")
    for corner in range(corners):
        for s in range(local_src):
            p_ref[corner, s] = jnp.concatenate(
                [pup_ref[0, s, corner], pup_ref[1, s, corner]], axis=1
            )
    pl.when(has_left)(zs_right.wait_recv)
    pl.when(has_right)(zs_left.wait_recv)
    spec = spec + zs_recv[0] + zs_recv[1]
    turned = swap(spec)
    same = jnp.where(first, spec, turned)
    cross = jnp.where(first, -turned, spec)

    need("f1", "f2")
    i_copies = []
    for corner in range(corners):
        parts = []
        for s in range(local_src):
            p = p_ref[corner, s]
            parts.append(p * same + swap(p) * cross)
        h = times_table(jnp.concatenate(parts, axis=0), tab["f1"])
        h = jnp.concatenate(
            [
                jnp.concatenate(
                    [h[s * freqs : (s + 1) * freqs, :grid], h[s * freqs : (s + 1) * freqs, grid:]],
                    axis=0,
                )
                for s in range(local_src)
            ],
            axis=1,
        )
        e = table_times(tab["f2"], h)
        e_ref[corner] = e
        total = jnp.zeros((grid, grid), jnp.float32)
        for s in range(local_src):
            e_re = e[:grid, s * grid : (s + 1) * grid]
            e_im = e[grid:, s * grid : (s + 1) * grid]
            total = total + (w_ref[s] * (1.0 / sources)) * (e_re * e_re + e_im * e_im)
        i_send[corner] = total
        for a in range(1, ns):
            copy = remote(
                i_send.at[corner], i_recv.at[a - 1, corner],
                i_ss.at[a - 1, corner], i_rs.at[a - 1, corner], {"src": chip(a)},
            )
            copy.start()
            i_copies.append(copy)

    need("fine", "target", "finet", "rowt")
    count = counts_ref[t]
    sum_x = jnp.zeros((freqs, grid), jnp.float32)
    sum_y = jnp.zeros((freqs, grid), jnp.float32)
    for corner in range(corners):
        total = i_send[corner]
        for a in range(1, ns):
            i_copies[corner * (ns - 1) + a - 1].wait_recv()
            total = total + i_recv[a - 1, corner]
        intensity = times_turned(table_times(tab["fine"], total), tab["fine"])
        wave = jnp.tanh((0.5 * resist_slope) * (intensity - resist_level))
        active = jnp.where(focus * corners + corner < count, 0.25 * resist_slope, 0.0)
        slope = active * ((1.0 - 2.0 * target_ref[...]) + wave) * (1.0 - wave * wave)
        slope = narrow(*split(slope), tab["fine"][0], tab["fine"][1], 1, dot)
        slope = narrow(tab["finet"][0], tab["finet"][1], *split(slope), 1, dot)
        slope = jnp.concatenate([slope, slope], axis=0)
        ge = jnp.concatenate(
            [e_ref[corner, :, s * grid : (s + 1) * grid] * slope for s in range(local_src)], axis=1
        )
        gh = table_times(tab["f1"], ge)
        gh = jnp.concatenate(
            [
                jnp.concatenate(
                    [gh[:freqs, s * grid : (s + 1) * grid], gh[freqs:, s * grid : (s + 1) * grid]],
                    axis=1,
                )
                for s in range(local_src)
            ],
            axis=0,
        )
        gg = narrow(*split(gh), tab["f1"][0], tab["f1"][1], 0, dot_t)
        for s in range(local_src):
            p = p_ref[corner, s]
            part = (w_ref[s] * (2.0 / sources)) * gg[s * freqs : (s + 1) * freqs]
            sum_x = sum_x + p * part
            sum_y = sum_y + swap(p) * part
    gs = jnp.where(first, sum_x + swap(sum_x), sum_y - swap(sum_y))

    def every(copies, step):
        def run():
            for copy in copies:
                getattr(copy, step)()

        return run

    g_send[...] = gs
    g_copies = []
    for b in range(1, nf):
        theirs = pl.multiple_of(core(b) * half, 8)
        g_copies.append(
            remote(
                g_send.at[pl.ds(theirs, half), :], g_recv.at[b - 1],
                g_ss.at[b - 1], g_rs.at[b - 1], {"focus": core(b)},
            )
        )
    every(g_copies, "start")()
    part = g_send[pl.ds(mine, half), :]
    for b, copy in enumerate(g_copies):
        copy.wait_recv()
        part = part + g_recv[b]
    c_recv[0, 0] = part

    def onward(kind, a, device):
        return remote(
            c_recv.at[0, 0], c_recv.at[kind, a], c_ss.at[kind, a], c_rs.at[kind, a],
            {"src": chip(a), **device},
        )

    chips = range(ns - 1, -1, -1)
    c_peers = [onward(0, a, {}) for a in chips if a > 0]
    c_right = [onward(1, a, {"tile": right}) for a in chips]
    c_left = [onward(2, a, {"tile": left}) for a in chips]
    pl.when(has_left)(every(c_left, "start"))
    pl.when(has_right)(every(c_right, "start"))
    every(c_peers, "start")()
    every(c_peers, "wait_recv")()
    pl.when(has_left)(every(c_right, "wait_recv"))
    pl.when(has_right)(every(c_left, "wait_recv"))
    for kind in range(3):
        total = c_recv[kind, 0]
        for a in range(1, ns):
            total = total + c_recv[kind, a]
        g_half[kind] = total
        g_all[kind, pl.ds(mine, half), :] = total

    h_copies = [
        remote(
            g_half, g_all.at[:, pl.ds(mine, half), :],
            h_ss.at[b - 1], h_rs.at[b - 1], {"focus": core(b)},
        )
        for b in range(1, nf)
    ]
    every(h_copies, "start")()

    def stacked(g):
        turned = swap(g)
        return jnp.concatenate([g, jnp.where(first, turned, -turned)], axis=0)

    every(h_copies, "wait_recv")()
    gx = table_times(
        tab["rowt"], jnp.concatenate([stacked(g_all[kind]) for kind in range(3)], axis=1)
    )
    out = times_table(gx[:, :grid], tab["own"])
    gx = gx[:, grid:]
    from_left = times_table(gx[:, :grid], tab["left"])
    from_right = times_table(gx[:, grid:], tab["right"])
    out_ref[:, :edge] = out[:, :edge] + from_left
    out_ref[:, edge : tile - edge] = out[:, edge : tile - edge]
    out_ref[:, tile - edge :] = out[:, tile - edge :] + from_right

    pl.when(has_left)(zs_left.wait_send)
    pl.when(has_right)(zs_right.wait_send)
    pl.when(has_left)(every(c_left, "wait_send"))
    pl.when(has_right)(every(c_right, "wait_send"))
    for copy in i_copies + g_copies + c_peers + h_copies:
        copy.wait_send()


def per_device(mask, target, pupil, weights, counts):
    tile = mask.shape[0]
    freqs = pupil.shape[-1]
    local_src = weights.shape[0]
    corners = pupil.shape[2]
    ns, nf, nt = (lax.axis_size(axis) for axis in ("src", "focus", "tile"))
    grid = 2 * freqs
    rows = tile // (ns * nf)
    half = freqs // nf
    held = tables(tile, freqs, AMBIT)
    held = {name: jnp.asarray(held[name]) for name in NAMES}
    vmem = pl.BlockSpec(memory_space=pltpu.VMEM)
    smem = pl.BlockSpec(memory_space=pltpu.SMEM)
    hbm = pl.BlockSpec(memory_space=pltpu.HBM)
    f32 = jnp.float32
    dma = pltpu.SemaphoreType.DMA
    return pl.pallas_call(
        functools.partial(kernel, (ns, nf, nt, local_src, corners, freqs, tile)),
        out_shape=jax.ShapeDtypeStruct((rows, tile), f32),
        in_specs=[smem, smem] + [hbm] * (3 + len(NAMES)),
        out_specs=vmem,
        scratch_shapes=[
            pltpu.VMEM(mask.shape, f32),
            pltpu.VMEM(target.shape, f32),
            pltpu.VMEM(pupil.shape, f32),
            *[
                pltpu.VMEM((2, rows, grid) if name == "rowt" else held[name].shape, jnp.bfloat16)
                for name in NAMES
            ],
            dma((len(NAMES) + 3,)),
            pltpu.VMEM((corners, local_src, freqs, grid), f32),
            pltpu.VMEM((corners, 2 * grid, local_src * grid), f32),
            pltpu.VMEM((2, freqs, grid), f32),
            pltpu.VMEM((2, freqs, grid), f32),
            pltpu.VMEM((corners, grid, grid), f32),
            pltpu.VMEM((max(ns - 1, 1), corners, grid, grid), f32),
            pltpu.VMEM((freqs, grid), f32),
            pltpu.VMEM((max(nf - 1, 1), half, grid), f32),
            pltpu.VMEM((3, ns, half, grid), f32),
            pltpu.VMEM((3, half, grid), f32),
            pltpu.VMEM((3, freqs, grid), f32),
            dma((2,)),
            dma((2,)),
            dma((max(ns - 1, 1), corners)),
            dma((max(ns - 1, 1), corners)),
            dma((max(nf - 1, 1),)),
            dma((max(nf - 1, 1),)),
            dma((3, ns)),
            dma((3, ns)),
            dma((max(nf - 1, 1),)),
            dma((max(nf - 1, 1),)),
        ],
        compiler_params=pltpu.CompilerParams(
            collective_id=0, has_side_effects=True, vmem_limit_bytes=64 * 1024 * 1024
        ),
        name="abbe_gradient",
    )(counts, weights, mask, target, pupil, *[held[name] for name in NAMES])


def solution(mesh):
    return jax.shard_map(
        per_device,
        mesh=mesh,
        in_specs=(
            P("parts", "tile"),
            P("parts", "tile"),
            P(None, "src", "focus", None, None),
            P("src"),
            P("parts"),
        ),
        out_specs=P(("parts", "src", "focus"), "tile"),
        check_vma=False,
    )
```

```python
import functools
import math

import jax
import jax.numpy as jnp
import ml_dtypes
import numpy as np
from jax import lax
from jax.experimental import pallas as pl
from jax.experimental.pallas import tpu as pltpu
from jax.sharding import PartitionSpec as P

AMBIT = 64
MESH = pl.DeviceIdType.MESH

resist_slope = 4.0
resist_level = 0.5


def halves(table):
    table = table.astype(np.float32)
    high = table.astype(ml_dtypes.bfloat16)
    low = (table - high.astype(np.float32)).astype(ml_dtypes.bfloat16)
    return np.stack([high, low])


def tables(tile, freqs, width):
    win = tile + 2 * width
    grid = 2 * freqs
    k = np.arange(freqs) - freqs // 2
    row = 2.0 * np.pi * ((k[:, None] * (np.arange(tile) + width)[None, :]) % win) / win
    row2 = np.concatenate([np.cos(row), -np.sin(row)], axis=0) / math.sqrt(win)
    col = 2.0 * np.pi * ((k[:, None] * np.arange(win)[None, :]) % win) / win
    col2 = np.concatenate([np.cos(col), -np.sin(col)], axis=0) / math.sqrt(win)
    own = col2[:, width : width + tile]
    edges = np.zeros((2, 2 * freqs, 2 * width))
    edges[0, :, :width] = col2[:, width + tile :]
    edges[1, :, width:] = col2[:, :width]
    at = 2.0 * np.pi * ((k[:, None] * np.arange(grid)[None, :]) % grid) / grid
    c, s = np.cos(at) * math.sqrt(2.0 / freqs), np.sin(at) * math.sqrt(2.0 / freqs)
    field = np.block([[c, s], [-s, c]])
    q = np.arange(1 - freqs, freqs)
    gap = (np.arange(tile) + width)[:, None] / win - np.arange(grid)[None, :] / grid
    fine = np.cos(2.0 * np.pi * gap[:, :, None] * q[None, None, :]).sum(-1) / grid
    return dict(
        row=halves(row2),
        own=halves(own),
        left=halves(edges[0]),
        right=halves(edges[1]),
        f1=halves(field),
        f2=halves(field.T),
        fine=halves(fine),
        finet=halves(fine.T),
        rowt=halves(row2.T),
    )


def split(x):
    high = x.astype(jnp.bfloat16)
    low = (x - high.astype(jnp.float32)).astype(jnp.bfloat16)
    return high, low


def dot(a, b):
    return jnp.dot(a, b, preferred_element_type=jnp.float32)


def dot_t(a, b):
    return lax.dot_general(a, b, (((1,), (1,)), ((), ())), preferred_element_type=jnp.float32)


def times_table(x, table):
    high, low = split(x)
    return dot(
        jnp.concatenate([high, high, low], axis=1),
        jnp.concatenate([table[0], table[1], table[0]], axis=0),
    )


def times_turned(x, table):
    high, low = split(x)
    return dot_t(
        jnp.concatenate([high, high, low], axis=1),
        jnp.concatenate([table[0], table[1], table[0]], axis=1),
    )


def table_times(table, x):
    high, low = split(x)
    return dot(
        jnp.concatenate([table[0], table[1], table[0]], axis=1),
        jnp.concatenate([high, high, low], axis=0),
    )


def narrow(high, low, table_high, table_low, axis, product):
    size = table_high.shape[axis]
    both = product(high, jnp.concatenate([table_high, table_low], axis=axis))
    return both[:, :size] + (both[:, size:] + product(low, table_high))


NAMES = ("row", "left", "right", "own", "f1", "f2", "fine", "finet", "rowt")


def kernel(dims, counts_ref, w_ref, mask_hbm, target_hbm, pup_hbm, *refs):
    ns, nf, nt, local_src, corners, freqs, tile = dims
    many = len(NAMES)
    held = dict(zip(NAMES, refs[:many]))
    out_ref = refs[many]
    mask_ref, target_ref, pup_ref = refs[many + 1 : many + 4]
    tab = dict(zip(NAMES, refs[many + 4 : 2 * many + 4]))
    (load_sem, p_ref, e_ref, zs_send, zs_recv, i_send, i_recv, g_send, g_recv, c_recv, g_half, g_all,
     zs_ss, zs_rs, i_ss, i_rs, g_ss, g_rs, c_ss, c_rs, h_ss, h_rs) = refs[2 * many + 4 :]
    grid = 2 * freqs
    rows = out_ref.shape[0]
    sources = local_src * ns
    t = lax.axis_index("tile")
    src = lax.axis_index("src")
    focus = lax.axis_index("focus")
    has_left = t > 0
    has_right = t < nt - 1
    left, right = jnp.maximum(t - 1, 0), jnp.minimum(t + 1, nt - 1)
    half = freqs // nf
    mine = pl.multiple_of(focus * half, 8)

    def chip(a):
        return lax.rem(src + a, ns)

    def core(b):
        return lax.rem(focus + b, nf)

    def remote(source, dest, ssem, rsem, device):
        return pltpu.make_async_remote_copy(
            src_ref=source, dst_ref=dest, send_sem=ssem, recv_sem=rsem,
            device_id=device, device_id_type=MESH,
        )

    begin = pl.multiple_of((src * nf + focus) * rows, 16)
    loads = {}

    def load(name, source, dest):
        loads[name] = pltpu.make_async_copy(source, dest, load_sem.at[len(loads)])
        loads[name].start()

    load("row", held["row"], tab["row"])
    load("mask", mask_hbm, mask_ref)
    for name in ("left", "right"):
        load(name, held[name], tab[name])

    def need(*names):
        for name in names:
            loads[name].wait()

    zs_recv[...] = jnp.zeros_like(zs_recv)
    c_recv[...] = jnp.zeros_like(c_recv)
    barrier = pltpu.get_barrier_semaphore()

    def greet(device):
        pl.semaphore_signal(barrier, inc=1, device_id=device, device_id_type=MESH)

    for b in range(1, nf):
        greet({"focus": core(b)})
    for a in range(1, ns):
        greet({"src": chip(a)})

    def greet_tile(tile_index):
        for a in range(ns):
            greet({"tile": tile_index, "src": chip(a)})

    pl.when(has_left)(functools.partial(greet_tile, left))
    pl.when(has_right)(functools.partial(greet_tile, right))

    lane = lax.broadcasted_iota(jnp.int32, (freqs, grid), 1)
    first = lane < freqs

    def swap(x):
        return pltpu.roll(x, freqs, 1)

    def complex_of(q):
        top, low = q[:freqs], swap(q[freqs:])
        return jnp.where(first, top - low, top + low)

    need("row", "mask", "left", "right")
    load("own", held["own"], tab["own"])
    load("pupil", pup_hbm, pup_ref)
    for name in ("f1", "f2", "fine"):
        load(name, held[name], tab[name])
    load("target", target_hbm, target_ref)
    load("finet", held["finet"], tab["finet"])
    load("rowt", held["rowt"].at[:, pl.ds(begin, rows), :], tab["rowt"])

    edge = 2 * AMBIT

    def columns(high, low, table):
        wide = jnp.concatenate([table[0], table[1], table[0]], axis=1)
        return complex_of(dot_t(jnp.concatenate([high, high, low], axis=1), wide))

    sides = jnp.concatenate([mask_ref[:, :edge], mask_ref[:, tile - edge :]], axis=1)
    sh, sl = split(table_times(tab["row"], sides))
    zs_send[0] = columns(sh[:, :edge], sl[:, :edge], tab["left"])
    zs_send[1] = columns(sh[:, edge:], sl[:, edge:], tab["right"])
    pl.semaphore_wait(
        barrier,
        (ns + nf - 2) + ns * (has_left.astype(jnp.int32) + has_right.astype(jnp.int32)),
    )
    zs_left = remote(zs_send.at[0], zs_recv.at[1], zs_ss.at[0], zs_rs.at[1], {"tile": left})
    zs_right = remote(zs_send.at[1], zs_recv.at[0], zs_ss.at[1], zs_rs.at[0], {"tile": right})
    pl.when(has_left)(zs_left.start)
    pl.when(has_right)(zs_right.start)
    mh, ml = split(table_times(tab["row"], mask_ref[:, edge : tile - edge]))
    need("own")
    spec = columns(
        jnp.concatenate([sh[:, :edge], mh, sh[:, edge:]], axis=1),
        jnp.concatenate([sl[:, :edge], ml, sl[:, edge:]], axis=1),
        tab["own"],
    )
    need("pupil")
    for corner in range(corners):
        for s in range(local_src):
            p_ref[corner, s] = jnp.concatenate(
                [pup_ref[0, s, corner], pup_ref[1, s, corner]], axis=1
            )
    pl.when(has_left)(zs_right.wait_recv)
    pl.when(has_right)(zs_left.wait_recv)
    spec = spec + zs_recv[0] + zs_recv[1]
    turned = swap(spec)
    same = jnp.where(first, spec, turned)
    cross = jnp.where(first, -turned, spec)

    need("f1", "f2")
    i_copies = []
    for corner in range(corners):
        parts = []
        for s in range(local_src):
            p = p_ref[corner, s]
            parts.append(p * same + swap(p) * cross)
        h = times_table(jnp.concatenate(parts, axis=0), tab["f1"])
        h = jnp.concatenate(
            [
                jnp.concatenate(
                    [h[s * freqs : (s + 1) * freqs, :grid], h[s * freqs : (s + 1) * freqs, grid:]],
                    axis=0,
                )
                for s in range(local_src)
            ],
            axis=1,
        )
        e = table_times(tab["f2"], h)
        e_ref[corner] = e
        total = jnp.zeros((grid, grid), jnp.float32)
        for s in range(local_src):
            e_re = e[:grid, s * grid : (s + 1) * grid]
            e_im = e[grid:, s * grid : (s + 1) * grid]
            total = total + (w_ref[s] * (1.0 / sources)) * (e_re * e_re + e_im * e_im)
        i_send[corner] = total
        for a in range(1, ns):
            copy = remote(
                i_send.at[corner], i_recv.at[a - 1, corner],
                i_ss.at[a - 1, corner], i_rs.at[a - 1, corner], {"src": chip(a)},
            )
            copy.start()
            i_copies.append(copy)

    need("fine", "target", "finet", "rowt")
    count = counts_ref[t]
    sum_x = jnp.zeros((freqs, grid), jnp.float32)
    sum_y = jnp.zeros((freqs, grid), jnp.float32)
    slopes = []
    for corner in range(corners):
        total = i_send[corner]
        for a in range(1, ns):
            i_copies[corner * (ns - 1) + a - 1].wait_recv()
            total = total + i_recv[a - 1, corner]
        intensity = times_turned(table_times(tab["fine"], total), tab["fine"])
        wave = jnp.tanh((0.5 * resist_slope) * (intensity - resist_level))
        active = jnp.where(focus * corners + corner < count, 0.25 * resist_slope, 0.0)
        slope = active * ((1.0 - 2.0 * target_ref[...]) + wave) * (1.0 - wave * wave)
        slope = narrow(*split(slope), tab["fine"][0], tab["fine"][1], 1, dot)
        slope = narrow(tab["finet"][0], tab["finet"][1], *split(slope), 1, dot)
        slopes.append(jnp.concatenate([slope, slope], axis=0))
    for corner, slope in enumerate(slopes):
        ge = jnp.concatenate(
            [e_ref[corner, :, s * grid : (s + 1) * grid] * slope for s in range(local_src)], axis=1
        )
        gh = table_times(tab["f1"], ge)
        gh = jnp.concatenate(
            [
                jnp.concatenate(
                    [gh[:freqs, s * grid : (s + 1) * grid], gh[freqs:, s * grid : (s + 1) * grid]],
                    axis=1,
                )
                for s in range(local_src)
            ],
            axis=0,
        )
        gg = narrow(*split(gh), tab["f1"][0], tab["f1"][1], 0, dot_t)
        for s in range(local_src):
            p = p_ref[corner, s]
            part = (w_ref[s] * (2.0 / sources)) * gg[s * freqs : (s + 1) * freqs]
            sum_x = sum_x + p * part
            sum_y = sum_y + swap(p) * part
    gs = jnp.where(first, sum_x + swap(sum_x), sum_y - swap(sum_y))

    def every(copies, step):
        def run():
            for copy in copies:
                getattr(copy, step)()

        return run

    g_send[...] = gs
    g_copies = []
    for b in range(1, nf):
        theirs = pl.multiple_of(core(b) * half, 8)
        g_copies.append(
            remote(
                g_send.at[pl.ds(theirs, half), :], g_recv.at[b - 1],
                g_ss.at[b - 1], g_rs.at[b - 1], {"focus": core(b)},
            )
        )
    every(g_copies, "start")()
    part = g_send[pl.ds(mine, half), :]
    for b, copy in enumerate(g_copies):
        copy.wait_recv()
        part = part + g_recv[b]
    c_recv[0, 0] = part

    def onward(kind, a, device):
        return remote(
            c_recv.at[0, 0], c_recv.at[kind, a], c_ss.at[kind, a], c_rs.at[kind, a],
            {"src": chip(a), **device},
        )

    chips = range(ns - 1, -1, -1)
    c_peers = [onward(0, a, {}) for a in chips if a > 0]
    c_right = [onward(1, a, {"tile": right}) for a in chips]
    c_left = [onward(2, a, {"tile": left}) for a in chips]
    pl.when(has_left)(every(c_left, "start"))
    pl.when(has_right)(every(c_right, "start"))
    every(c_peers, "start")()
    every(c_peers, "wait_recv")()
    pl.when(has_left)(every(c_right, "wait_recv"))
    pl.when(has_right)(every(c_left, "wait_recv"))
    for kind in range(3):
        total = c_recv[kind, 0]
        for a in range(1, ns):
            total = total + c_recv[kind, a]
        g_half[kind] = total
        g_all[kind, pl.ds(mine, half), :] = total

    h_copies = [
        remote(
            g_half, g_all.at[:, pl.ds(mine, half), :],
            h_ss.at[b - 1], h_rs.at[b - 1], {"focus": core(b)},
        )
        for b in range(1, nf)
    ]
    every(h_copies, "start")()

    def stacked(g):
        turned = swap(g)
        return jnp.concatenate([g, jnp.where(first, turned, -turned)], axis=0)

    every(h_copies, "wait_recv")()
    gx = table_times(
        tab["rowt"], jnp.concatenate([stacked(g_all[kind]) for kind in range(3)], axis=1)
    )
    out = times_table(gx[:, :grid], tab["own"])
    gx = gx[:, grid:]
    from_left = times_table(gx[:, :grid], tab["left"])
    from_right = times_table(gx[:, grid:], tab["right"])
    out_ref[:, :edge] = out[:, :edge] + from_left
    out_ref[:, edge : tile - edge] = out[:, edge : tile - edge]
    out_ref[:, tile - edge :] = out[:, tile - edge :] + from_right

    pl.when(has_left)(zs_left.wait_send)
    pl.when(has_right)(zs_right.wait_send)
    pl.when(has_left)(every(c_left, "wait_send"))
    pl.when(has_right)(every(c_right, "wait_send"))
    for copy in i_copies + g_copies + c_peers + h_copies:
        copy.wait_send()


def per_device(mask, target, pupil, weights, counts):
    tile = mask.shape[0]
    freqs = pupil.shape[-1]
    local_src = weights.shape[0]
    corners = pupil.shape[2]
    ns, nf, nt = (lax.axis_size(axis) for axis in ("src", "focus", "tile"))
    grid = 2 * freqs
    rows = tile // (ns * nf)
    half = freqs // nf
    held = tables(tile, freqs, AMBIT)
    held = {name: jnp.asarray(held[name]) for name in NAMES}
    vmem = pl.BlockSpec(memory_space=pltpu.VMEM)
    smem = pl.BlockSpec(memory_space=pltpu.SMEM)
    hbm = pl.BlockSpec(memory_space=pltpu.HBM)
    f32 = jnp.float32
    dma = pltpu.SemaphoreType.DMA
    return pl.pallas_call(
        functools.partial(kernel, (ns, nf, nt, local_src, corners, freqs, tile)),
        out_shape=jax.ShapeDtypeStruct((rows, tile), f32),
        in_specs=[smem, smem] + [hbm] * (3 + len(NAMES)),
        out_specs=vmem,
        scratch_shapes=[
            pltpu.VMEM(mask.shape, f32),
            pltpu.VMEM(target.shape, f32),
            pltpu.VMEM(pupil.shape, f32),
            *[
                pltpu.VMEM((2, rows, grid) if name == "rowt" else held[name].shape, jnp.bfloat16)
                for name in NAMES
            ],
            dma((len(NAMES) + 3,)),
            pltpu.VMEM((corners, local_src, freqs, grid), f32),
            pltpu.VMEM((corners, 2 * grid, local_src * grid), f32),
            pltpu.VMEM((2, freqs, grid), f32),
            pltpu.VMEM((2, freqs, grid), f32),
            pltpu.VMEM((corners, grid, grid), f32),
            pltpu.VMEM((max(ns - 1, 1), corners, grid, grid), f32),
            pltpu.VMEM((freqs, grid), f32),
            pltpu.VMEM((max(nf - 1, 1), half, grid), f32),
            pltpu.VMEM((3, ns, half, grid), f32),
            pltpu.VMEM((3, half, grid), f32),
            pltpu.VMEM((3, freqs, grid), f32),
            dma((2,)),
            dma((2,)),
            dma((max(ns - 1, 1), corners)),
            dma((max(ns - 1, 1), corners)),
            dma((max(nf - 1, 1),)),
            dma((max(nf - 1, 1),)),
            dma((3, ns)),
            dma((3, ns)),
            dma((max(nf - 1, 1),)),
            dma((max(nf - 1, 1),)),
        ],
        compiler_params=pltpu.CompilerParams(
            collective_id=0, has_side_effects=True, vmem_limit_bytes=64 * 1024 * 1024
        ),
        name="abbe_gradient",
    )(counts, weights, mask, target, pupil, *[held[name] for name in NAMES])


def solution(mesh):
    return jax.shard_map(
        per_device,
        mesh=mesh,
        in_specs=(
            P("parts", "tile"),
            P("parts", "tile"),
            P(None, "src", "focus", None, None),
            P("src"),
            P("parts"),
        ),
        out_specs=P(("parts", "src", "focus"), "tile"),
        check_vma=False,
    )
```

```python
import functools
import math

import jax
import jax.numpy as jnp
import ml_dtypes
import numpy as np
from jax import lax
from jax.experimental import pallas as pl
from jax.experimental.pallas import tpu as pltpu
from jax.sharding import PartitionSpec as P

AMBIT = 64
MESH = pl.DeviceIdType.MESH

resist_slope = 4.0
resist_level = 0.5


def halves(table):
    table = table.astype(np.float32)
    high = table.astype(ml_dtypes.bfloat16)
    low = (table - high.astype(np.float32)).astype(ml_dtypes.bfloat16)
    return np.stack([high, low])


def tables(tile, freqs, width):
    win = tile + 2 * width
    grid = 2 * freqs
    k = np.arange(freqs) - freqs // 2
    even, odd = np.flatnonzero(k % 2 == 0), np.flatnonzero(k % 2)
    order = np.concatenate([even, odd])
    row = 2.0 * np.pi * ((k[order][:, None] * (np.arange(tile) + width)[None, :]) % win) / win
    row2 = np.concatenate([np.cos(row), -np.sin(row)], axis=0) / math.sqrt(win)
    col = 2.0 * np.pi * ((k[:, None] * np.arange(win)[None, :]) % win) / win
    col2 = np.concatenate([np.cos(col), -np.sin(col)], axis=0) / math.sqrt(win)
    own = col2[:, width : width + tile]
    edges = np.zeros((2, 2 * freqs, 2 * width))
    edges[0, :, :width] = col2[:, width + tile :]
    edges[1, :, width:] = col2[:, :width]
    at = 2.0 * np.pi * ((k[:, None] * np.arange(grid)[None, :]) % grid) / grid
    c, s = np.cos(at) * math.sqrt(2.0 / freqs), np.sin(at) * math.sqrt(2.0 / freqs)
    field = np.block([[c, s], [-s, c]])

    def by_parity(chosen):
        points = np.concatenate([np.arange(freqs), grid + np.arange(freqs)])
        high, low = halves(field.T[points][:, np.concatenate([chosen, freqs + chosen])])
        return np.concatenate([high, low, high, low], axis=1)

    q = np.arange(1 - freqs, freqs)
    gap = (np.arange(tile) + width)[:, None] / win - np.arange(grid)[None, :] / grid
    fine = np.cos(2.0 * np.pi * gap[:, :, None] * q[None, None, :]).sum(-1) / grid
    return dict(
        row=halves(row2),
        own=halves(own),
        left=halves(edges[0]),
        right=halves(edges[1]),
        f1=halves(field),
        f2=np.stack([by_parity(even), by_parity(odd)]),
        f3=halves(field[np.concatenate([order, freqs + order])]),
        fine=halves(fine),
        finet=halves(fine.T),
        rowt=halves(row2.T),
    )


def split(x):
    high = x.astype(jnp.bfloat16)
    low = (x - high.astype(jnp.float32)).astype(jnp.bfloat16)
    return high, low


def dot(a, b):
    return jnp.dot(a, b, preferred_element_type=jnp.float32)


def dot_t(a, b):
    return lax.dot_general(a, b, (((1,), (1,)), ((), ())), preferred_element_type=jnp.float32)


def times_table(x, table):
    high, low = split(x)
    return dot(
        jnp.concatenate([high, high, low], axis=1),
        jnp.concatenate([table[0], table[1], table[0]], axis=0),
    )


def times_turned(x, table):
    high, low = split(x)
    return dot_t(
        jnp.concatenate([high, high, low], axis=1),
        jnp.concatenate([table[0], table[1], table[0]], axis=1),
    )


def table_times(table, x):
    high, low = split(x)
    return dot(
        jnp.concatenate([table[0], table[1], table[0]], axis=1),
        jnp.concatenate([high, high, low], axis=0),
    )


def narrow(high, low, table_high, table_low, axis, product):
    size = table_high.shape[axis]
    both = product(high, jnp.concatenate([table_high, table_low], axis=axis))
    return both[:, :size] + (both[:, size:] + product(low, table_high))


NAMES = ("row", "left", "right", "own", "f1", "f2", "f3", "fine", "finet", "rowt")


def kernel(dims, counts_ref, w_ref, mask_hbm, target_hbm, pup_hbm, *refs):
    ns, nf, nt, local_src, corners, freqs, tile = dims
    many = len(NAMES)
    held = dict(zip(NAMES, refs[:many]))
    out_ref = refs[many]
    mask_ref, target_ref, pup_ref = refs[many + 1 : many + 4]
    tab = dict(zip(NAMES, refs[many + 4 : 2 * many + 4]))
    (load_sem, p_ref, e_ref, zs_send, zs_recv, i_send, i_recv, g_send, g_recv, c_recv, g_half, g_all,
     zs_ss, zs_rs, i_ss, i_rs, g_ss, g_rs, c_ss, c_rs, h_ss, h_rs) = refs[2 * many + 4 :]
    grid = 2 * freqs
    rows = out_ref.shape[0]
    sources = local_src * ns
    t = lax.axis_index("tile")
    src = lax.axis_index("src")
    focus = lax.axis_index("focus")
    has_left = t > 0
    has_right = t < nt - 1
    left, right = jnp.maximum(t - 1, 0), jnp.minimum(t + 1, nt - 1)
    half = freqs // nf
    mine = pl.multiple_of(focus * half, 8)

    def chip(a):
        return lax.rem(src + a, ns)

    def core(b):
        return lax.rem(focus + b, nf)

    def remote(source, dest, ssem, rsem, device):
        return pltpu.make_async_remote_copy(
            src_ref=source, dst_ref=dest, send_sem=ssem, recv_sem=rsem,
            device_id=device, device_id_type=MESH,
        )

    begin = pl.multiple_of((src * nf + focus) * rows, 16)
    loads = {}

    def load(name, source, dest):
        loads[name] = pltpu.make_async_copy(source, dest, load_sem.at[len(loads)])
        loads[name].start()

    load("row", held["row"], tab["row"])
    load("mask", mask_hbm, mask_ref)
    for name in ("left", "right"):
        load(name, held[name], tab[name])

    def need(*names):
        for name in names:
            loads[name].wait()

    zs_recv[...] = jnp.zeros_like(zs_recv)
    c_recv[...] = jnp.zeros_like(c_recv)
    barrier = pltpu.get_barrier_semaphore()

    def greet(device):
        pl.semaphore_signal(barrier, inc=1, device_id=device, device_id_type=MESH)

    for b in range(1, nf):
        greet({"focus": core(b)})
    for a in range(1, ns):
        greet({"src": chip(a)})

    def greet_tile(tile_index):
        for a in range(ns):
            greet({"tile": tile_index, "src": chip(a)})

    pl.when(has_left)(functools.partial(greet_tile, left))
    pl.when(has_right)(functools.partial(greet_tile, right))

    lane = lax.broadcasted_iota(jnp.int32, (freqs, grid), 1)
    first = lane < freqs

    def swap(x):
        return pltpu.roll(x, freqs, 1)

    def complex_of(q):
        top, low = q[:freqs], swap(q[freqs:])
        return jnp.where(first, top - low, top + low)

    need("row", "mask", "left", "right")
    load("own", held["own"], tab["own"])
    load("pupil", pup_hbm, pup_ref)
    for name in ("f1", "f2", "f3", "fine"):
        load(name, held[name], tab[name])
    load("target", target_hbm, target_ref)
    load("finet", held["finet"], tab["finet"])
    load("rowt", held["rowt"].at[:, pl.ds(begin, rows), :], tab["rowt"])

    edge = 2 * AMBIT

    def columns(high, low, table):
        wide = jnp.concatenate([table[0], table[1], table[0]], axis=1)
        return complex_of(dot_t(jnp.concatenate([high, high, low], axis=1), wide))

    sides = jnp.concatenate([mask_ref[:, :edge], mask_ref[:, tile - edge :]], axis=1)
    sh, sl = split(table_times(tab["row"], sides))
    zs_send[0] = columns(sh[:, :edge], sl[:, :edge], tab["left"])
    zs_send[1] = columns(sh[:, edge:], sl[:, edge:], tab["right"])
    pl.semaphore_wait(
        barrier,
        (ns + nf - 2) + ns * (has_left.astype(jnp.int32) + has_right.astype(jnp.int32)),
    )
    zs_left = remote(zs_send.at[0], zs_recv.at[1], zs_ss.at[0], zs_rs.at[1], {"tile": left})
    zs_right = remote(zs_send.at[1], zs_recv.at[0], zs_ss.at[1], zs_rs.at[0], {"tile": right})
    pl.when(has_left)(zs_left.start)
    pl.when(has_right)(zs_right.start)
    mh, ml = split(table_times(tab["row"], mask_ref[:, edge : tile - edge]))
    few = freqs // 2
    need("own")
    spec = columns(
        jnp.concatenate([sh[:, :edge], mh, sh[:, edge:]], axis=1),
        jnp.concatenate([sl[:, :edge], ml, sl[:, edge:]], axis=1),
        tab["own"],
    )
    need("pupil")
    for corner in range(corners):
        for s in range(local_src):
            p_ref[corner, s] = jnp.concatenate(
                [
                    jnp.concatenate(
                        [pup_ref[n, s, corner, pl.ds(m, few, stride=2), :] for m in range(2)],
                        axis=0,
                    )
                    for n in range(2)
                ],
                axis=1,
            )
    pl.when(has_left)(zs_right.wait_recv)
    pl.when(has_right)(zs_left.wait_recv)
    spec = spec + zs_recv[0] + zs_recv[1]
    turned = swap(spec)
    same = jnp.where(first, spec, turned)
    cross = jnp.where(first, -turned, spec)

    need("f1", "f2")
    i_copies = []
    for corner in range(corners):
        parts = []
        for s in range(local_src):
            p = p_ref[corner, s]
            parts.append(p * same + swap(p) * cross)
        h = times_table(jnp.concatenate(parts, axis=0), tab["f1"])
        h_high, h_low = split(h)

        def parity(n):
            def pieces(x):
                return jnp.concatenate(
                    [
                        jnp.concatenate(
                            [
                                x[s * freqs + n * few : s * freqs + (n + 1) * few, :grid],
                                x[s * freqs + n * few : s * freqs + (n + 1) * few, grid:],
                            ],
                            axis=0,
                        )
                        for s in range(local_src)
                    ],
                    axis=1,
                )

            high, low = pieces(h_high), pieces(h_low)
            return dot(tab["f2"][n], jnp.concatenate([high, high, low, low], axis=0))

        h_even, h_odd = parity(0), parity(1)
        plus, minus = h_even + h_odd, h_even - h_odd
        e = jnp.concatenate(
            [plus[:freqs], minus[:freqs], plus[freqs:], minus[freqs:]], axis=0
        )
        e_ref[corner] = e
        total = jnp.zeros((grid, grid), jnp.float32)
        for s in range(local_src):
            e_re = e[:grid, s * grid : (s + 1) * grid]
            e_im = e[grid:, s * grid : (s + 1) * grid]
            total = total + (w_ref[s] * (1.0 / sources)) * (e_re * e_re + e_im * e_im)
        i_send[corner] = total
        for a in range(1, ns):
            copy = remote(
                i_send.at[corner], i_recv.at[a - 1, corner],
                i_ss.at[a - 1, corner], i_rs.at[a - 1, corner], {"src": chip(a)},
            )
            copy.start()
            i_copies.append(copy)

    need("f3", "fine", "target", "finet", "rowt")
    count = counts_ref[t]
    sum_x = jnp.zeros((freqs, grid), jnp.float32)
    sum_y = jnp.zeros((freqs, grid), jnp.float32)
    slopes = []
    for corner in range(corners):
        total = i_send[corner]
        for a in range(1, ns):
            i_copies[corner * (ns - 1) + a - 1].wait_recv()
            total = total + i_recv[a - 1, corner]
        intensity = times_turned(table_times(tab["fine"], total), tab["fine"])
        wave = jnp.tanh((0.5 * resist_slope) * (intensity - resist_level))
        active = jnp.where(focus * corners + corner < count, 0.25 * resist_slope, 0.0)
        slope = active * ((1.0 - 2.0 * target_ref[...]) + wave) * (1.0 - wave * wave)
        slope = narrow(*split(slope), tab["fine"][0], tab["fine"][1], 1, dot)
        slope = narrow(tab["finet"][0], tab["finet"][1], *split(slope), 1, dot)
        slopes.append(jnp.concatenate([slope, slope], axis=0))
    for corner, slope in enumerate(slopes):
        ge = jnp.concatenate(
            [e_ref[corner, :, s * grid : (s + 1) * grid] * slope for s in range(local_src)], axis=1
        )
        gh = table_times(tab["f3"], ge)
        gh = jnp.concatenate(
            [
                jnp.concatenate(
                    [gh[:freqs, s * grid : (s + 1) * grid], gh[freqs:, s * grid : (s + 1) * grid]],
                    axis=1,
                )
                for s in range(local_src)
            ],
            axis=0,
        )
        gg = narrow(*split(gh), tab["f1"][0], tab["f1"][1], 0, dot_t)
        for s in range(local_src):
            p = p_ref[corner, s]
            part = (w_ref[s] * (2.0 / sources)) * gg[s * freqs : (s + 1) * freqs]
            sum_x = sum_x + p * part
            sum_y = sum_y + swap(p) * part
    gs = jnp.where(first, sum_x + swap(sum_x), sum_y - swap(sum_y))

    def every(copies, step):
        def run():
            for copy in copies:
                getattr(copy, step)()

        return run

    g_send[...] = gs
    g_copies = []
    for b in range(1, nf):
        theirs = pl.multiple_of(core(b) * half, 8)
        g_copies.append(
            remote(
                g_send.at[pl.ds(theirs, half), :], g_recv.at[b - 1],
                g_ss.at[b - 1], g_rs.at[b - 1], {"focus": core(b)},
            )
        )
    every(g_copies, "start")()
    part = g_send[pl.ds(mine, half), :]
    for b, copy in enumerate(g_copies):
        copy.wait_recv()
        part = part + g_recv[b]
    c_recv[0, 0] = part

    def onward(kind, a, device):
        return remote(
            c_recv.at[0, 0], c_recv.at[kind, a], c_ss.at[kind, a], c_rs.at[kind, a],
            {"src": chip(a), **device},
        )

    chips = range(ns - 1, -1, -1)
    c_peers = [onward(0, a, {}) for a in chips if a > 0]
    c_right = [onward(1, a, {"tile": right}) for a in chips]
    c_left = [onward(2, a, {"tile": left}) for a in chips]
    pl.when(has_left)(every(c_left, "start"))
    pl.when(has_right)(every(c_right, "start"))
    every(c_peers, "start")()
    every(c_peers, "wait_recv")()
    pl.when(has_left)(every(c_right, "wait_recv"))
    pl.when(has_right)(every(c_left, "wait_recv"))
    for kind in range(3):
        total = c_recv[kind, 0]
        for a in range(1, ns):
            total = total + c_recv[kind, a]
        g_half[kind] = total
        g_all[kind, pl.ds(mine, half), :] = total

    h_copies = [
        remote(
            g_half, g_all.at[:, pl.ds(mine, half), :],
            h_ss.at[b - 1], h_rs.at[b - 1], {"focus": core(b)},
        )
        for b in range(1, nf)
    ]
    every(h_copies, "start")()

    def stacked(g):
        turned = swap(g)
        return jnp.concatenate([g, jnp.where(first, turned, -turned)], axis=0)

    every(h_copies, "wait_recv")()
    gx = table_times(
        tab["rowt"], jnp.concatenate([stacked(g_all[kind]) for kind in range(3)], axis=1)
    )
    out = times_table(gx[:, :grid], tab["own"])
    gx = gx[:, grid:]
    from_left = times_table(gx[:, :grid], tab["left"])
    from_right = times_table(gx[:, grid:], tab["right"])
    out_ref[:, :edge] = out[:, :edge] + from_left
    out_ref[:, edge : tile - edge] = out[:, edge : tile - edge]
    out_ref[:, tile - edge :] = out[:, tile - edge :] + from_right

    pl.when(has_left)(zs_left.wait_send)
    pl.when(has_right)(zs_right.wait_send)
    pl.when(has_left)(every(c_left, "wait_send"))
    pl.when(has_right)(every(c_right, "wait_send"))
    for copy in i_copies + g_copies + c_peers + h_copies:
        copy.wait_send()


def per_device(mask, target, pupil, weights, counts):
    tile = mask.shape[0]
    freqs = pupil.shape[-1]
    local_src = weights.shape[0]
    corners = pupil.shape[2]
    ns, nf, nt = (lax.axis_size(axis) for axis in ("src", "focus", "tile"))
    grid = 2 * freqs
    rows = tile // (ns * nf)
    half = freqs // nf
    held = tables(tile, freqs, AMBIT)
    held = {name: jnp.asarray(held[name]) for name in NAMES}
    vmem = pl.BlockSpec(memory_space=pltpu.VMEM)
    smem = pl.BlockSpec(memory_space=pltpu.SMEM)
    hbm = pl.BlockSpec(memory_space=pltpu.HBM)
    f32 = jnp.float32
    dma = pltpu.SemaphoreType.DMA
    return pl.pallas_call(
        functools.partial(kernel, (ns, nf, nt, local_src, corners, freqs, tile)),
        out_shape=jax.ShapeDtypeStruct((rows, tile), f32),
        in_specs=[smem, smem] + [hbm] * (3 + len(NAMES)),
        out_specs=vmem,
        scratch_shapes=[
            pltpu.VMEM(mask.shape, f32),
            pltpu.VMEM(target.shape, f32),
            pltpu.VMEM(pupil.shape, f32),
            *[
                pltpu.VMEM((2, rows, grid) if name == "rowt" else held[name].shape, jnp.bfloat16)
                for name in NAMES
            ],
            dma((len(NAMES) + 3,)),
            pltpu.VMEM((corners, local_src, freqs, grid), f32),
            pltpu.VMEM((corners, 2 * grid, local_src * grid), f32),
            pltpu.VMEM((2, freqs, grid), f32),
            pltpu.VMEM((2, freqs, grid), f32),
            pltpu.VMEM((corners, grid, grid), f32),
            pltpu.VMEM((max(ns - 1, 1), corners, grid, grid), f32),
            pltpu.VMEM((freqs, grid), f32),
            pltpu.VMEM((max(nf - 1, 1), half, grid), f32),
            pltpu.VMEM((3, ns, half, grid), f32),
            pltpu.VMEM((3, half, grid), f32),
            pltpu.VMEM((3, freqs, grid), f32),
            dma((2,)),
            dma((2,)),
            dma((max(ns - 1, 1), corners)),
            dma((max(ns - 1, 1), corners)),
            dma((max(nf - 1, 1),)),
            dma((max(nf - 1, 1),)),
            dma((3, ns)),
            dma((3, ns)),
            dma((max(nf - 1, 1),)),
            dma((max(nf - 1, 1),)),
        ],
        compiler_params=pltpu.CompilerParams(
            collective_id=0, has_side_effects=True, vmem_limit_bytes=64 * 1024 * 1024
        ),
        name="abbe_gradient",
    )(counts, weights, mask, target, pupil, *[held[name] for name in NAMES])


def solution(mesh):
    return jax.shard_map(
        per_device,
        mesh=mesh,
        in_specs=(
            P("parts", "tile"),
            P("parts", "tile"),
            P(None, "src", "focus", None, None),
            P("src"),
            P("parts"),
        ),
        out_specs=P(("parts", "src", "focus"), "tile"),
        check_vma=False,
    )
```

```python
import functools
import math

import jax
import jax.numpy as jnp
import ml_dtypes
import numpy as np
from jax import lax
from jax.experimental import pallas as pl
from jax.experimental.pallas import tpu as pltpu
from jax.sharding import PartitionSpec as P

AMBIT = 64
MESH = pl.DeviceIdType.MESH

resist_slope = 4.0
resist_level = 0.5


def halves(table):
    table = table.astype(np.float32)
    high = table.astype(ml_dtypes.bfloat16)
    low = (table - high.astype(np.float32)).astype(ml_dtypes.bfloat16)
    return np.stack([high, low])


def tables(tile, freqs, width):
    win = tile + 2 * width
    grid = 2 * freqs
    k = np.arange(freqs) - freqs // 2
    even, odd = np.flatnonzero(k % 2 == 0), np.flatnonzero(k % 2)
    order = np.concatenate([even, odd])
    row = 2.0 * np.pi * ((k[order][:, None] * (np.arange(tile) + width)[None, :]) % win) / win
    row2 = np.concatenate([np.cos(row), -np.sin(row)], axis=0) / math.sqrt(win)
    col = 2.0 * np.pi * ((k[:, None] * np.arange(win)[None, :]) % win) / win
    col2 = np.concatenate([np.cos(col), -np.sin(col)], axis=0) / math.sqrt(win)
    own = col2[:, width : width + tile]
    edges = np.zeros((2, 2 * freqs, 2 * width))
    edges[0, :, :width] = col2[:, width + tile :]
    edges[1, :, width:] = col2[:, :width]
    at = 2.0 * np.pi * ((k[:, None] * np.arange(grid)[None, :]) % grid) / grid
    c, s = np.cos(at) * math.sqrt(2.0 / freqs), np.sin(at) * math.sqrt(2.0 / freqs)
    field = np.block([[c, s], [-s, c]])

    def by_parity(chosen):
        points = np.concatenate([np.arange(freqs), grid + np.arange(freqs)])
        high, low = halves(field.T[points][:, np.concatenate([chosen, freqs + chosen])])
        return np.concatenate([high, low, high, low], axis=1)

    q = np.arange(1 - freqs, freqs)
    gap = (np.arange(tile) + width)[:, None] / win - np.arange(grid)[None, :] / grid
    fine = np.cos(2.0 * np.pi * gap[:, :, None] * q[None, None, :]).sum(-1) / grid
    return dict(
        row=halves(row2),
        own=halves(own),
        left=halves(edges[0]),
        right=halves(edges[1]),
        f1=halves(field),
        f2=np.stack([by_parity(even), by_parity(odd)]),
        f3=halves(field[np.concatenate([order, freqs + order])]),
        fine=halves(fine),
        finet=halves(fine.T),
        rowt=halves(row2.T),
    )


def split(x):
    high = x.astype(jnp.bfloat16)
    low = (x - high.astype(jnp.float32)).astype(jnp.bfloat16)
    return high, low


def dot(a, b):
    return jnp.dot(a, b, preferred_element_type=jnp.float32)


def dot_t(a, b):
    return lax.dot_general(a, b, (((1,), (1,)), ((), ())), preferred_element_type=jnp.float32)


def times_table(x, table):
    high, low = split(x)
    return dot(
        jnp.concatenate([high, high, low], axis=1),
        jnp.concatenate([table[0], table[1], table[0]], axis=0),
    )


def times_turned(x, table):
    high, low = split(x)
    return dot_t(
        jnp.concatenate([high, high, low], axis=1),
        jnp.concatenate([table[0], table[1], table[0]], axis=1),
    )


def table_times(table, x):
    high, low = split(x)
    return dot(
        jnp.concatenate([table[0], table[1], table[0]], axis=1),
        jnp.concatenate([high, high, low], axis=0),
    )


def narrow(high, low, table_high, table_low, axis, product):
    size = table_high.shape[axis]
    both = product(high, jnp.concatenate([table_high, table_low], axis=axis))
    return both[:, :size] + (both[:, size:] + product(low, table_high))


NAMES = ("row", "left", "right", "own", "f1", "f2", "f3", "fine", "finet", "rowt")


def kernel(dims, counts_ref, w_ref, mask_hbm, target_hbm, pup_hbm, *refs):
    ns, nf, nt, local_src, corners, freqs, tile = dims
    many = len(NAMES)
    held = dict(zip(NAMES, refs[:many]))
    out_ref = refs[many]
    mask_ref, target_ref, pup_ref = refs[many + 1 : many + 4]
    tab = dict(zip(NAMES, refs[many + 4 : 2 * many + 4]))
    (load_sem, p_ref, e_ref, zs_send, zs_recv, i_send, i_recv, g_send, g_recv, c_recv, g_half, g_all,
     zs_ss, zs_rs, i_ss, i_rs, g_ss, g_rs, c_ss, c_rs, h_ss, h_rs) = refs[2 * many + 4 :]
    grid = 2 * freqs
    rows = out_ref.shape[0]
    sources = local_src * ns
    t = lax.axis_index("tile")
    src = lax.axis_index("src")
    focus = lax.axis_index("focus")
    has_left = t > 0
    has_right = t < nt - 1
    left, right = jnp.maximum(t - 1, 0), jnp.minimum(t + 1, nt - 1)
    half = freqs // nf
    mine = pl.multiple_of(focus * half, 8)

    def chip(a):
        return lax.rem(src + a, ns)

    def core(b):
        return lax.rem(focus + b, nf)

    def remote(source, dest, ssem, rsem, device):
        return pltpu.make_async_remote_copy(
            src_ref=source, dst_ref=dest, send_sem=ssem, recv_sem=rsem,
            device_id=device, device_id_type=MESH,
        )

    begin = pl.multiple_of((src * nf + focus) * rows, 16)
    loads = {}

    def load(name, source, dest):
        loads[name] = pltpu.make_async_copy(source, dest, load_sem.at[len(loads)])
        loads[name].start()

    load("row", held["row"], tab["row"])
    load("mask", mask_hbm, mask_ref)
    for name in ("left", "right"):
        load(name, held[name], tab[name])

    def need(*names):
        for name in names:
            loads[name].wait()

    zs_recv[...] = jnp.zeros_like(zs_recv)
    c_recv[...] = jnp.zeros_like(c_recv)
    barrier = pltpu.get_barrier_semaphore()

    def greet(device):
        pl.semaphore_signal(barrier, inc=1, device_id=device, device_id_type=MESH)

    for b in range(1, nf):
        greet({"focus": core(b)})
    for a in range(1, ns):
        greet({"src": chip(a)})

    def greet_tile(tile_index):
        for a in range(ns):
            greet({"tile": tile_index, "src": chip(a)})

    pl.when(has_left)(functools.partial(greet_tile, left))
    pl.when(has_right)(functools.partial(greet_tile, right))

    lane = lax.broadcasted_iota(jnp.int32, (freqs, grid), 1)
    first = lane < freqs

    def swap(x):
        return pltpu.roll(x, freqs, 1)

    def complex_of(q):
        top, low = q[:freqs], swap(q[freqs:])
        return jnp.where(first, top - low, top + low)

    need("row", "mask", "left", "right")
    load("own", held["own"], tab["own"])
    load("pupil", pup_hbm, pup_ref)
    for name in ("f1", "f2", "f3", "fine"):
        load(name, held[name], tab[name])
    load("target", target_hbm, target_ref)
    load("finet", held["finet"], tab["finet"])
    load("rowt", held["rowt"].at[:, pl.ds(begin, rows), :], tab["rowt"])

    edge = 2 * AMBIT

    def columns(high, low, table):
        wide = jnp.concatenate([table[0], table[1], table[0]], axis=1)
        return complex_of(dot_t(jnp.concatenate([high, high, low], axis=1), wide))

    sides = jnp.concatenate([mask_ref[:, :edge], mask_ref[:, tile - edge :]], axis=1)
    sh, sl = split(table_times(tab["row"], sides))
    zs_send[0] = columns(sh[:, :edge], sl[:, :edge], tab["left"])
    zs_send[1] = columns(sh[:, edge:], sl[:, edge:], tab["right"])
    pl.semaphore_wait(
        barrier,
        (ns + nf - 2) + ns * (has_left.astype(jnp.int32) + has_right.astype(jnp.int32)),
    )
    zs_left = remote(zs_send.at[0], zs_recv.at[1], zs_ss.at[0], zs_rs.at[1], {"tile": left})
    zs_right = remote(zs_send.at[1], zs_recv.at[0], zs_ss.at[1], zs_rs.at[0], {"tile": right})
    pl.when(has_left)(zs_left.start)
    pl.when(has_right)(zs_right.start)
    mh, ml = split(table_times(tab["row"], mask_ref[:, edge : tile - edge]))
    few = freqs // 2
    need("own")
    spec = columns(
        jnp.concatenate([sh[:, :edge], mh, sh[:, edge:]], axis=1),
        jnp.concatenate([sl[:, :edge], ml, sl[:, edge:]], axis=1),
        tab["own"],
    )
    need("pupil")
    for corner in range(corners):
        for s in range(local_src):
            p_ref[corner, s] = jnp.concatenate(
                [
                    jnp.concatenate(
                        [pup_ref[n, s, corner, pl.ds(m, few, stride=2), :] for m in range(2)],
                        axis=0,
                    )
                    for n in range(2)
                ],
                axis=1,
            )
    pl.when(has_left)(zs_right.wait_recv)
    pl.when(has_right)(zs_left.wait_recv)
    spec = spec + zs_recv[0] + zs_recv[1]
    turned = swap(spec)
    same = jnp.where(first, spec, turned)
    cross = jnp.where(first, -turned, spec)

    need("f1", "f2")
    i_copies = []
    for corner in range(corners):
        parts = []
        for s in range(local_src):
            p = p_ref[corner, s]
            parts.append(p * same + swap(p) * cross)
        h = times_table(jnp.concatenate(parts, axis=0), tab["f1"])
        h_high, h_low = split(h)

        def parity(n):
            def pieces(x):
                return jnp.concatenate(
                    [
                        jnp.concatenate(
                            [
                                x[s * freqs + n * few : s * freqs + (n + 1) * few, :grid],
                                x[s * freqs + n * few : s * freqs + (n + 1) * few, grid:],
                            ],
                            axis=0,
                        )
                        for s in range(local_src)
                    ],
                    axis=1,
                )

            high, low = pieces(h_high), pieces(h_low)
            return dot(tab["f2"][n], jnp.concatenate([high, high, low, low], axis=0))

        h_even, h_odd = parity(0), parity(1)
        plus, minus = h_even + h_odd, h_even - h_odd
        e = jnp.concatenate(
            [plus[:freqs], minus[:freqs], plus[freqs:], minus[freqs:]], axis=0
        )
        e_ref[corner] = e
        total = jnp.zeros((grid, grid), jnp.float32)
        for s in range(local_src):
            e_re = e[:grid, s * grid : (s + 1) * grid]
            e_im = e[grid:, s * grid : (s + 1) * grid]
            total = total + (w_ref[s] * (1.0 / sources)) * (e_re * e_re + e_im * e_im)
        i_send[corner] = total
        for a in range(1, ns):
            copy = remote(
                i_send.at[corner], i_recv.at[a - 1, corner],
                i_ss.at[a - 1, corner], i_rs.at[a - 1, corner], {"src": chip(a)},
            )
            copy.start()
            i_copies.append(copy)

    need("f3", "fine", "target", "finet", "rowt")
    count = counts_ref[t]
    sum_x = jnp.zeros((freqs, grid), jnp.float32)
    sum_y = jnp.zeros((freqs, grid), jnp.float32)
    slopes = []
    for corner in range(corners):
        total = i_send[corner]
        for a in range(1, ns):
            i_copies[corner * (ns - 1) + a - 1].wait_recv()
            total = total + i_recv[a - 1, corner]
        intensity = table_times(tab["fine"], times_turned(total, tab["fine"]))
        wave = jnp.tanh((0.5 * resist_slope) * (intensity - resist_level))
        active = jnp.where(focus * corners + corner < count, 0.25 * resist_slope, 0.0)
        slope = active * ((1.0 - 2.0 * target_ref[...]) + wave) * (1.0 - wave * wave)
        slope = table_times(tab["finet"], slope)
        slope = narrow(*split(slope), tab["fine"][0], tab["fine"][1], 1, dot)
        slopes.append(jnp.concatenate([slope, slope], axis=0))
    for corner, slope in enumerate(slopes):
        ge = jnp.concatenate(
            [e_ref[corner, :, s * grid : (s + 1) * grid] * slope for s in range(local_src)], axis=1
        )
        gh = table_times(tab["f3"], ge)
        gh = jnp.concatenate(
            [
                jnp.concatenate(
                    [gh[:freqs, s * grid : (s + 1) * grid], gh[freqs:, s * grid : (s + 1) * grid]],
                    axis=1,
                )
                for s in range(local_src)
            ],
            axis=0,
        )
        gg = narrow(*split(gh), tab["f1"][0], tab["f1"][1], 0, dot_t)
        for s in range(local_src):
            p = p_ref[corner, s]
            part = (w_ref[s] * (2.0 / sources)) * gg[s * freqs : (s + 1) * freqs]
            sum_x = sum_x + p * part
            sum_y = sum_y + swap(p) * part
    gs = jnp.where(first, sum_x + swap(sum_x), sum_y - swap(sum_y))

    def every(copies, step):
        def run():
            for copy in copies:
                getattr(copy, step)()

        return run

    g_send[...] = gs
    g_copies = []
    for b in range(1, nf):
        theirs = pl.multiple_of(core(b) * half, 8)
        g_copies.append(
            remote(
                g_send.at[pl.ds(theirs, half), :], g_recv.at[b - 1],
                g_ss.at[b - 1], g_rs.at[b - 1], {"focus": core(b)},
            )
        )
    every(g_copies, "start")()
    part = g_send[pl.ds(mine, half), :]
    for b, copy in enumerate(g_copies):
        copy.wait_recv()
        part = part + g_recv[b]
    c_recv[0, 0] = part

    def onward(kind, a, device):
        return remote(
            c_recv.at[0, 0], c_recv.at[kind, a], c_ss.at[kind, a], c_rs.at[kind, a],
            {"src": chip(a), **device},
        )

    chips = range(ns - 1, -1, -1)
    c_peers = [onward(0, a, {}) for a in chips if a > 0]
    c_right = [onward(1, a, {"tile": right}) for a in chips]
    c_left = [onward(2, a, {"tile": left}) for a in chips]
    pl.when(has_left)(every(c_left, "start"))
    pl.when(has_right)(every(c_right, "start"))
    every(c_peers, "start")()
    every(c_peers, "wait_recv")()
    pl.when(has_left)(every(c_right, "wait_recv"))
    pl.when(has_right)(every(c_left, "wait_recv"))
    for kind in range(3):
        total = c_recv[kind, 0]
        for a in range(1, ns):
            total = total + c_recv[kind, a]
        g_half[kind] = total
        g_all[kind, pl.ds(mine, half), :] = total

    h_copies = [
        remote(
            g_half, g_all.at[:, pl.ds(mine, half), :],
            h_ss.at[b - 1], h_rs.at[b - 1], {"focus": core(b)},
        )
        for b in range(1, nf)
    ]
    every(h_copies, "start")()

    def stacked(g):
        turned = swap(g)
        return jnp.concatenate([g, jnp.where(first, turned, -turned)], axis=0)

    every(h_copies, "wait_recv")()
    gx = table_times(
        tab["rowt"], jnp.concatenate([stacked(g_all[kind]) for kind in range(3)], axis=1)
    )
    out = times_table(gx[:, :grid], tab["own"])
    gx = gx[:, grid:]
    from_left = times_table(gx[:, :grid], tab["left"])
    from_right = times_table(gx[:, grid:], tab["right"])
    out_ref[:, :edge] = out[:, :edge] + from_left
    out_ref[:, edge : tile - edge] = out[:, edge : tile - edge]
    out_ref[:, tile - edge :] = out[:, tile - edge :] + from_right

    pl.when(has_left)(zs_left.wait_send)
    pl.when(has_right)(zs_right.wait_send)
    pl.when(has_left)(every(c_left, "wait_send"))
    pl.when(has_right)(every(c_right, "wait_send"))
    for copy in i_copies + g_copies + c_peers + h_copies:
        copy.wait_send()


def per_device(mask, target, pupil, weights, counts):
    tile = mask.shape[0]
    freqs = pupil.shape[-1]
    local_src = weights.shape[0]
    corners = pupil.shape[2]
    ns, nf, nt = (lax.axis_size(axis) for axis in ("src", "focus", "tile"))
    grid = 2 * freqs
    rows = tile // (ns * nf)
    half = freqs // nf
    held = tables(tile, freqs, AMBIT)
    held = {name: jnp.asarray(held[name]) for name in NAMES}
    vmem = pl.BlockSpec(memory_space=pltpu.VMEM)
    smem = pl.BlockSpec(memory_space=pltpu.SMEM)
    hbm = pl.BlockSpec(memory_space=pltpu.HBM)
    f32 = jnp.float32
    dma = pltpu.SemaphoreType.DMA
    return pl.pallas_call(
        functools.partial(kernel, (ns, nf, nt, local_src, corners, freqs, tile)),
        out_shape=jax.ShapeDtypeStruct((rows, tile), f32),
        in_specs=[smem, smem] + [hbm] * (3 + len(NAMES)),
        out_specs=vmem,
        scratch_shapes=[
            pltpu.VMEM(mask.shape, f32),
            pltpu.VMEM(target.shape, f32),
            pltpu.VMEM(pupil.shape, f32),
            *[
                pltpu.VMEM((2, rows, grid) if name == "rowt" else held[name].shape, jnp.bfloat16)
                for name in NAMES
            ],
            dma((len(NAMES) + 3,)),
            pltpu.VMEM((corners, local_src, freqs, grid), f32),
            pltpu.VMEM((corners, 2 * grid, local_src * grid), f32),
            pltpu.VMEM((2, freqs, grid), f32),
            pltpu.VMEM((2, freqs, grid), f32),
            pltpu.VMEM((corners, grid, grid), f32),
            pltpu.VMEM((max(ns - 1, 1), corners, grid, grid), f32),
            pltpu.VMEM((freqs, grid), f32),
            pltpu.VMEM((max(nf - 1, 1), half, grid), f32),
            pltpu.VMEM((3, ns, half, grid), f32),
            pltpu.VMEM((3, half, grid), f32),
            pltpu.VMEM((3, freqs, grid), f32),
            dma((2,)),
            dma((2,)),
            dma((max(ns - 1, 1), corners)),
            dma((max(ns - 1, 1), corners)),
            dma((max(nf - 1, 1),)),
            dma((max(nf - 1, 1),)),
            dma((3, ns)),
            dma((3, ns)),
            dma((max(nf - 1, 1),)),
            dma((max(nf - 1, 1),)),
        ],
        compiler_params=pltpu.CompilerParams(
            collective_id=0, has_side_effects=True, vmem_limit_bytes=64 * 1024 * 1024
        ),
        name="abbe_gradient",
    )(counts, weights, mask, target, pupil, *[held[name] for name in NAMES])


def solution(mesh):
    return jax.shard_map(
        per_device,
        mesh=mesh,
        in_specs=(
            P("parts", "tile"),
            P("parts", "tile"),
            P(None, "src", "focus", None, None),
            P("src"),
            P("parts"),
        ),
        out_specs=P(("parts", "src", "focus"), "tile"),
        check_vma=False,
    )
```

```python
import functools
import math

import jax
import jax.numpy as jnp
import ml_dtypes
import numpy as np
from jax import lax
from jax.experimental import pallas as pl
from jax.experimental.pallas import tpu as pltpu
from jax.sharding import PartitionSpec as P

AMBIT = 64
MESH = pl.DeviceIdType.MESH

resist_slope = 4.0
resist_level = 0.5


def halves(table):
    table = table.astype(np.float32)
    high = table.astype(ml_dtypes.bfloat16)
    low = (table - high.astype(np.float32)).astype(ml_dtypes.bfloat16)
    return np.stack([high, low])


def tables(tile, freqs, width):
    win = tile + 2 * width
    grid = 2 * freqs
    k = np.arange(freqs) - freqs // 2
    even, odd = np.flatnonzero(k % 2 == 0), np.flatnonzero(k % 2)
    order = np.concatenate([even, odd])
    row = 2.0 * np.pi * ((k[order][:, None] * (np.arange(tile) + width)[None, :]) % win) / win
    row2 = np.concatenate([np.cos(row), -np.sin(row)], axis=0) / math.sqrt(win)
    col = 2.0 * np.pi * ((k[:, None] * np.arange(win)[None, :]) % win) / win
    col2 = np.concatenate([np.cos(col), -np.sin(col)], axis=0) / math.sqrt(win)
    own = col2[:, width : width + tile]
    edges = np.zeros((2, 2 * freqs, 2 * width))
    edges[0, :, :width] = col2[:, width + tile :]
    edges[1, :, width:] = col2[:, :width]
    at = 2.0 * np.pi * ((k[:, None] * np.arange(grid)[None, :]) % grid) / grid
    c, s = np.cos(at) * math.sqrt(2.0 / freqs), np.sin(at) * math.sqrt(2.0 / freqs)
    field = np.block([[c, s], [-s, c]])

    def by_parity(chosen):
        points = np.concatenate([np.arange(freqs), grid + np.arange(freqs)])
        high, low = halves(field.T[points][:, np.concatenate([chosen, freqs + chosen])])
        return np.concatenate([high, low, high, low], axis=1)

    q = np.arange(1 - freqs, freqs)
    gap = (np.arange(tile) + width)[:, None] / win - np.arange(grid)[None, :] / grid
    fine = np.cos(2.0 * np.pi * gap[:, :, None] * q[None, None, :]).sum(-1) / grid
    return dict(
        row=halves(row2),
        own=halves(own),
        left=halves(edges[0]),
        right=halves(edges[1]),
        f1=halves(field),
        f2=np.stack([by_parity(even), by_parity(odd)]),
        f3=halves(field[np.concatenate([order, freqs + order])]),
        fine=halves(fine),
        finet=halves(fine.T),
        rowt=halves(row2.T),
    )


def split(x):
    high = x.astype(jnp.bfloat16)
    low = (x - high.astype(jnp.float32)).astype(jnp.bfloat16)
    return high, low


def dot(a, b):
    return jnp.dot(a, b, preferred_element_type=jnp.float32)


def dot_t(a, b):
    return lax.dot_general(a, b, (((1,), (1,)), ((), ())), preferred_element_type=jnp.float32)


def times_table(x, table):
    high, low = split(x)
    return dot(
        jnp.concatenate([high, high, low], axis=1),
        jnp.concatenate([table[0], table[1], table[0]], axis=0),
    )


def times_turned(x, table):
    high, low = split(x)
    return dot_t(
        jnp.concatenate([high, high, low], axis=1),
        jnp.concatenate([table[0], table[1], table[0]], axis=1),
    )


def table_times(table, x):
    high, low = split(x)
    return dot(
        jnp.concatenate([table[0], table[1], table[0]], axis=1),
        jnp.concatenate([high, high, low], axis=0),
    )


def narrow(high, low, table_high, table_low, axis, product):
    size = table_high.shape[axis]
    both = product(high, jnp.concatenate([table_high, table_low], axis=axis))
    return both[:, :size] + (both[:, size:] + product(low, table_high))


NAMES = ("row", "left", "right", "own", "f1", "f2", "f3", "fine", "finet", "rowt")


def kernel(dims, counts_ref, w_ref, mask_hbm, target_hbm, pup_hbm, *refs):
    ns, nf, nt, local_src, corners, freqs, tile = dims
    many = len(NAMES)
    held = dict(zip(NAMES, refs[:many]))
    out_ref = refs[many]
    mask_ref, target_ref, pup_ref = refs[many + 1 : many + 4]
    tab = dict(zip(NAMES, refs[many + 4 : 2 * many + 4]))
    (load_sem, p_ref, e_ref, zs_send, zs_recv, i_send, i_recv, g_send, g_recv, c_recv, g_half, g_all,
     zs_ss, zs_rs, i_ss, i_rs, g_ss, g_rs, c_ss, c_rs, h_ss, h_rs) = refs[2 * many + 4 :]
    grid = 2 * freqs
    rows = out_ref.shape[0]
    sources = local_src * ns
    t = lax.axis_index("tile")
    src = lax.axis_index("src")
    focus = lax.axis_index("focus")
    has_left = t > 0
    has_right = t < nt - 1
    left, right = jnp.maximum(t - 1, 0), jnp.minimum(t + 1, nt - 1)
    half = freqs // nf
    mine = pl.multiple_of(focus * half, 8)

    def chip(a):
        return lax.rem(src + a, ns)

    def core(b):
        return lax.rem(focus + b, nf)

    def remote(source, dest, ssem, rsem, device):
        return pltpu.make_async_remote_copy(
            src_ref=source, dst_ref=dest, send_sem=ssem, recv_sem=rsem,
            device_id=device, device_id_type=MESH,
        )

    begin = pl.multiple_of((src * nf + focus) * rows, 16)
    loads = {}

    def load(name, source, dest):
        loads[name] = pltpu.make_async_copy(source, dest, load_sem.at[len(loads)])
        loads[name].start()

    load("row", held["row"], tab["row"])
    load("mask", mask_hbm, mask_ref)
    for name in ("left", "right"):
        load(name, held[name], tab[name])

    def need(*names):
        for name in names:
            loads[name].wait()

    zs_recv[...] = jnp.zeros_like(zs_recv)
    c_recv[...] = jnp.zeros_like(c_recv)
    barrier = pltpu.get_barrier_semaphore()

    def greet(device):
        pl.semaphore_signal(barrier, inc=1, device_id=device, device_id_type=MESH)

    for b in range(1, nf):
        greet({"focus": core(b)})
    for a in range(1, ns):
        greet({"src": chip(a)})

    def greet_tile(tile_index):
        for a in range(ns):
            greet({"tile": tile_index, "src": chip(a)})

    pl.when(has_left)(functools.partial(greet_tile, left))
    pl.when(has_right)(functools.partial(greet_tile, right))

    lane = lax.broadcasted_iota(jnp.int32, (freqs, grid), 1)
    first = lane < freqs

    def swap(x):
        return pltpu.roll(x, freqs, 1)

    def complex_of(q):
        top, low = q[:freqs], swap(q[freqs:])
        return jnp.where(first, top - low, top + low)

    need("row", "mask", "left", "right")
    load("own", held["own"], tab["own"])
    load("pupil", pup_hbm, pup_ref)
    for name in ("f1", "f2", "f3", "fine"):
        load(name, held[name], tab[name])
    load("target", target_hbm, target_ref)
    load("finet", held["finet"], tab["finet"])
    load("rowt", held["rowt"].at[:, pl.ds(begin, rows), :], tab["rowt"])

    edge = 2 * AMBIT

    def columns(high, low, table):
        wide = jnp.concatenate([table[0], table[1], table[0]], axis=1)
        return complex_of(dot_t(jnp.concatenate([high, high, low], axis=1), wide))

    sides = jnp.concatenate([mask_ref[:, :edge], mask_ref[:, tile - edge :]], axis=1)
    sh, sl = split(table_times(tab["row"], sides))
    zs_send[0] = columns(sh[:, :edge], sl[:, :edge], tab["left"])
    zs_send[1] = columns(sh[:, edge:], sl[:, edge:], tab["right"])
    pl.semaphore_wait(
        barrier,
        (ns + nf - 2) + ns * (has_left.astype(jnp.int32) + has_right.astype(jnp.int32)),
    )
    zs_left = remote(zs_send.at[0], zs_recv.at[1], zs_ss.at[0], zs_rs.at[1], {"tile": left})
    zs_right = remote(zs_send.at[1], zs_recv.at[0], zs_ss.at[1], zs_rs.at[0], {"tile": right})
    pl.when(has_left)(zs_left.start)
    pl.when(has_right)(zs_right.start)
    mh, ml = split(table_times(tab["row"], mask_ref[:, edge : tile - edge]))
    few = freqs // 2
    need("own")
    spec = columns(
        jnp.concatenate([sh[:, :edge], mh, sh[:, edge:]], axis=1),
        jnp.concatenate([sl[:, :edge], ml, sl[:, edge:]], axis=1),
        tab["own"],
    )
    need("pupil")
    for corner in range(corners):
        for s in range(local_src):
            p_ref[corner, s] = jnp.concatenate(
                [
                    jnp.concatenate(
                        [pup_ref[n, s, corner, pl.ds(m, few, stride=2), :] for m in range(2)],
                        axis=0,
                    )
                    for n in range(2)
                ],
                axis=1,
            )
    pl.when(has_left)(zs_right.wait_recv)
    pl.when(has_right)(zs_left.wait_recv)
    spec = spec + zs_recv[0] + zs_recv[1]
    turned = swap(spec)
    same = jnp.where(first, spec, turned)
    cross = jnp.where(first, -turned, spec)

    need("f1", "f2")
    i_copies = []
    for corner in range(corners):
        parts = []
        for s in range(local_src):
            p = p_ref[corner, s]
            parts.append(p * same + swap(p) * cross)
        h = times_table(jnp.concatenate(parts, axis=0), tab["f1"])
        h_high, h_low = split(h)

        def parity(n):
            def pieces(x):
                return jnp.concatenate(
                    [
                        jnp.concatenate(
                            [
                                x[s * freqs + n * few : s * freqs + (n + 1) * few, :grid],
                                x[s * freqs + n * few : s * freqs + (n + 1) * few, grid:],
                            ],
                            axis=0,
                        )
                        for s in range(local_src)
                    ],
                    axis=1,
                )

            high, low = pieces(h_high), pieces(h_low)
            return dot(tab["f2"][n], jnp.concatenate([high, high, low, low], axis=0))

        h_even, h_odd = parity(0), parity(1)
        plus, minus = h_even + h_odd, h_even - h_odd
        e = jnp.concatenate(
            [plus[:freqs], minus[:freqs], plus[freqs:], minus[freqs:]], axis=0
        )
        e_ref[corner] = e
        total = jnp.zeros((grid, grid), jnp.float32)
        for s in range(local_src):
            e_re = e[:grid, s * grid : (s + 1) * grid]
            e_im = e[grid:, s * grid : (s + 1) * grid]
            total = total + (w_ref[s] * (1.0 / sources)) * (e_re * e_re + e_im * e_im)
        i_send[corner] = total
        for a in range(1, ns):
            copy = remote(
                i_send.at[corner], i_recv.at[a - 1, corner],
                i_ss.at[a - 1, corner], i_rs.at[a - 1, corner], {"src": chip(a)},
            )
            copy.start()
            i_copies.append(copy)

    need("f3", "fine", "target", "finet", "rowt")
    count = counts_ref[t]
    sum_x = jnp.zeros((freqs, grid), jnp.float32)
    sum_y = jnp.zeros((freqs, grid), jnp.float32)
    slopes = []
    for corner in range(corners):
        total = i_send[corner]
        for a in range(1, ns):
            i_copies[corner * (ns - 1) + a - 1].wait_recv()
            total = total + i_recv[a - 1, corner]
        intensity = times_turned(table_times(tab["fine"], total), tab["fine"])
        wave = jnp.tanh((0.5 * resist_slope) * (intensity - resist_level))
        active = jnp.where(focus * corners + corner < count, 0.25 * resist_slope, 0.0)
        slope = active * ((1.0 - 2.0 * target_ref[...]) + wave) * (1.0 - wave * wave)
        slope = narrow(*split(slope), tab["fine"][0], tab["fine"][1], 1, dot)
        slope = narrow(tab["finet"][0], tab["finet"][1], *split(slope), 1, dot)
        slopes.append(jnp.concatenate([slope, slope], axis=0))
    for corner, slope in enumerate(slopes):
        ge = jnp.concatenate(
            [e_ref[corner, :, s * grid : (s + 1) * grid] * slope for s in range(local_src)], axis=1
        )
        gh = table_times(tab["f3"], ge)
        gh = jnp.concatenate(
            [
                jnp.concatenate(
                    [gh[:freqs, s * grid : (s + 1) * grid], gh[freqs:, s * grid : (s + 1) * grid]],
                    axis=1,
                )
                for s in range(local_src)
            ],
            axis=0,
        )
        gg = narrow(*split(gh), tab["f1"][0], tab["f1"][1], 0, dot_t)
        for s in range(local_src):
            p = p_ref[corner, s]
            part = (w_ref[s] * (2.0 / sources)) * gg[s * freqs : (s + 1) * freqs]
            sum_x = sum_x + p * part
            sum_y = sum_y + swap(p) * part
    gs = jnp.where(first, sum_x + swap(sum_x), sum_y - swap(sum_y))

    def every(copies, step):
        def run():
            for copy in copies:
                getattr(copy, step)()

        return run

    g_send[...] = gs
    g_copies = []
    for b in range(1, nf):
        theirs = pl.multiple_of(core(b) * half, 8)
        g_copies.append(
            remote(
                g_send.at[pl.ds(theirs, half), :], g_recv.at[b - 1],
                g_ss.at[b - 1], g_rs.at[b - 1], {"focus": core(b)},
            )
        )
    every(g_copies, "start")()
    part = g_send[pl.ds(mine, half), :]
    for b, copy in enumerate(g_copies):
        copy.wait_recv()
        part = part + g_recv[b]
    c_recv[0, 0] = part

    def onward(kind, a, device):
        return remote(
            c_recv.at[0, 0], c_recv.at[kind, a], c_ss.at[kind, a], c_rs.at[kind, a],
            {"src": chip(a), **device},
        )

    chips = range(ns - 1, -1, -1)
    c_peers = [onward(0, a, {}) for a in chips if a > 0]
    c_right = [onward(1, a, {"tile": right}) for a in chips]
    c_left = [onward(2, a, {"tile": left}) for a in chips]
    pl.when(has_left)(every(c_left, "start"))
    pl.when(has_right)(every(c_right, "start"))
    every(c_peers, "start")()
    every(c_peers, "wait_recv")()
    pl.when(has_left)(every(c_right, "wait_recv"))
    pl.when(has_right)(every(c_left, "wait_recv"))
    for kind in range(3):
        total = c_recv[kind, 0]
        for a in range(1, ns):
            total = total + c_recv[kind, a]
        g_half[kind] = total
        g_all[kind, pl.ds(mine, half), :] = total

    h_copies = [
        remote(
            g_half, g_all.at[:, pl.ds(mine, half), :],
            h_ss.at[b - 1], h_rs.at[b - 1], {"focus": core(b)},
        )
        for b in range(1, nf)
    ]
    every(h_copies, "start")()

    def stacked(g):
        turned = swap(g)
        return jnp.concatenate([g, jnp.where(first, turned, -turned)], axis=0)

    every(h_copies, "wait_recv")()
    gx = table_times(
        tab["rowt"], jnp.concatenate([stacked(g_all[kind]) for kind in range(3)], axis=1)
    )
    out = times_table(gx[:, :grid], tab["own"])
    gx = gx[:, grid:]
    from_left = times_table(gx[:, :grid], tab["left"])
    from_right = times_table(gx[:, grid:], tab["right"])
    out_ref[:, :edge] = out[:, :edge] + from_left
    out_ref[:, edge : tile - edge] = out[:, edge : tile - edge]
    out_ref[:, tile - edge :] = out[:, tile - edge :] + from_right

    pl.when(has_left)(zs_left.wait_send)
    pl.when(has_right)(zs_right.wait_send)
    pl.when(has_left)(every(c_left, "wait_send"))
    pl.when(has_right)(every(c_right, "wait_send"))
    for copy in i_copies + g_copies + c_peers + h_copies:
        copy.wait_send()


def handed_on(step, source, dest, sems):
    copies = []
    for n, begin in enumerate(range(0, source.shape[0], step)):
        rows = pl.ds(begin, step)
        copies.append(pltpu.make_async_copy(source.at[rows, :], dest.at[rows, :], sems.at[n]))
    for copy in copies:
        copy.start()
    for copy in copies:
        copy.wait()


def per_device(mask, target, pupil, weights, counts):
    tile = mask.shape[0]
    freqs = pupil.shape[-1]
    local_src = weights.shape[0]
    corners = pupil.shape[2]
    ns, nf, nt = (lax.axis_size(axis) for axis in ("src", "focus", "tile"))
    grid = 2 * freqs
    rows = tile // (ns * nf)
    half = freqs // nf
    held = tables(tile, freqs, AMBIT)
    held = {name: jnp.asarray(held[name]) for name in NAMES}
    vmem = pl.BlockSpec(memory_space=pltpu.VMEM)
    smem = pl.BlockSpec(memory_space=pltpu.SMEM)
    hbm = pl.BlockSpec(memory_space=pltpu.HBM)
    f32 = jnp.float32
    dma = pltpu.SemaphoreType.DMA
    result = pl.pallas_call(
        functools.partial(kernel, (ns, nf, nt, local_src, corners, freqs, tile)),
        out_shape=jax.ShapeDtypeStruct((rows, tile), f32),
        in_specs=[smem, smem] + [hbm] * (3 + len(NAMES)),
        out_specs=vmem,
        scratch_shapes=[
            pltpu.VMEM(mask.shape, f32),
            pltpu.VMEM(target.shape, f32),
            pltpu.VMEM(pupil.shape, f32),
            *[
                pltpu.VMEM((2, rows, grid) if name == "rowt" else held[name].shape, jnp.bfloat16)
                for name in NAMES
            ],
            dma((len(NAMES) + 3,)),
            pltpu.VMEM((corners, local_src, freqs, grid), f32),
            pltpu.VMEM((corners, 2 * grid, local_src * grid), f32),
            pltpu.VMEM((2, freqs, grid), f32),
            pltpu.VMEM((2, freqs, grid), f32),
            pltpu.VMEM((corners, grid, grid), f32),
            pltpu.VMEM((max(ns - 1, 1), corners, grid, grid), f32),
            pltpu.VMEM((freqs, grid), f32),
            pltpu.VMEM((max(nf - 1, 1), half, grid), f32),
            pltpu.VMEM((3, ns, half, grid), f32),
            pltpu.VMEM((3, half, grid), f32),
            pltpu.VMEM((3, freqs, grid), f32),
            dma((2,)),
            dma((2,)),
            dma((max(ns - 1, 1), corners)),
            dma((max(ns - 1, 1), corners)),
            dma((max(nf - 1, 1),)),
            dma((max(nf - 1, 1),)),
            dma((3, ns)),
            dma((3, ns)),
            dma((max(nf - 1, 1),)),
            dma((max(nf - 1, 1),)),
        ],
        compiler_params=pltpu.CompilerParams(
            collective_id=0, has_side_effects=True, vmem_limit_bytes=64 * 1024 * 1024
        ),
        name="abbe_gradient",
    )(counts, weights, mask, target, pupil, *[held[name] for name in NAMES])
    step = 8 * max(1, rows // 32)
    return pl.pallas_call(
        functools.partial(handed_on, step),
        out_shape=jax.ShapeDtypeStruct((rows, tile), f32),
        in_specs=[hbm],
        out_specs=hbm,
        scratch_shapes=[dma((rows // step,))],
        compiler_params=pltpu.CompilerParams(vmem_limit_bytes=64 * 1024 * 1024),
        name="hand_on",
    )(result)


def solution(mesh):
    return jax.shard_map(
        per_device,
        mesh=mesh,
        in_specs=(
            P("parts", "tile"),
            P("parts", "tile"),
            P(None, "src", "focus", None, None),
            P("src"),
            P("parts"),
        ),
        out_specs=P(("parts", "src", "focus"), "tile"),
        check_vma=False,
    )
```

```python
import functools
import math

import jax
import jax.numpy as jnp
import ml_dtypes
import numpy as np
from jax import lax
from jax.experimental import pallas as pl
from jax.experimental.pallas import tpu as pltpu
from jax.sharding import PartitionSpec as P

AMBIT = 64
MESH = pl.DeviceIdType.MESH

resist_slope = 4.0
resist_level = 0.5


def halves(table):
    table = table.astype(np.float32)
    high = table.astype(ml_dtypes.bfloat16)
    low = (table - high.astype(np.float32)).astype(ml_dtypes.bfloat16)
    return np.stack([high, low])


def tables(tile, freqs, width):
    win = tile + 2 * width
    grid = 2 * freqs
    k = np.arange(freqs) - freqs // 2
    even, odd = np.flatnonzero(k % 2 == 0), np.flatnonzero(k % 2)
    order = np.concatenate([even, odd])
    row = 2.0 * np.pi * ((k[order][:, None] * (np.arange(tile) + width)[None, :]) % win) / win
    row2 = np.concatenate([np.cos(row), -np.sin(row)], axis=0) / math.sqrt(win)
    col = 2.0 * np.pi * ((k[:, None] * np.arange(win)[None, :]) % win) / win
    col2 = np.concatenate([np.cos(col), -np.sin(col)], axis=0) / math.sqrt(win)
    own = col2[:, width : width + tile]
    edges = np.zeros((2, 2 * freqs, 2 * width))
    edges[0, :, :width] = col2[:, width + tile :]
    edges[1, :, width:] = col2[:, :width]
    at = 2.0 * np.pi * ((k[:, None] * np.arange(grid)[None, :]) % grid) / grid
    c, s = np.cos(at) * math.sqrt(2.0 / freqs), np.sin(at) * math.sqrt(2.0 / freqs)
    field = np.block([[c, s], [-s, c]])

    def by_parity(chosen):
        points = np.concatenate([np.arange(freqs), grid + np.arange(freqs)])
        high, low = halves(field.T[points][:, np.concatenate([chosen, freqs + chosen])])
        return np.concatenate([high, low, high, low], axis=1)

    q = np.arange(1 - freqs, freqs)
    gap = (np.arange(tile) + width)[:, None] / win - np.arange(grid)[None, :] / grid
    fine = np.cos(2.0 * np.pi * gap[:, :, None] * q[None, None, :]).sum(-1) / grid
    return dict(
        row=halves(row2),
        own=halves(own),
        left=halves(edges[0]),
        right=halves(edges[1]),
        f1=halves(field),
        f2=np.stack([by_parity(even), by_parity(odd)]),
        f3=halves(field[np.concatenate([order, freqs + order])]),
        fine=halves(fine),
        finet=halves(fine.T),
        rowt=halves(row2.T),
    )


def split(x):
    high = x.astype(jnp.bfloat16)
    low = (x - high.astype(jnp.float32)).astype(jnp.bfloat16)
    return high, low


def dot(a, b):
    return jnp.dot(a, b, preferred_element_type=jnp.float32)


def dot_t(a, b):
    return lax.dot_general(a, b, (((1,), (1,)), ((), ())), preferred_element_type=jnp.float32)


def times_table(x, table):
    high, low = split(x)
    return dot(
        jnp.concatenate([high, high, low], axis=1),
        jnp.concatenate([table[0], table[1], table[0]], axis=0),
    )


def times_turned(x, table):
    high, low = split(x)
    return dot_t(
        jnp.concatenate([high, high, low], axis=1),
        jnp.concatenate([table[0], table[1], table[0]], axis=1),
    )


def table_times(table, x):
    high, low = split(x)
    return dot(
        jnp.concatenate([table[0], table[1], table[0]], axis=1),
        jnp.concatenate([high, high, low], axis=0),
    )


def narrow(high, low, table_high, table_low, axis, product):
    size = table_high.shape[axis]
    both = product(high, jnp.concatenate([table_high, table_low], axis=axis))
    return both[:, :size] + (both[:, size:] + product(low, table_high))


NAMES = ("row", "left", "right", "own", "f1", "f2", "f3", "fine", "finet", "rowt")


def kernel(dims, counts_ref, w_ref, mask_hbm, target_hbm, pup_hbm, *refs):
    ns, nf, nt, local_src, corners, freqs, tile = dims
    many = len(NAMES)
    held = dict(zip(NAMES, refs[:many]))
    out_ref = refs[many]
    mask_ref, target_ref, pup_ref = refs[many + 1 : many + 4]
    tab = dict(zip(NAMES, refs[many + 4 : 2 * many + 4]))
    (load_sem, p_ref, e_ref, zs_send, zs_recv, i_send, i_recv, g_send, g_recv, c_recv, g_half, g_all,
     zs_ss, zs_rs, i_ss, i_rs, g_ss, g_rs, c_ss, c_rs, h_ss, h_rs) = refs[2 * many + 4 :]
    grid = 2 * freqs
    rows = out_ref.shape[0]
    sources = local_src * ns
    t = lax.axis_index("tile")
    src = lax.axis_index("src")
    focus = lax.axis_index("focus")
    has_left = t > 0
    has_right = t < nt - 1
    left, right = jnp.maximum(t - 1, 0), jnp.minimum(t + 1, nt - 1)
    half = freqs // nf
    mine = pl.multiple_of(focus * half, 8)

    def chip(a):
        return lax.rem(src + a, ns)

    def core(b):
        return lax.rem(focus + b, nf)

    def remote(source, dest, ssem, rsem, device):
        return pltpu.make_async_remote_copy(
            src_ref=source, dst_ref=dest, send_sem=ssem, recv_sem=rsem,
            device_id=device, device_id_type=MESH,
        )

    begin = pl.multiple_of((src * nf + focus) * rows, 16)
    loads = {}

    def load(name, source, dest):
        loads[name] = pltpu.make_async_copy(source, dest, load_sem.at[len(loads)])
        loads[name].start()

    load("row", held["row"], tab["row"])
    edge = 2 * AMBIT
    for name, at, size in (
        ("first", 0, edge), ("last", tile - edge, edge), ("middle", edge, tile - 2 * edge)
    ):
        if name == "middle":
            for side in ("left", "right"):
                load(side, held[side], tab[side])
        place = pl.ds(at, size)
        load(name, mask_hbm.at[:, place], mask_ref.at[:, place])

    def need(*names):
        for name in names:
            loads[name].wait()

    zs_recv[...] = jnp.zeros_like(zs_recv)
    c_recv[...] = jnp.zeros_like(c_recv)
    barrier = pltpu.get_barrier_semaphore()

    def greet(device):
        pl.semaphore_signal(barrier, inc=1, device_id=device, device_id_type=MESH)

    for b in range(1, nf):
        greet({"focus": core(b)})
    for a in range(1, ns):
        greet({"src": chip(a)})

    def greet_tile(tile_index):
        for a in range(ns):
            greet({"tile": tile_index, "src": chip(a)})

    pl.when(has_left)(functools.partial(greet_tile, left))
    pl.when(has_right)(functools.partial(greet_tile, right))

    lane = lax.broadcasted_iota(jnp.int32, (freqs, grid), 1)
    first = lane < freqs

    def swap(x):
        return pltpu.roll(x, freqs, 1)

    def complex_of(q):
        top, low = q[:freqs], swap(q[freqs:])
        return jnp.where(first, top - low, top + low)

    need("row", "first", "last")
    load("own", held["own"], tab["own"])
    load("pupil", pup_hbm, pup_ref)
    for name in ("f1", "f2", "f3", "fine"):
        load(name, held[name], tab[name])
    load("target", target_hbm, target_ref)
    load("finet", held["finet"], tab["finet"])
    load("rowt", held["rowt"].at[:, pl.ds(begin, rows), :], tab["rowt"])

    def columns(high, low, table):
        wide = jnp.concatenate([table[0], table[1], table[0]], axis=1)
        return complex_of(dot_t(jnp.concatenate([high, high, low], axis=1), wide))

    sides = jnp.concatenate([mask_ref[:, :edge], mask_ref[:, tile - edge :]], axis=1)
    sh, sl = split(table_times(tab["row"], sides))
    need("left", "right")
    zs_send[0] = columns(sh[:, :edge], sl[:, :edge], tab["left"])
    zs_send[1] = columns(sh[:, edge:], sl[:, edge:], tab["right"])
    pl.semaphore_wait(
        barrier,
        (ns + nf - 2) + ns * (has_left.astype(jnp.int32) + has_right.astype(jnp.int32)),
    )
    zs_left = remote(zs_send.at[0], zs_recv.at[1], zs_ss.at[0], zs_rs.at[1], {"tile": left})
    zs_right = remote(zs_send.at[1], zs_recv.at[0], zs_ss.at[1], zs_rs.at[0], {"tile": right})
    pl.when(has_left)(zs_left.start)
    pl.when(has_right)(zs_right.start)
    need("middle")
    mh, ml = split(table_times(tab["row"], mask_ref[:, edge : tile - edge]))
    few = freqs // 2
    need("own")
    spec = columns(
        jnp.concatenate([sh[:, :edge], mh, sh[:, edge:]], axis=1),
        jnp.concatenate([sl[:, :edge], ml, sl[:, edge:]], axis=1),
        tab["own"],
    )
    need("pupil")
    for corner in range(corners):
        for s in range(local_src):
            p_ref[corner, s] = jnp.concatenate(
                [
                    jnp.concatenate(
                        [pup_ref[n, s, corner, pl.ds(m, few, stride=2), :] for m in range(2)],
                        axis=0,
                    )
                    for n in range(2)
                ],
                axis=1,
            )
    pl.when(has_left)(zs_right.wait_recv)
    pl.when(has_right)(zs_left.wait_recv)
    spec = spec + zs_recv[0] + zs_recv[1]
    turned = swap(spec)
    same = jnp.where(first, spec, turned)
    cross = jnp.where(first, -turned, spec)

    need("f1", "f2")
    i_copies = []
    for corner in range(corners):
        parts = []
        for s in range(local_src):
            p = p_ref[corner, s]
            parts.append(p * same + swap(p) * cross)
        h = times_table(jnp.concatenate(parts, axis=0), tab["f1"])
        h_high, h_low = split(h)

        def parity(n):
            def pieces(x):
                return jnp.concatenate(
                    [
                        jnp.concatenate(
                            [
                                x[s * freqs + n * few : s * freqs + (n + 1) * few, :grid],
                                x[s * freqs + n * few : s * freqs + (n + 1) * few, grid:],
                            ],
                            axis=0,
                        )
                        for s in range(local_src)
                    ],
                    axis=1,
                )

            high, low = pieces(h_high), pieces(h_low)
            return dot(tab["f2"][n], jnp.concatenate([high, high, low, low], axis=0))

        h_even, h_odd = parity(0), parity(1)
        plus, minus = h_even + h_odd, h_even - h_odd
        e = jnp.concatenate(
            [plus[:freqs], minus[:freqs], plus[freqs:], minus[freqs:]], axis=0
        )
        e_ref[corner] = e
        total = jnp.zeros((grid, grid), jnp.float32)
        for s in range(local_src):
            e_re = e[:grid, s * grid : (s + 1) * grid]
            e_im = e[grid:, s * grid : (s + 1) * grid]
            total = total + (w_ref[s] * (1.0 / sources)) * (e_re * e_re + e_im * e_im)
        i_send[corner] = total
        for a in range(1, ns):
            copy = remote(
                i_send.at[corner], i_recv.at[a - 1, corner],
                i_ss.at[a - 1, corner], i_rs.at[a - 1, corner], {"src": chip(a)},
            )
            copy.start()
            i_copies.append(copy)

    need("f3", "fine", "target", "finet", "rowt")
    count = counts_ref[t]
    sum_x = jnp.zeros((freqs, grid), jnp.float32)
    sum_y = jnp.zeros((freqs, grid), jnp.float32)
    slopes = []
    for corner in range(corners):
        total = i_send[corner]
        for a in range(1, ns):
            i_copies[corner * (ns - 1) + a - 1].wait_recv()
            total = total + i_recv[a - 1, corner]
        intensity = times_turned(table_times(tab["fine"], total), tab["fine"])
        wave = jnp.tanh((0.5 * resist_slope) * (intensity - resist_level))
        active = jnp.where(focus * corners + corner < count, 0.25 * resist_slope, 0.0)
        slope = active * ((1.0 - 2.0 * target_ref[...]) + wave) * (1.0 - wave * wave)
        slope = narrow(*split(slope), tab["fine"][0], tab["fine"][1], 1, dot)
        slope = narrow(tab["finet"][0], tab["finet"][1], *split(slope), 1, dot)
        slopes.append(jnp.concatenate([slope, slope], axis=0))
    for corner, slope in enumerate(slopes):
        ge = jnp.concatenate(
            [e_ref[corner, :, s * grid : (s + 1) * grid] * slope for s in range(local_src)], axis=1
        )
        gh = table_times(tab["f3"], ge)
        gh = jnp.concatenate(
            [
                jnp.concatenate(
                    [gh[:freqs, s * grid : (s + 1) * grid], gh[freqs:, s * grid : (s + 1) * grid]],
                    axis=1,
                )
                for s in range(local_src)
            ],
            axis=0,
        )
        gg = narrow(*split(gh), tab["f1"][0], tab["f1"][1], 0, dot_t)
        for s in range(local_src):
            p = p_ref[corner, s]
            part = (w_ref[s] * (2.0 / sources)) * gg[s * freqs : (s + 1) * freqs]
            sum_x = sum_x + p * part
            sum_y = sum_y + swap(p) * part
    gs = jnp.where(first, sum_x + swap(sum_x), sum_y - swap(sum_y))

    def every(copies, step):
        def run():
            for copy in copies:
                getattr(copy, step)()

        return run

    g_send[...] = gs
    g_copies = []
    for b in range(1, nf):
        theirs = pl.multiple_of(core(b) * half, 8)
        g_copies.append(
            remote(
                g_send.at[pl.ds(theirs, half), :], g_recv.at[b - 1],
                g_ss.at[b - 1], g_rs.at[b - 1], {"focus": core(b)},
            )
        )
    every(g_copies, "start")()
    part = g_send[pl.ds(mine, half), :]
    for b, copy in enumerate(g_copies):
        copy.wait_recv()
        part = part + g_recv[b]
    c_recv[0, 0] = part

    def onward(kind, a, device):
        return remote(
            c_recv.at[0, 0], c_recv.at[kind, a], c_ss.at[kind, a], c_rs.at[kind, a],
            {"src": chip(a), **device},
        )

    chips = range(ns - 1, -1, -1)
    c_peers = [onward(0, a, {}) for a in chips if a > 0]
    c_right = [onward(1, a, {"tile": right}) for a in chips]
    c_left = [onward(2, a, {"tile": left}) for a in chips]
    pl.when(has_left)(every(c_left, "start"))
    pl.when(has_right)(every(c_right, "start"))
    every(c_peers, "start")()
    every(c_peers, "wait_recv")()
    pl.when(has_left)(every(c_right, "wait_recv"))
    pl.when(has_right)(every(c_left, "wait_recv"))
    for kind in range(3):
        total = c_recv[kind, 0]
        for a in range(1, ns):
            total = total + c_recv[kind, a]
        g_half[kind] = total
        g_all[kind, pl.ds(mine, half), :] = total

    h_copies = [
        remote(
            g_half, g_all.at[:, pl.ds(mine, half), :],
            h_ss.at[b - 1], h_rs.at[b - 1], {"focus": core(b)},
        )
        for b in range(1, nf)
    ]
    every(h_copies, "start")()

    def stacked(g):
        turned = swap(g)
        return jnp.concatenate([g, jnp.where(first, turned, -turned)], axis=0)

    every(h_copies, "wait_recv")()
    gx = table_times(
        tab["rowt"], jnp.concatenate([stacked(g_all[kind]) for kind in range(3)], axis=1)
    )
    out = times_table(gx[:, :grid], tab["own"])
    gx = gx[:, grid:]
    from_left = times_table(gx[:, :grid], tab["left"])
    from_right = times_table(gx[:, grid:], tab["right"])
    out_ref[:, :edge] = out[:, :edge] + from_left
    out_ref[:, edge : tile - edge] = out[:, edge : tile - edge]
    out_ref[:, tile - edge :] = out[:, tile - edge :] + from_right

    pl.when(has_left)(zs_left.wait_send)
    pl.when(has_right)(zs_right.wait_send)
    pl.when(has_left)(every(c_left, "wait_send"))
    pl.when(has_right)(every(c_right, "wait_send"))
    for copy in i_copies + g_copies + c_peers + h_copies:
        copy.wait_send()


def per_device(mask, target, pupil, weights, counts):
    tile = mask.shape[0]
    freqs = pupil.shape[-1]
    local_src = weights.shape[0]
    corners = pupil.shape[2]
    ns, nf, nt = (lax.axis_size(axis) for axis in ("src", "focus", "tile"))
    grid = 2 * freqs
    rows = tile // (ns * nf)
    half = freqs // nf
    held = tables(tile, freqs, AMBIT)
    held = {name: jnp.asarray(held[name]) for name in NAMES}
    vmem = pl.BlockSpec(memory_space=pltpu.VMEM)
    smem = pl.BlockSpec(memory_space=pltpu.SMEM)
    hbm = pl.BlockSpec(memory_space=pltpu.HBM)
    f32 = jnp.float32
    dma = pltpu.SemaphoreType.DMA
    return pl.pallas_call(
        functools.partial(kernel, (ns, nf, nt, local_src, corners, freqs, tile)),
        out_shape=jax.ShapeDtypeStruct((rows, tile), f32),
        in_specs=[smem, smem] + [hbm] * (3 + len(NAMES)),
        out_specs=vmem,
        scratch_shapes=[
            pltpu.VMEM(mask.shape, f32),
            pltpu.VMEM(target.shape, f32),
            pltpu.VMEM(pupil.shape, f32),
            *[
                pltpu.VMEM((2, rows, grid) if name == "rowt" else held[name].shape, jnp.bfloat16)
                for name in NAMES
            ],
            dma((len(NAMES) + 5,)),
            pltpu.VMEM((corners, local_src, freqs, grid), f32),
            pltpu.VMEM((corners, 2 * grid, local_src * grid), f32),
            pltpu.VMEM((2, freqs, grid), f32),
            pltpu.VMEM((2, freqs, grid), f32),
            pltpu.VMEM((corners, grid, grid), f32),
            pltpu.VMEM((max(ns - 1, 1), corners, grid, grid), f32),
            pltpu.VMEM((freqs, grid), f32),
            pltpu.VMEM((max(nf - 1, 1), half, grid), f32),
            pltpu.VMEM((3, ns, half, grid), f32),
            pltpu.VMEM((3, half, grid), f32),
            pltpu.VMEM((3, freqs, grid), f32),
            dma((2,)),
            dma((2,)),
            dma((max(ns - 1, 1), corners)),
            dma((max(ns - 1, 1), corners)),
            dma((max(nf - 1, 1),)),
            dma((max(nf - 1, 1),)),
            dma((3, ns)),
            dma((3, ns)),
            dma((max(nf - 1, 1),)),
            dma((max(nf - 1, 1),)),
        ],
        compiler_params=pltpu.CompilerParams(
            collective_id=0, has_side_effects=True, vmem_limit_bytes=64 * 1024 * 1024
        ),
        name="abbe_gradient",
    )(counts, weights, mask, target, pupil, *[held[name] for name in NAMES])


def solution(mesh):
    return jax.shard_map(
        per_device,
        mesh=mesh,
        in_specs=(
            P("parts", "tile"),
            P("parts", "tile"),
            P(None, "src", "focus", None, None),
            P("src"),
            P("parts"),
        ),
        out_specs=P(("parts", "src", "focus"), "tile"),
        check_vma=False,
    )
```

```python
import functools
import math

import jax
import jax.numpy as jnp
import ml_dtypes
import numpy as np
from jax import lax
from jax.experimental import pallas as pl
from jax.experimental.pallas import tpu as pltpu
from jax.sharding import PartitionSpec as P

AMBIT = 64
MESH = pl.DeviceIdType.MESH

resist_slope = 4.0
resist_level = 0.5


def halves(table):
    table = table.astype(np.float32)
    high = table.astype(ml_dtypes.bfloat16)
    low = (table - high.astype(np.float32)).astype(ml_dtypes.bfloat16)
    return np.stack([high, low])


def tables(tile, freqs, width):
    win = tile + 2 * width
    grid = 2 * freqs
    k = np.arange(freqs) - freqs // 2
    even, odd = np.flatnonzero(k % 2 == 0), np.flatnonzero(k % 2)
    order = np.concatenate([even, odd])
    row = 2.0 * np.pi * ((k[order][:, None] * (np.arange(tile) + width)[None, :]) % win) / win
    row2 = np.concatenate([np.cos(row), -np.sin(row)], axis=0) / math.sqrt(win)
    col = 2.0 * np.pi * ((k[:, None] * np.arange(win)[None, :]) % win) / win
    col2 = np.concatenate([np.cos(col), -np.sin(col)], axis=0) / math.sqrt(win)
    own = col2[:, width : width + tile]
    edges = np.zeros((2, 2 * freqs, 2 * width))
    edges[0, :, :width] = col2[:, width + tile :]
    edges[1, :, width:] = col2[:, :width]
    at = 2.0 * np.pi * ((k[:, None] * np.arange(grid)[None, :]) % grid) / grid
    c, s = np.cos(at) * math.sqrt(2.0 / freqs), np.sin(at) * math.sqrt(2.0 / freqs)
    field = np.block([[c, s], [-s, c]])

    def by_parity(chosen):
        points = np.concatenate([np.arange(freqs), grid + np.arange(freqs)])
        high, low = halves(field.T[points][:, np.concatenate([chosen, freqs + chosen])])
        return np.concatenate([high, low, high, low], axis=1)

    q = np.arange(1 - freqs, freqs)
    gap = (np.arange(tile) + width)[:, None] / win - np.arange(grid)[None, :] / grid
    fine = np.cos(2.0 * np.pi * gap[:, :, None] * q[None, None, :]).sum(-1) / grid
    return dict(
        row=halves(row2),
        own=halves(own),
        left=halves(edges[0]),
        right=halves(edges[1]),
        f1=halves(field),
        f2=np.stack([by_parity(even), by_parity(odd)]),
        f3=halves(field[np.concatenate([order, freqs + order])]),
        fine=halves(fine),
        finet=halves(fine.T),
        rowt=halves(row2.T),
    )


def split(x):
    high = x.astype(jnp.bfloat16)
    low = (x - high.astype(jnp.float32)).astype(jnp.bfloat16)
    return high, low


def dot(a, b):
    return jnp.dot(a, b, preferred_element_type=jnp.float32)


def dot_t(a, b):
    return lax.dot_general(a, b, (((1,), (1,)), ((), ())), preferred_element_type=jnp.float32)


def times_table(x, table):
    high, low = split(x)
    return dot(
        jnp.concatenate([high, high, low], axis=1),
        jnp.concatenate([table[0], table[1], table[0]], axis=0),
    )


def times_turned(x, table):
    high, low = split(x)
    return dot_t(
        jnp.concatenate([high, high, low], axis=1),
        jnp.concatenate([table[0], table[1], table[0]], axis=1),
    )


def table_times(table, x):
    high, low = split(x)
    return dot(
        jnp.concatenate([table[0], table[1], table[0]], axis=1),
        jnp.concatenate([high, high, low], axis=0),
    )


def narrow(high, low, table_high, table_low, axis, product):
    size = table_high.shape[axis]
    both = product(high, jnp.concatenate([table_high, table_low], axis=axis))
    return both[:, :size] + (both[:, size:] + product(low, table_high))


NAMES = ("row", "left", "right", "own", "f1", "f2", "f3", "fine", "finet", "rowt")


def kernel(dims, counts_ref, w_ref, mask_hbm, target_hbm, pup_hbm, *refs):
    ns, nf, nt, local_src, corners, freqs, tile = dims
    many = len(NAMES)
    held = dict(zip(NAMES, refs[:many]))
    out_ref = refs[many]
    mask_ref, target_ref, pup_ref = refs[many + 1 : many + 4]
    tab = dict(zip(NAMES, refs[many + 4 : 2 * many + 4]))
    (load_sem, p_ref, e_ref, zs_send, zs_recv, i_send, i_recv, g_send, g_recv, c_recv, g_half, g_all,
     zs_ss, zs_rs, i_ss, i_rs, g_ss, g_rs, c_ss, c_rs, h_ss, h_rs) = refs[2 * many + 4 :]
    grid = 2 * freqs
    rows = out_ref.shape[0]
    sources = local_src * ns
    t = lax.axis_index("tile")
    src = lax.axis_index("src")
    focus = lax.axis_index("focus")
    has_left = t > 0
    has_right = t < nt - 1
    left, right = jnp.maximum(t - 1, 0), jnp.minimum(t + 1, nt - 1)
    half = freqs // nf
    mine = pl.multiple_of(focus * half, 8)

    def chip(a):
        return lax.rem(src + a, ns)

    def core(b):
        return lax.rem(focus + b, nf)

    def remote(source, dest, ssem, rsem, device):
        return pltpu.make_async_remote_copy(
            src_ref=source, dst_ref=dest, send_sem=ssem, recv_sem=rsem,
            device_id=device, device_id_type=MESH,
        )

    begin = pl.multiple_of((src * nf + focus) * rows, 16)
    loads = {}

    def load(name, source, dest):
        loads[name] = pltpu.make_async_copy(source, dest, load_sem.at[len(loads)])
        loads[name].start()

    load("row", held["row"], tab["row"])
    load("mask", mask_hbm, mask_ref)
    for name in ("left", "right"):
        load(name, held[name], tab[name])
    load("pupil", pup_hbm, pup_ref)

    def need(*names):
        for name in names:
            loads[name].wait()

    zs_recv[...] = jnp.zeros_like(zs_recv)
    c_recv[...] = jnp.zeros_like(c_recv)
    barrier = pltpu.get_barrier_semaphore()

    def greet(device):
        pl.semaphore_signal(barrier, inc=1, device_id=device, device_id_type=MESH)

    for b in range(1, nf):
        greet({"focus": core(b)})
    for a in range(1, ns):
        greet({"src": chip(a)})

    def greet_tile(tile_index):
        for a in range(ns):
            greet({"tile": tile_index, "src": chip(a)})

    pl.when(has_left)(functools.partial(greet_tile, left))
    pl.when(has_right)(functools.partial(greet_tile, right))

    lane = lax.broadcasted_iota(jnp.int32, (freqs, grid), 1)
    first = lane < freqs

    def swap(x):
        return pltpu.roll(x, freqs, 1)

    def complex_of(q):
        top, low = q[:freqs], swap(q[freqs:])
        return jnp.where(first, top - low, top + low)

    need("row", "mask", "left", "right")
    load("own", held["own"], tab["own"])
    for name in ("f1", "f2", "f3", "fine"):
        load(name, held[name], tab[name])
    load("target", target_hbm, target_ref)
    load("finet", held["finet"], tab["finet"])
    load("rowt", held["rowt"].at[:, pl.ds(begin, rows), :], tab["rowt"])

    edge = 2 * AMBIT

    def columns(high, low, table):
        wide = jnp.concatenate([table[0], table[1], table[0]], axis=1)
        return complex_of(dot_t(jnp.concatenate([high, high, low], axis=1), wide))

    sides = jnp.concatenate([mask_ref[:, :edge], mask_ref[:, tile - edge :]], axis=1)
    sh, sl = split(table_times(tab["row"], sides))
    zs_send[0] = columns(sh[:, :edge], sl[:, :edge], tab["left"])
    zs_send[1] = columns(sh[:, edge:], sl[:, edge:], tab["right"])
    pl.semaphore_wait(
        barrier,
        (ns + nf - 2) + ns * (has_left.astype(jnp.int32) + has_right.astype(jnp.int32)),
    )
    zs_left = remote(zs_send.at[0], zs_recv.at[1], zs_ss.at[0], zs_rs.at[1], {"tile": left})
    zs_right = remote(zs_send.at[1], zs_recv.at[0], zs_ss.at[1], zs_rs.at[0], {"tile": right})
    pl.when(has_left)(zs_left.start)
    pl.when(has_right)(zs_right.start)
    mh, ml = split(table_times(tab["row"], mask_ref[:, edge : tile - edge]))
    few = freqs // 2
    need("own")
    spec = columns(
        jnp.concatenate([sh[:, :edge], mh, sh[:, edge:]], axis=1),
        jnp.concatenate([sl[:, :edge], ml, sl[:, edge:]], axis=1),
        tab["own"],
    )
    need("pupil")
    for corner in range(corners):
        for s in range(local_src):
            p_ref[corner, s] = jnp.concatenate(
                [
                    jnp.concatenate(
                        [pup_ref[n, s, corner, pl.ds(m, few, stride=2), :] for m in range(2)],
                        axis=0,
                    )
                    for n in range(2)
                ],
                axis=1,
            )
    pl.when(has_left)(zs_right.wait_recv)
    pl.when(has_right)(zs_left.wait_recv)
    spec = spec + zs_recv[0] + zs_recv[1]
    turned = swap(spec)
    same = jnp.where(first, spec, turned)
    cross = jnp.where(first, -turned, spec)

    need("f1", "f2")
    i_copies = []
    for corner in range(corners):
        parts = []
        for s in range(local_src):
            p = p_ref[corner, s]
            parts.append(p * same + swap(p) * cross)
        h = times_table(jnp.concatenate(parts, axis=0), tab["f1"])
        h_high, h_low = split(h)

        def parity(n):
            def pieces(x):
                return jnp.concatenate(
                    [
                        jnp.concatenate(
                            [
                                x[s * freqs + n * few : s * freqs + (n + 1) * few, :grid],
                                x[s * freqs + n * few : s * freqs + (n + 1) * few, grid:],
                            ],
                            axis=0,
                        )
                        for s in range(local_src)
                    ],
                    axis=1,
                )

            high, low = pieces(h_high), pieces(h_low)
            return dot(tab["f2"][n], jnp.concatenate([high, high, low, low], axis=0))

        h_even, h_odd = parity(0), parity(1)
        plus, minus = h_even + h_odd, h_even - h_odd
        e = jnp.concatenate(
            [plus[:freqs], minus[:freqs], plus[freqs:], minus[freqs:]], axis=0
        )
        e_ref[corner] = e
        total = jnp.zeros((grid, grid), jnp.float32)
        for s in range(local_src):
            e_re = e[:grid, s * grid : (s + 1) * grid]
            e_im = e[grid:, s * grid : (s + 1) * grid]
            total = total + (w_ref[s] * (1.0 / sources)) * (e_re * e_re + e_im * e_im)
        i_send[corner] = total
        for a in range(1, ns):
            copy = remote(
                i_send.at[corner], i_recv.at[a - 1, corner],
                i_ss.at[a - 1, corner], i_rs.at[a - 1, corner], {"src": chip(a)},
            )
            copy.start()
            i_copies.append(copy)

    need("f3", "fine", "target", "finet", "rowt")
    count = counts_ref[t]
    sum_x = jnp.zeros((freqs, grid), jnp.float32)
    sum_y = jnp.zeros((freqs, grid), jnp.float32)
    slopes = []
    for corner in range(corners):
        total = i_send[corner]
        for a in range(1, ns):
            i_copies[corner * (ns - 1) + a - 1].wait_recv()
            total = total + i_recv[a - 1, corner]
        intensity = times_turned(table_times(tab["fine"], total), tab["fine"])
        wave = jnp.tanh((0.5 * resist_slope) * (intensity - resist_level))
        active = jnp.where(focus * corners + corner < count, 0.25 * resist_slope, 0.0)
        slope = active * ((1.0 - 2.0 * target_ref[...]) + wave) * (1.0 - wave * wave)
        slope = narrow(*split(slope), tab["fine"][0], tab["fine"][1], 1, dot)
        slope = narrow(tab["finet"][0], tab["finet"][1], *split(slope), 1, dot)
        slopes.append(jnp.concatenate([slope, slope], axis=0))
    for corner, slope in enumerate(slopes):
        ge = jnp.concatenate(
            [e_ref[corner, :, s * grid : (s + 1) * grid] * slope for s in range(local_src)], axis=1
        )
        gh = table_times(tab["f3"], ge)
        gh = jnp.concatenate(
            [
                jnp.concatenate(
                    [gh[:freqs, s * grid : (s + 1) * grid], gh[freqs:, s * grid : (s + 1) * grid]],
                    axis=1,
                )
                for s in range(local_src)
            ],
            axis=0,
        )
        gg = narrow(*split(gh), tab["f1"][0], tab["f1"][1], 0, dot_t)
        for s in range(local_src):
            p = p_ref[corner, s]
            part = (w_ref[s] * (2.0 / sources)) * gg[s * freqs : (s + 1) * freqs]
            sum_x = sum_x + p * part
            sum_y = sum_y + swap(p) * part
    gs = jnp.where(first, sum_x + swap(sum_x), sum_y - swap(sum_y))

    def every(copies, step):
        def run():
            for copy in copies:
                getattr(copy, step)()

        return run

    g_send[...] = gs
    g_copies = []
    for b in range(1, nf):
        theirs = pl.multiple_of(core(b) * half, 8)
        g_copies.append(
            remote(
                g_send.at[pl.ds(theirs, half), :], g_recv.at[b - 1],
                g_ss.at[b - 1], g_rs.at[b - 1], {"focus": core(b)},
            )
        )
    every(g_copies, "start")()
    part = g_send[pl.ds(mine, half), :]
    for b, copy in enumerate(g_copies):
        copy.wait_recv()
        part = part + g_recv[b]
    c_recv[0, 0] = part

    def onward(kind, a, device):
        return remote(
            c_recv.at[0, 0], c_recv.at[kind, a], c_ss.at[kind, a], c_rs.at[kind, a],
            {"src": chip(a), **device},
        )

    chips = range(ns - 1, -1, -1)
    c_peers = [onward(0, a, {}) for a in chips if a > 0]
    c_right = [onward(1, a, {"tile": right}) for a in chips]
    c_left = [onward(2, a, {"tile": left}) for a in chips]
    pl.when(has_left)(every(c_left, "start"))
    pl.when(has_right)(every(c_right, "start"))
    every(c_peers, "start")()
    every(c_peers, "wait_recv")()
    pl.when(has_left)(every(c_right, "wait_recv"))
    pl.when(has_right)(every(c_left, "wait_recv"))
    for kind in range(3):
        total = c_recv[kind, 0]
        for a in range(1, ns):
            total = total + c_recv[kind, a]
        g_half[kind] = total
        g_all[kind, pl.ds(mine, half), :] = total

    h_copies = [
        remote(
            g_half, g_all.at[:, pl.ds(mine, half), :],
            h_ss.at[b - 1], h_rs.at[b - 1], {"focus": core(b)},
        )
        for b in range(1, nf)
    ]
    every(h_copies, "start")()

    def stacked(g):
        turned = swap(g)
        return jnp.concatenate([g, jnp.where(first, turned, -turned)], axis=0)

    every(h_copies, "wait_recv")()
    gx = table_times(
        tab["rowt"], jnp.concatenate([stacked(g_all[kind]) for kind in range(3)], axis=1)
    )
    out = times_table(gx[:, :grid], tab["own"])
    gx = gx[:, grid:]
    from_left = times_table(gx[:, :grid], tab["left"])
    from_right = times_table(gx[:, grid:], tab["right"])
    out_ref[:, :edge] = out[:, :edge] + from_left
    out_ref[:, edge : tile - edge] = out[:, edge : tile - edge]
    out_ref[:, tile - edge :] = out[:, tile - edge :] + from_right

    pl.when(has_left)(zs_left.wait_send)
    pl.when(has_right)(zs_right.wait_send)
    pl.when(has_left)(every(c_left, "wait_send"))
    pl.when(has_right)(every(c_right, "wait_send"))
    for copy in i_copies + g_copies + c_peers + h_copies:
        copy.wait_send()


def per_device(mask, target, pupil, weights, counts):
    tile = mask.shape[0]
    freqs = pupil.shape[-1]
    local_src = weights.shape[0]
    corners = pupil.shape[2]
    ns, nf, nt = (lax.axis_size(axis) for axis in ("src", "focus", "tile"))
    grid = 2 * freqs
    rows = tile // (ns * nf)
    half = freqs // nf
    held = tables(tile, freqs, AMBIT)
    held = {name: jnp.asarray(held[name]) for name in NAMES}
    vmem = pl.BlockSpec(memory_space=pltpu.VMEM)
    smem = pl.BlockSpec(memory_space=pltpu.SMEM)
    hbm = pl.BlockSpec(memory_space=pltpu.HBM)
    f32 = jnp.float32
    dma = pltpu.SemaphoreType.DMA
    return pl.pallas_call(
        functools.partial(kernel, (ns, nf, nt, local_src, corners, freqs, tile)),
        out_shape=jax.ShapeDtypeStruct((rows, tile), f32),
        in_specs=[smem, smem] + [hbm] * (3 + len(NAMES)),
        out_specs=vmem,
        scratch_shapes=[
            pltpu.VMEM(mask.shape, f32),
            pltpu.VMEM(target.shape, f32),
            pltpu.VMEM(pupil.shape, f32),
            *[
                pltpu.VMEM((2, rows, grid) if name == "rowt" else held[name].shape, jnp.bfloat16)
                for name in NAMES
            ],
            dma((len(NAMES) + 3,)),
            pltpu.VMEM((corners, local_src, freqs, grid), f32),
            pltpu.VMEM((corners, 2 * grid, local_src * grid), f32),
            pltpu.VMEM((2, freqs, grid), f32),
            pltpu.VMEM((2, freqs, grid), f32),
            pltpu.VMEM((corners, grid, grid), f32),
            pltpu.VMEM((max(ns - 1, 1), corners, grid, grid), f32),
            pltpu.VMEM((freqs, grid), f32),
            pltpu.VMEM((max(nf - 1, 1), half, grid), f32),
            pltpu.VMEM((3, ns, half, grid), f32),
            pltpu.VMEM((3, half, grid), f32),
            pltpu.VMEM((3, freqs, grid), f32),
            dma((2,)),
            dma((2,)),
            dma((max(ns - 1, 1), corners)),
            dma((max(ns - 1, 1), corners)),
            dma((max(nf - 1, 1),)),
            dma((max(nf - 1, 1),)),
            dma((3, ns)),
            dma((3, ns)),
            dma((max(nf - 1, 1),)),
            dma((max(nf - 1, 1),)),
        ],
        compiler_params=pltpu.CompilerParams(
            collective_id=0, has_side_effects=True, vmem_limit_bytes=64 * 1024 * 1024
        ),
        name="abbe_gradient",
    )(counts, weights, mask, target, pupil, *[held[name] for name in NAMES])


def solution(mesh):
    return jax.shard_map(
        per_device,
        mesh=mesh,
        in_specs=(
            P("parts", "tile"),
            P("parts", "tile"),
            P(None, "src", "focus", None, None),
            P("src"),
            P("parts"),
        ),
        out_specs=P(("parts", "src", "focus"), "tile"),
        check_vma=False,
    )
```
